128 devices in a mesh: img: 2 (over y_hi), row: 16 (over x, z), col: 4 (over y_lo, core).
Axes of the slice: x: 4, y: 4 (y_hi: 2, y_lo: 2; y = y_hi * 2 + y_lo), z: 4, core: 2. Of those that a mesh axis runs over, the one named last changes fastest.
Arguments:
- image: bfloat16 [512, 256, 1024], P('img', 'row', 'col'), parts along dimension 0, may hold values from -6 to 6
- from_local: bfloat16 [9, 256, 64], replicated, may hold values from -0.25 to 0.25
- from_global: bfloat16 [9, 64, 192], replicated, may hold values from -0.15625 to 0.15625
- section_weight: bfloat16 [96, 192], replicated, may hold values from -0.4375 to 0.4375
- section_scale: float32 [96], replicated, may hold values from 0.5 to 2
- section_shift: float32 [96], replicated, may hold values from -2 to 2
- fourier_weight: bfloat16 [192, 192], replicated, may hold values from -0.4375 to 0.4375
- fourier_scale: float32 [192], replicated, may hold values from 0.5 to 2
- fourier_shift: float32 [192], replicated, may hold values from -2 to 2
- mix_weight: bfloat16 [192, 96], replicated, may hold values from -0.625 to 0.625
- out_scale: float32 [256], replicated, may hold values from 0.5 to 2
- out_shift: float32 [256], replicated, may hold values from -2 to 2
Outputs:
- result: bfloat16 [512, 256, 1024], P('img', 'row', 'col'), parts along dimension 0
The draws below stay inside these ranges and needn't reach their ends.
There are 2 independent parts, one for each index of `img`. The reference program is written for one: setup_inputs(seed, part) draws one part's arguments, and reference() takes and returns one part's arrays. A program takes and returns all parts, laid end to end along the dimension named above; an argument that names none is the same for every part. Nothing has to cross between parts.
All inputs are finite; a program needn't handle non-finite values.
Results may differ from the reference program's by a relative error of at most 0.013.
Values may be sent and summed in bfloat16 or wider, within the bound.
No kernel may reach another device: no remote copies, remote signals or barrier semaphores. Data moves between devices by JAX's collectives and lax.ppermute only.
A program may use at most 128 MiB of HBM per device.

```python
import math
import jax
import jax.numpy as jnp
from jax import lax

C = 256
CL = 64
CG = 192
CF = 96
W = 1024
H = 256


def block_scale(key, dims, shards, smallest, top_value):
    loudness, own = 1.0, jax.random.fold_in(key, 6)
    for axis_at, parts in shards:
        draws = jnp.exp(jax.random.uniform(jax.random.fold_in(own, axis_at), (parts,), jnp.float32, smallest / len(shards), top_value / len(shards)))
        loudness = loudness * jnp.repeat(draws, dims[axis_at] // parts).reshape([-1 if axis == axis_at else 1 for axis in range(len(dims))])
    return loudness


def scatter_about(stream_key, extent, scale, most, pieces=(), dtype=jnp.bfloat16):
    entries = jax.random.normal(stream_key, extent, jnp.float32) * scale
    if len(pieces) > 0:
        entries = block_scale(stream_key, extent, pieces, -0.22, 0.18) * entries
    return jnp.clip(entries, min=-most, max=most).astype(dtype)


def setup_inputs(seed: int = 0, part: int = 0) -> dict:
    keys = jax.random.split(jax.random.key(seed), 13)
    own_keys = jax.random.split(jax.random.fold_in(keys[12], part), 13)
    return {
        "image": scatter_about(own_keys[0], (C, H, W), 1.0, 6.0, ((1, 16), (2, 4))),
        "from_local": scatter_about(keys[1], (9, C, CL), (9 * CL) ** -0.5, 0.25),
        "from_global": scatter_about(keys[2], (9, CL, CG), (9 * CG) ** -0.5, 0.15625),
        "section_weight": scatter_about(keys[3], (CF, CG), CG ** -0.5, 0.4375),
        "section_scale": jnp.clip(jnp.exp(jax.random.uniform(keys[4], (CF,), jnp.float32, math.log(0.5), math.log(2.0))), 0.5, 2.0),
        "section_shift": scatter_about(keys[5], (CF,), 0.5, 2.0, (), jnp.float32),
        "fourier_weight": scatter_about(keys[6], (2 * CF, 2 * CF), (2 * CF) ** -0.5, 0.4375),
        "fourier_scale": jnp.clip(jnp.exp(jax.random.uniform(keys[7], (2 * CF,), jnp.float32, math.log(0.5), math.log(2.0))), 0.5, 2.0),
        "fourier_shift": scatter_about(keys[8], (2 * CF,), 0.5, 2.0, (), jnp.float32),
        "mix_weight": scatter_about(keys[9], (CG, CF), CF ** -0.5, 0.625),
        "out_scale": jnp.clip(jnp.exp(jax.random.uniform(keys[10], (C,), jnp.float32, math.log(0.5), math.log(2.0))), 0.5, 2.0),
        "out_shift": scatter_about(keys[11], (C,), 0.5, 2.0, (), jnp.float32),
    }


def spatial_conv(inputs, weights):
    kernel = weights.astype(jnp.float32).reshape(3, 3, weights.shape[1], weights.shape[2]).transpose(2, 3, 0, 1)
    return lax.conv_general_dilated(inputs.astype(jnp.float32)[None], kernel, (1, 1), ((1, 1), (1, 1)), dimension_numbers=("NCHW", "OIHW", "NCHW"), precision=lax.Precision.HIGHEST)[0]


def reference(image, from_local, from_global, section_weight, section_scale, section_shift, fourier_weight, fourier_scale, fourier_shift, mix_weight, out_scale, out_shift):
    local_in = image[:CL]
    global_in = image[CL:]
    from_loc = spatial_conv(local_in, from_local)
    from_glob = spatial_conv(global_in, from_global)
    section_lin = jnp.einsum("oc,chw->ohw", section_weight.astype(jnp.float32), global_in.astype(jnp.float32), precision=lax.Precision.HIGHEST)
    section_map = jax.nn.relu(section_scale[:, None, None] * section_lin + section_shift[:, None, None]).astype(jnp.bfloat16)
    spectrum = jnp.fft.rfft2(section_map.astype(jnp.float32), norm="ortho")
    stacked = jnp.concatenate([jnp.real(spectrum), jnp.imag(spectrum)], 0).astype(jnp.bfloat16)
    mixed_spec = jnp.einsum("oj,jhk->ohk", fourier_weight.astype(jnp.float32), stacked.astype(jnp.float32), precision=lax.Precision.HIGHEST)
    activated = jax.nn.relu(fourier_scale[:, None, None] * mixed_spec + fourier_shift[:, None, None])
    complex_spec = lax.complex(activated[:CF], activated[CF:])
    along_h = jnp.fft.ifft(complex_spec, axis=1, norm="ortho")
    first_col = jnp.real(along_h[:, :, 0])
    last_col = jnp.real(along_h[:, :, W // 2])
    along_h = along_h.at[:, :, 0].set(lax.complex(first_col, jnp.zeros_like(first_col)))
    along_h = along_h.at[:, :, W // 2].set(lax.complex(last_col, jnp.zeros_like(last_col)))
    fourier = jnp.fft.irfft(along_h, n=W, axis=2, norm="ortho").astype(jnp.bfloat16)
    mixed_map = (section_map.astype(jnp.float32) + fourier.astype(jnp.float32)).astype(jnp.bfloat16)
    from_mix = jnp.einsum("oc,chw->ohw", mix_weight.astype(jnp.float32), mixed_map.astype(jnp.float32), precision=lax.Precision.HIGHEST)
    pre_act = jnp.concatenate([from_loc[:CL] + from_glob, from_loc[CL:] + from_mix], 0)
    result = image.astype(jnp.float32) + jax.nn.relu(out_scale[:, None, None] * pre_act + out_shift[:, None, None])
    return result.astype(jnp.bfloat16)
```

```python
import functools
import math

import jax
import jax.numpy as jnp
import numpy as np
from jax import lax
from jax.experimental import pallas as pl
from jax.experimental.pallas import tpu as pltpu
from jax.sharding import PartitionSpec as P

F32 = jnp.float32
BF16 = jnp.bfloat16
VMEM_LIMIT = 48 * 1024 * 1024

H, W = 256, 1024
ROWS, COLS = 16, 4
PEERS = ROWS * COLS
NF = W // 2 // PEERS
CF = 96
HS = H // PEERS
LANES = HS * CF
MID = H // HS


def bf(table):
    return np.asarray(table, np.float32).astype(jnp.bfloat16)


@functools.lru_cache(None)
def width_tables():
    k = np.arange(W // 2)
    w = np.arange(W)
    angle = 2 * math.pi / W * ((w[:, None] * k[None, :]) % W)
    alternate = np.where(w % 2 == 0, 1.0, -1.0)
    cos, sin = np.cos(angle), np.sin(angle)
    fwd = np.stack([cos, np.where(k[None, :] == 0, alternate[:, None], -sin)], 0)
    inv = np.stack([np.where(k[None, :] == 0, 1.0, 2.0) * cos, np.where(k[None, :] == 0, alternate[:, None], -2.0 * sin)], 0)
    order = lambda t: t.reshape(2, W, PEERS, NF).transpose(2, 0, 3, 1).reshape(W, W)
    norm = 1.0 / math.sqrt(W)
    return bf(order(fwd) * norm), bf(order(inv).T * norm)


@functools.lru_cache(None)
def height_tables():
    m = np.arange(MID)
    angle = 2 * math.pi / MID * ((m[:, None] * m[None, :]) % MID)
    cos, sin = np.cos(angle), np.sin(angle)
    norm = 1.0 / math.sqrt(H)
    fwd = np.zeros((2, NF + 1, 2, MID, MID, 2, NF))
    inv = np.zeros((2, MID, 2, NF, NF + 1, 2, MID))
    for z in range(2):
        for f in range(NF + 1):
            src = f % NF
            use_re = f < NF and True
            if f < NF and not (z and f == 0):
                fwd[z, f, 0, :, :, 0, f] = cos
                fwd[z, f, 0, :, :, 1, f] = sin
                fwd[z, f, 1, :, :, 0, f] = -sin
                fwd[z, f, 1, :, :, 1, f] = cos
                inv[z, :, 0, f, f, 0, :] = cos
                inv[z, :, 0, f, f, 1, :] = -sin
                inv[z, :, 1, f, f, 0, :] = sin
                inv[z, :, 1, f, f, 1, :] = cos
            elif z:
                part = 0 if f == 0 else 1
                fwd[z, f, 0, :, :, part, 0] = cos
                fwd[z, f, 1, :, :, part, 0] = -sin
                inv[z, :, part, 0, f, 0, :] = cos
                inv[z, :, part, 0, f, 1, :] = -sin
    size = 2 * NF * MID
    wide = 2 * (NF + 1) * MID
    return bf(fwd.reshape(2, wide, size) * norm), bf(inv.reshape(2, size, 3, wide // 3).transpose(0, 2, 1, 3) * norm)


@functools.lru_cache(None)
def twiddles():
    m = np.arange(MID)[:, None]
    r = np.repeat(np.arange(HS), CF)[None, :]
    angle = 2 * math.pi / H * (m * r)
    return np.stack([np.cos(angle), -np.sin(angle)], 0).astype(np.float32)


def quarter_turn(t):
    return np.round(np.cos(math.pi / 2 * t)), np.round(np.sin(math.pi / 2 * t))


@functools.lru_cache(None)
def mix_signs():
    j = np.arange(HS)[:, None]
    r = np.arange(HS)[None, :]
    c, s = quarter_turn(j * r)
    s = -s
    real = np.stack([c, -s], 1)
    imag = np.stack([s, c], 1)
    return real.astype(np.float32), imag.astype(np.float32)


@functools.lru_cache(None)
def unmix_table():
    table = np.zeros((HS, 2, CF, 2, HS, CF))
    eye = np.eye(CF)
    for j in range(HS):
        for r in range(HS):
            c, s = quarter_turn(np.asarray(j * r))
            table[j, 0, :, 0, r, :] = c * eye
            table[j, 1, :, 0, r, :] = -s * eye
            table[j, 0, :, 1, r, :] = s * eye
            table[j, 1, :, 1, r, :] = c * eye
    return bf(table.reshape(HS, 2 * CF, 2 * LANES))


def dot(a, b):
    return jnp.dot(a, b, preferred_element_type=F32)


def dot_nt(a, b):
    return lax.dot_general(a, b, (((1,), (1,)), ((), ())), preferred_element_type=F32)


def call(body, out_shape, flops, nbytes, **kw):
    return pl.pallas_call(
        body,
        out_shape=out_shape,
        compiler_params=pltpu.CompilerParams(vmem_limit_bytes=VMEM_LIMIT),
        cost_estimate=pl.CostEstimate(flops=flops, bytes_accessed=nbytes, transcendentals=0),
        **kw,
    )


def section_body(x_ref, w_ref, scale_ref, shift_ref, o_ref):
    skip = x_ref.shape[1] - w_ref.shape[1]
    for h in range(x_ref.shape[0]):
        lin = dot(w_ref[...], x_ref[h, skip:, :])
        o_ref[h] = jnp.maximum(scale_ref[...] * lin + shift_ref[...], 0.0).astype(BF16)


def width_body(t_ref, d_ref, o_ref):
    wide = d_ref.shape[2]
    total = dot_nt(t_ref[:, :wide], d_ref[0])
    for p in range(1, d_ref.shape[0]):
        total = total + dot_nt(t_ref[:, p * wide : (p + 1) * wide], d_ref[p])
    o_ref[...] = total.astype(BF16)


def middle_body(z_ref, fwd_ref, inv_ref, d_ref, tw_ref, g_ref, q_ref, scale_ref, shift_ref, o_ref, total):
    step = pl.program_id(0)
    count = fwd_ref.shape[1] // (2 * MID)
    u = dot(fwd_ref[0], d_ref[...])
    twr, twi = tw_ref[0], tw_ref[1]
    rows = []
    for f in range(count):
        ur = u[2 * f * MID : (2 * f + 1) * MID]
        ui = u[(2 * f + 1) * MID : (2 * f + 2) * MID]
        rows.append(jnp.concatenate([ur * twr - ui * twi, ur * twi + ui * twr], 1).astype(BF16))
    v = jnp.concatenate(rows, 0)
    back = None
    for j in range(HS):
        mixed = dot(v, g_ref[j])
        active = jnp.maximum(scale_ref[...] * mixed + shift_ref[...], 0.0).astype(BF16)
        term = dot(active, q_ref[j])
        back = term if back is None else back + term
    rows = []
    for f in range(count):
        br = back[f * MID : (f + 1) * MID, :LANES]
        bi = back[f * MID : (f + 1) * MID, LANES:]
        rows.append((br * twr + bi * twi).astype(BF16))
        rows.append((bi * twr - br * twi).astype(BF16))
    part = dot(inv_ref[0, 0], jnp.concatenate(rows, 0))

    @pl.when(step == 0)
    def _():
        total[...] = part

    @pl.when(step > 0)
    def _():
        total[...] += part

    @pl.when(step == pl.num_programs(0) - 1)
    def _():
        o_ref[...] = total[...].astype(BF16)


def inverse_body(t_ref, d_ref, o_ref):
    o_ref[...] = dot(t_ref[...], d_ref[...]).astype(BF16)


def conv_body(x_ref, wl_ref, wg_ref, wm_ref, sec_ref, o_ref):
    h = pl.program_id(0)
    cl = wl_ref.shape[1] // 3
    cg = wg_ref.shape[1] // 3
    channels = cl + cg
    width = o_ref.shape[2]
    ext = x_ref.shape[2]
    rows = [x_ref[h + dy] for dy in range(3)]
    local = jnp.concatenate([row[:cl] for row in rows], 0)
    other = jnp.concatenate([row[cl:] for row in rows], 0)
    parts = []
    for dx in range(3):
        yl = dot(wl_ref[dx * channels : (dx + 1) * channels], local)
        yg = dot(wg_ref[dx * cl : (dx + 1) * cl], other)
        parts.append(jnp.concatenate([yl[:cl] + yg, yl[cl:]], 0))
    acc = parts[1] + pltpu.roll(parts[0], 1, 1) + pltpu.roll(parts[2], ext - 1, 1)
    mix = dot(wm_ref[...], sec_ref[0])
    o_ref[0, :cl] = acc[:cl, :width].astype(BF16)
    o_ref[0, cl:] = (acc[cl:, :width] + mix).astype(BF16)


def final_body(x_ref, pre_ref, f_ref, w_ref, scale_ref, shift_ref, o_ref):
    outs = w_ref.shape[0] // HS
    low = x_ref.shape[1] - outs
    res = dot_nt(w_ref[...], f_ref[0])
    for r in range(HS):
        pre = pre_ref[r].astype(F32)
        pre = jnp.concatenate([pre[:low], pre[low:] + res[r * outs : (r + 1) * outs]], 0)
        act = jnp.maximum(scale_ref[...] * pre + shift_ref[...], 0.0)
        o_ref[r] = (x_ref[r].astype(F32) + act).astype(BF16)


def shift_along(block, axis, step):
    count = lax.axis_size(axis)
    pairs = [(i, i + step) for i in range(count) if 0 <= i + step < count]
    return lax.ppermute(block, axis, pairs)


def full(shape):
    return pl.BlockSpec(shape, lambda *_: (0,) * len(shape))


def per_device(
    image,
    from_local,
    from_global,
    section_weight,
    section_scale,
    section_shift,
    fourier_weight,
    fourier_scale,
    fourier_shift,
    mix_weight,
    out_scale,
    out_shift,
):
    channels, rows, width = image.shape
    cl = from_local.shape[2]
    cg = channels - cl
    holds_zero = jnp.logical_and(lax.axis_index("row") == 0, lax.axis_index("col") == 0)
    z = holds_zero.astype(jnp.int32).reshape(1)

    x = jnp.transpose(image, (1, 0, 2))
    section = call(
        section_body,
        jax.ShapeDtypeStruct((rows, CF, width), BF16),
        2 * rows * CF * cg * width,
        4 * 2**20,
    )(x, section_weight, section_scale[:, None], section_shift[:, None])

    sent = lax.all_to_all(section.reshape(COLS, HS * CF, width), "col", split_axis=0, concat_axis=0, tiled=True)

    fwd_w, inv_w = width_tables()
    spectra = call(
        width_body,
        jax.ShapeDtypeStruct((W, LANES), BF16),
        2 * W * W * LANES,
        4 * 2**20,
        grid=(4,),
        in_specs=[pl.BlockSpec((W // 4, W), lambda i: (i, 0)), full((COLS, LANES, width))],
        out_specs=pl.BlockSpec((W // 4, LANES), lambda i: (i, 0)),
    )(jnp.asarray(fwd_w), sent)

    spectra = lax.all_to_all(
        spectra.reshape(PEERS, 2 * NF, LANES), ("row", "col"), split_axis=0, concat_axis=0, tiled=True
    ).reshape(W, LANES)

    fwd_h, inv_h = height_tables()
    sign_re, sign_im = mix_signs()
    fw_re = fourier_weight[:, :CF].T[None, None, None]
    fw_im = fourier_weight[:, CF:].T[None, None, None]
    mixer = (
        jnp.asarray(sign_re, BF16)[..., None, None] * fw_re + jnp.asarray(sign_im, BF16)[..., None, None] * fw_im
    ).reshape(HS, 2 * LANES, 2 * CF)
    wide = 2 * (NF + 1) * MID // 3
    returned = pl.pallas_call(
        middle_body,
        out_shape=jax.ShapeDtypeStruct((W, LANES), BF16),
        grid_spec=pltpu.PrefetchScalarGridSpec(
            num_scalar_prefetch=1,
            grid=(3,),
            in_specs=[
                pl.BlockSpec((1, wide, W), lambda i, s: (s[0], i, 0)),
                pl.BlockSpec((1, 1, W, wide), lambda i, s: (s[0], i, 0, 0)),
                full((W, LANES)),
                full((2, MID, LANES)),
                full((HS, 2 * LANES, 2 * CF)),
                full((HS, 2 * CF, 2 * LANES)),
                full((1, 2 * CF)),
                full((1, 2 * CF)),
            ],
            out_specs=full((W, LANES)),
            scratch_shapes=[pltpu.VMEM((W, LANES), F32)],
        ),
        compiler_params=pltpu.CompilerParams(vmem_limit_bytes=VMEM_LIMIT),
        cost_estimate=pl.CostEstimate(flops=3 * 10**9, bytes_accessed=10 * 2**20, transcendentals=0),
    )(
        z,
        jnp.asarray(fwd_h),
        jnp.asarray(inv_h),
        spectra,
        jnp.asarray(twiddles()),
        mixer,
        jnp.asarray(unmix_table()),
        fourier_scale[None],
        fourier_shift[None],
    )

    returned = lax.all_to_all(
        returned.reshape(PEERS, 2 * NF, LANES), ("row", "col"), split_axis=0, concat_axis=0, tiled=True
    ).reshape(W, LANES)

    fourier = call(
        inverse_body,
        jax.ShapeDtypeStruct((W, LANES), BF16),
        2 * W * W * LANES,
        4 * 2**20,
        grid=(4,),
        in_specs=[pl.BlockSpec((W // 4, W), lambda i: (i, 0)), full((W, LANES))],
        out_specs=pl.BlockSpec((W // 4, LANES), lambda i: (i, 0)),
    )(jnp.asarray(inv_w), returned)
    fourier = lax.all_to_all(
        fourier.reshape(COLS, width, LANES), "col", split_axis=0, concat_axis=0, tiled=True
    )

    above = shift_along(x[rows - 1], "row", 1)
    below = shift_along(x[0], "row", -1)
    tall = jnp.concatenate([above[None], x, below[None]], 0)
    left = shift_along(tall[:, :, width - 1], "col", 1)
    right = shift_along(tall[:, :, 0], "col", -1)
    ext = width + 128
    padded = jnp.concatenate(
        [tall, right[:, :, None], jnp.zeros((rows + 2, channels, 126), BF16), left[:, :, None]], 2
    )
    wl = from_local.reshape(3, 3, channels, cl).transpose(1, 2, 0, 3).reshape(3 * channels, 3 * cl)
    wg = from_global.reshape(3, 3, cl, cg).transpose(1, 2, 0, 3).reshape(3 * cl, 3 * cg)
    pre = call(
        conv_body,
        jax.ShapeDtypeStruct((rows, channels, width), BF16),
        3 * 10**9,
        6 * 2**20,
        grid=(rows,),
        in_specs=[
            full((rows + 2, channels, ext)),
            full((3 * channels, 3 * cl)),
            full((3 * cl, 3 * cg)),
            full((cg, CF)),
            pl.BlockSpec((1, CF, width), lambda i: (i, 0, 0)),
        ],
        out_specs=pl.BlockSpec((1, channels, width), lambda i: (i, 0, 0)),
    )(padded, wl, wg, mix_weight, section)

    eye = jnp.asarray(np.eye(HS, dtype=np.float32), BF16)
    mix4 = (eye[:, None, :, None] * mix_weight[None, :, None, :]).reshape(HS * cg, LANES)
    result = call(
        final_body,
        jax.ShapeDtypeStruct((rows, channels, width), BF16),
        10**9,
        7 * 2**20,
        grid=(COLS,),
        in_specs=[
            pl.BlockSpec((HS, channels, width), lambda i: (i, 0, 0)),
            pl.BlockSpec((HS, channels, width), lambda i: (i, 0, 0)),
            pl.BlockSpec((1, width, LANES), lambda i: (i, 0, 0)),
            full((HS * cg, LANES)),
            full((channels, 1)),
            full((channels, 1)),
        ],
        out_specs=pl.BlockSpec((HS, channels, width), lambda i: (i, 0, 0)),
    )(x, pre, fourier, mix4, out_scale[:, None], out_shift[:, None])
    return jnp.transpose(result, (1, 0, 2))


def solution(mesh):
    return jax.shard_map(
        per_device,
        mesh=mesh,
        in_specs=(P("img", "row", "col"), P(), P(), P(), P(), P(), P(), P(), P(), P(), P(), P()),
        out_specs=P("img", "row", "col"),
        check_vma=False,
    )
```

```python
import functools
import math

import jax
import jax.numpy as jnp
import numpy as np
from jax import lax
from jax.experimental import pallas as pl
from jax.experimental.pallas import tpu as pltpu
from jax.sharding import PartitionSpec as P

F32 = jnp.float32
BF16 = jnp.bfloat16
MIB = 1024 * 1024

H, W = 256, 1024
ROWS, COLS = 16, 4
PEERS = ROWS * COLS
NF = W // 2 // PEERS
CF = 96
HS = H // PEERS
LANES = HS * CF
LANE = 128
WIDE = HS * LANE
MID = H // HS
ORDER = (2, 3, 1, 0)


def bf(table):
    return np.asarray(table, np.float32).astype(jnp.bfloat16)


@functools.lru_cache(None)
def width_tables():
    k = np.arange(W // 2)
    w = np.arange(W)
    angle = 2 * math.pi / W * ((w[:, None] * k[None, :]) % W)
    alternate = np.where(w % 2 == 0, 1.0, -1.0)
    cos, sin = np.cos(angle), np.sin(angle)
    fwd = np.stack([cos, np.where(k[None, :] == 0, alternate[:, None], -sin)], 0)
    inv = np.stack([np.where(k[None, :] == 0, 1.0, 2.0) * cos, np.where(k[None, :] == 0, alternate[:, None], -2.0 * sin)], 0)
    order = lambda t: t.reshape(2, W, PEERS, NF).transpose(2, 0, 3, 1).reshape(W, W)
    norm = 1.0 / math.sqrt(W)
    fwd = (order(fwd) * norm).reshape(W, COLS, W // COLS).transpose(1, 0, 2)
    inv = (order(inv).T * norm).reshape(COLS, W // COLS, W)
    return bf(fwd), bf(inv)


@functools.lru_cache(None)
def height_tables():
    m = np.arange(MID)
    angle = 2 * math.pi / MID * ((m[:, None] * m[None, :]) % MID)
    cos, sin = np.cos(angle), np.sin(angle)
    norm = 1.0 / math.sqrt(H)
    fwd = np.zeros((2, NF + 1, 2, MID, MID, 2, NF))
    inv = np.zeros((2, MID, 2, NF, NF + 1, 2, MID))
    for z in range(2):
        for f in range(NF + 1):
            if f < NF and not (z and f == 0):
                fwd[z, f, 0, :, :, 0, f] = cos
                fwd[z, f, 0, :, :, 1, f] = sin
                fwd[z, f, 1, :, :, 0, f] = -sin
                fwd[z, f, 1, :, :, 1, f] = cos
                inv[z, :, 0, f, f, 0, :] = cos
                inv[z, :, 0, f, f, 1, :] = -sin
                inv[z, :, 1, f, f, 0, :] = sin
                inv[z, :, 1, f, f, 1, :] = cos
            elif z:
                part = 0 if f == 0 else 1
                fwd[z, f, 0, :, :, part, 0] = cos
                fwd[z, f, 1, :, :, part, 0] = -sin
                inv[z, :, part, 0, f, 0, :] = cos
                inv[z, :, part, 0, f, 1, :] = -sin
    size = 2 * NF * MID
    wide = 2 * (NF + 1) * MID
    return bf(fwd.reshape(2, wide, size) * norm), bf(inv.reshape(2, size, wide) * norm)


@functools.lru_cache(None)
def twiddles():
    m = np.arange(MID)[:, None]
    r = np.repeat(np.arange(HS), LANE)[None, :]
    angle = 2 * math.pi / H * (m * r)
    return np.stack([np.cos(angle), -np.sin(angle)], 0).astype(np.float32)


def dot(a, b):
    return jnp.dot(a, b, preferred_element_type=F32)


def dot_nt(a, b):
    return lax.dot_general(a, b, (((1,), (1,)), ((), ())), preferred_element_type=F32)


def call(body, out_shape, operands, smem=(), hbm=(), hbm_out=False, limit=16, flops=10**9, **kw):
    place = lambda i: pltpu.SMEM if i in smem else pltpu.HBM if i in hbm else pltpu.VMEM
    out_place = pltpu.HBM if hbm_out else pltpu.VMEM
    operands = [v if i in smem else pltpu.with_memory_space_constraint(v, place(i)) for i, v in enumerate(operands)]
    return pl.pallas_call(
        body,
        out_shape=jax.tree.map(lambda s: out_place(s.shape, s.dtype), out_shape),
        in_specs=[pl.BlockSpec(memory_space=place(i)) for i in range(len(operands))],
        out_specs=jax.tree.map(lambda _: pl.BlockSpec(memory_space=out_place), out_shape),
        compiler_params=pltpu.CompilerParams(vmem_limit_bytes=limit * MIB),
        cost_estimate=pl.CostEstimate(flops=flops, bytes_accessed=4 * MIB, transcendentals=0),
        **kw,
    )(*operands)


def prepare_body(fl_ref, fg_ref, mix_ref, fw_ref, scale_ref, shift_ref, wl_ref, wg_ref, mix4_ref, mixer_ref, affine_ref):
    cl, channels = fl_ref.shape[1], fl_ref.shape[2]
    for dx in range(3):
        taps = jnp.concatenate([fl_ref[3 * dy + dx] for dy in range(3)], 0)
        wl_ref[dx * channels : (dx + 1) * channels] = taps.T
        wg_ref[dx * cl : (dx + 1) * cl] = jnp.concatenate([fg_ref[3 * dy + dx] for dy in range(3)], 1)
    mix = mix_ref[...]
    count = mix.shape[0]
    for r in range(HS):
        sides = [jnp.zeros((count, CF * r), BF16), mix, jnp.zeros((count, LANES - CF * (r + 1)), BF16)]
        mix4_ref[r * count : (r + 1) * count] = jnp.concatenate([s for s in sides if s.shape[1]], 1)
    spread = lambda t: jnp.concatenate([t[:, :CF], gap(t), t[:, CF:], gap(t)], 1)
    gap = lambda t: jnp.zeros((t.shape[0], LANE - CF), t.dtype)
    wide = spread(fw_ref[...].T)
    low = jnp.zeros((LANE - CF, 2 * LANE), BF16)
    mixer_ref[...] = jnp.concatenate([wide[:CF], low, wide[CF:], low], 0)
    affine_ref[...] = jnp.concatenate([spread(scale_ref[...]), spread(shift_ref[...])], 0)


def section_body(me_ref, x_ref, w_ref, affine_ref, o_ref, *sent):
    rows, channels, width = x_ref.shape
    skip = channels - w_ref.shape[1]
    for s in ORDER:
        first = HS * lax.bitwise_xor(me_ref[0], s)
        for r in range(HS):
            lin = dot(w_ref[...], x_ref[first + r, skip:, :])
            value = jnp.maximum(affine_ref[:, 0:1] * lin + affine_ref[:, 1:2], 0.0).astype(BF16)
            o_ref[first + r] = value
            sent[s][r * CF : (r + 1) * CF] = value
    place = lax.broadcasted_iota(jnp.int32, (2 * rows, width), 0)
    lane = lax.broadcasted_iota(jnp.int32, (2 * rows, width), 1)
    ends = jnp.zeros((2 * rows, channels), F32)
    for h in range(rows):
        pick = ((place == h) & (lane == 0)) | ((place == rows + h) & (lane == width - 1))
        ends = ends + dot_nt(pick.astype(F32).astype(BF16), x_ref[h])
    ends = ends.astype(BF16)
    sent[1][LANES:] = ends
    sent[3][LANES:] = ends


def halo_body(me_ref, x_ref, next_ref, last_ref, down_ref, up_ref, side_ref):
    rows, channels, _ = x_ref.shape
    me = me_ref[0]
    odd = lax.rem(me, 2).astype(F32)
    near = next_ref[LANES:].astype(F32)
    far = last_ref[LANES:].astype(F32)
    even = 1.0 - odd
    left = (odd * near[rows:] + even * far[rows:]) * jnp.where(me > 0, 1.0, 0.0)
    right = (odd * far[:rows] + even * near[:rows]) * jnp.where(me < COLS - 1, 1.0, 0.0)
    sides = jnp.concatenate([left, right], 0).astype(BF16)
    side_ref[...] = sides
    down_ref[:channels] = x_ref[rows - 1]
    down_ref[channels:] = sides
    up_ref[:channels] = x_ref[0]
    up_ref[channels:] = sides


def width_near_body(me_ref, t_ref, near_ref, next_ref, o_ref):
    me = me_ref[0]
    o_ref[...] = dot_nt(t_ref[me], near_ref[...]) + dot_nt(t_ref[lax.bitwise_xor(me, 1)], next_ref[:LANES])


def width_far_body(me_ref, t_ref, part_ref, far_ref, last_ref, o_ref, held, sem):
    me = me_ref[0]
    size = o_ref.shape[0] // 4
    copies = []
    for i in range(4):
        span = pl.ds(i * size, size)
        total = part_ref[span] + dot_nt(t_ref[lax.bitwise_xor(me, 2), span], far_ref[...])
        held[span] = (total + dot_nt(t_ref[lax.bitwise_xor(me, 3), span], last_ref[:LANES])).astype(BF16)
        copies.append(pltpu.make_async_copy(held.at[span], o_ref.at[span], sem.at[i]))
        copies[-1].start()
    for copy in copies:
        copy.wait()


def widen(d):
    gap = jnp.zeros((d.shape[0], LANE - CF), d.dtype)
    return jnp.concatenate(sum([[d[:, CF * r : CF * r + CF], gap] for r in range(HS)], []), 1)


def narrow(d):
    return jnp.concatenate([d[:, LANE * r : LANE * r + CF] for r in range(HS)], 1)


def turns(real, imag):
    s02r, d02r, s13r, d13r = real[0] + real[2], real[0] - real[2], real[1] + real[3], real[1] - real[3]
    s02i, d02i, s13i, d13i = imag[0] + imag[2], imag[0] - imag[2], imag[1] + imag[3], imag[1] - imag[3]
    return (
        (s02r + s13r, s02i + s13i),
        (d02r + d13i, d02i - d13r),
        (s02r - s13r, s02i - s13i),
        (d02r - d13i, d02i + d13r),
    )


def middle_body(z_ref, fwd_ref, inv_ref, d_ref, tw_ref, w_ref, affine_ref, o_ref, fwd, inv, held, sem):
    z = z_ref[0]
    step = fwd.shape[0] // 3
    loads = []
    for i in range(3):
        span = pl.ds(i * step, step)
        loads.append(pltpu.make_async_copy(fwd_ref.at[z, span], fwd.at[span], sem.at[i]))
    quarter = inv.shape[0] // 4
    for i in range(4):
        span = pl.ds(i * quarter, quarter)
        loads.append(pltpu.make_async_copy(inv_ref.at[z, span], inv.at[span], sem.at[3 + i]))
    for load in loads:
        load.start()
    d = widen(d_ref[...])
    parts = []
    for i in range(3):
        loads[i].wait()
        parts.append(dot(fwd[pl.ds(i * step, step)], d))
    u = jnp.concatenate(parts, 0)
    twr, twi = tw_ref[0], tw_ref[1]
    rows = []
    for f in range(NF + 1):
        ur = u[2 * f * MID : (2 * f + 1) * MID]
        ui = u[(2 * f + 1) * MID : (2 * f + 2) * MID]
        vr = ur * twr - ui * twi
        vi = ur * twi + ui * twr
        groups = [slice(LANE * r, LANE * r + LANE) for r in range(HS)]
        for real, imag in turns([vr[:, g] for g in groups], [vi[:, g] for g in groups]):
            rows.append(jnp.concatenate([real, imag], 1).astype(BF16))
    mixed = dot(jnp.concatenate(rows, 0), w_ref[...])
    active = jnp.maximum(affine_ref[0:1] * mixed + affine_ref[1:2], 0.0)
    rows = []
    for f in range(NF + 1):
        own = [active[(HS * f + j) * MID : (HS * f + j + 1) * MID] for j in range(HS)]
        own = [own[j] for j in (0, 3, 2, 1)]
        turned = turns([v[:, :LANE] for v in own], [v[:, LANE:] for v in own])
        br = jnp.concatenate([v[0] for v in turned], 1)
        bi = jnp.concatenate([v[1] for v in turned], 1)
        rows.append((br * twr + bi * twi).astype(BF16))
        rows.append((bi * twr - br * twi).astype(BF16))
    back = jnp.concatenate(rows, 0)
    stores = []
    for i in range(4):
        span = pl.ds(i * quarter, quarter)
        loads[3 + i].wait()
        held[span] = narrow(dot(inv[span], back).astype(BF16))
        stores.append(pltpu.make_async_copy(held.at[span], o_ref.at[span], sem.at[7 + i]))
        stores[-1].start()
    for store in stores:
        store.wait()


def inverse_body(pair, me_ref, t_ref, d_ref, a_ref, b_ref):
    for s, o_ref in zip(pair, (a_ref, b_ref)):
        o_ref[...] = dot(t_ref[lax.bitwise_xor(me_ref[0], s)], d_ref[...]).astype(BF16)


def conv_body(x_ref, above_ref, below_ref, side_ref, wl_ref, wg_ref, wm_ref, sec_ref, o_ref, cols, edge):
    cl = wl_ref.shape[1] // 3
    cg = wg_ref.shape[1] // 3
    rows, channels, width = x_ref.shape
    cols[...] = jnp.zeros_like(cols)
    for side in range(2):
        own = pl.ds(side * rows, rows)
        held = pl.ds(channels + side * rows, rows)
        cols[side, 0:rows] = above_ref[held]
        cols[side, rows : 2 * rows] = side_ref[own]
        cols[side, 2 * rows : 3 * rows] = below_ref[held]
        dx = 2 * side
        total = None
        for dy in range(3):
            taps = wl_ref[dx * channels : (dx + 1) * channels, dy * cl : (dy + 1) * cl]
            term = dot_nt(taps, cols[side, :, :cl])
            taps = wg_ref[dx * cl : (dx + 1) * cl, dy * cg : (dy + 1) * cg]
            extra = dot_nt(taps, cols[side, :, cl:])
            term = jnp.concatenate([term[:cl] + extra, term[cl:]], 0)
            term = pltpu.roll(term, LANE - (rows - 1 + dy), 1)
            total = term if total is None else total + term
        edge[side] = total
    lane = lax.broadcasted_iota(jnp.int32, (channels, LANE), 1)

    def emit(h, three):
        local = jnp.concatenate([row[:cl] for row in three], 0)
        other = jnp.concatenate([row[cl:] for row in three], 0)
        parts = []
        for dx in range(3):
            yl = dot(wl_ref[dx * channels : (dx + 1) * channels], local)
            yg = dot(wg_ref[dx * cl : (dx + 1) * cl], other)
            parts.append(jnp.concatenate([yl[:cl] + yg, yl[cl:]], 0))
        before = pltpu.roll(parts[0], 1, 1)
        behind = pltpu.roll(parts[2], width - 1, 1)
        first = pltpu.roll(edge[0], lax.rem(LANE - h, LANE), 1)
        final = pltpu.roll(edge[1], LANE - 1 - h, 1)
        before = jnp.concatenate([jnp.where(lane == 0, first, before[:, :LANE]), before[:, LANE:]], 1)
        behind = jnp.concatenate([behind[:, : width - LANE], jnp.where(lane == LANE - 1, final, behind[:, width - LANE :])], 1)
        acc = parts[1] + before + behind
        mix = dot(wm_ref[...], sec_ref[h])
        o_ref[h, :cl] = acc[:cl].astype(BF16)
        o_ref[h, cl:] = (acc[cl:] + mix).astype(BF16)

    emit(0, [above_ref[:channels], x_ref[0], x_ref[1]])

    def step(h, carry):
        emit(h, [x_ref[h - 1], x_ref[h], x_ref[h + 1]])
        return carry

    lax.fori_loop(1, rows - 1, step, 0)
    emit(rows - 1, [x_ref[rows - 2], x_ref[rows - 1], below_ref[:channels]])


def final_body(pair, me_ref, x_ref, pre_ref, a_ref, b_ref, w_ref, affine_ref, *outs):
    o_ref = outs[-1]
    count = w_ref.shape[0] // HS
    low = x_ref.shape[1] - count
    for s, f_ref in zip(pair, (a_ref, b_ref)):
        first = HS * lax.bitwise_xor(me_ref[0], s)
        res = dot_nt(w_ref[...], f_ref[...])
        for r in range(HS):
            pre = pre_ref[first + r].astype(F32)
            pre = jnp.concatenate([pre[:low], pre[low:] + res[r * count : (r + 1) * count]], 0)
            act = jnp.maximum(affine_ref[:, 0:1] * pre + affine_ref[:, 1:2], 0.0)
            o_ref[first + r] = (x_ref[first + r].astype(F32) + act).astype(BF16)


def shift_along(block, axis, step):
    count = lax.axis_size(axis)
    pairs = [(i, i + step) for i in range(count) if 0 <= i + step < count]
    return lax.ppermute(block, axis, pairs)


def swap(block, s):
    return lax.ppermute(block, "col", [(i, i ^ s) for i in range(COLS)])


def after(value, *others):
    return lax.optimization_barrier((value,) + others)


def per_device(
    image,
    from_local,
    from_global,
    section_weight,
    section_scale,
    section_shift,
    fourier_weight,
    fourier_scale,
    fourier_shift,
    mix_weight,
    out_scale,
    out_shift,
):
    channels, rows, width = image.shape
    cl = from_local.shape[2]
    cg = channels - cl
    me = lax.axis_index("col").astype(jnp.int32).reshape(1)
    z = jnp.logical_and(lax.axis_index("row") == 0, lax.axis_index("col") == 0).astype(jnp.int32).reshape(1)
    shape = jax.ShapeDtypeStruct

    x = jnp.transpose(image, (1, 0, 2))
    block, block_ends = shape((LANES, width), BF16), shape((LANES + 2 * rows, width), BF16)
    section, near, other, far, last = call(
        section_body,
        (shape((rows, CF, width), BF16), block, block_ends, block, block_ends),
        (me, x, section_weight, jnp.stack([section_scale, section_shift], 1)),
        smem=(0,),
    )
    far, last, other = swap(far, 2), swap(last, 3), swap(other, 1)

    wl, wg, mix4, mixer, affine = call(
        prepare_body,
        (
            shape((3 * channels, 3 * cl), BF16),
            shape((3 * cl, 3 * cg), BF16),
            shape((HS * cg, LANES), BF16),
            shape((2 * LANE, 2 * LANE), BF16),
            shape((2, 2 * LANE), F32),
        ),
        (
            jnp.transpose(from_local, (0, 2, 1)),
            from_global,
            mix_weight,
            fourier_weight,
            fourier_scale[None],
            fourier_shift[None],
        ),
    )

    fwd_w, inv_w = (jnp.asarray(t) for t in width_tables())
    part = call(width_near_body, shape((W, LANES), F32), (me, fwd_w, near, other), smem=(0,))
    spectra = call(
        width_far_body,
        shape((W, LANES), BF16),
        (me, fwd_w, part, far, last),
        smem=(0,),
        hbm_out=True,
        scratch_shapes=[pltpu.VMEM((W, LANES), BF16), pltpu.SemaphoreType.DMA((4,))],
    )
    down, up, sides = call(
        halo_body,
        (shape((channels + 2 * rows, width), BF16),) * 2 + (shape((2 * rows, channels), BF16),),
        (me, x, other, last),
        smem=(0,),
        flops=10**6,
    )
    spectra, down, up = after(spectra, down, up)
    spectra = lax.all_to_all(
        spectra.reshape(PEERS, 2 * NF, LANES), ("row", "col"), split_axis=0, concat_axis=0, tiled=True
    ).reshape(W, LANES)
    above, below = shift_along(down, "row", 1), shift_along(up, "row", -1)
    spectra, above, below = after(spectra, above, below)

    fwd_h, inv_h = (jnp.asarray(t) for t in height_tables())
    size, wide = 2 * NF * MID, 2 * (NF + 1) * MID
    returned = call(
        middle_body,
        shape((W, LANES), BF16),
        (z, fwd_h, inv_h, spectra, jnp.asarray(twiddles()), mixer, affine),
        smem=(0,),
        hbm=(1, 2),
        hbm_out=True,
        limit=32,
        scratch_shapes=[
            pltpu.VMEM((wide, size), BF16),
            pltpu.VMEM((size, wide), BF16),
            pltpu.VMEM((W, LANES), BF16),
            pltpu.SemaphoreType.DMA((11,)),
        ],
    )
    returned, above, below = after(returned, above, below)
    returned = lax.all_to_all(
        returned.reshape(PEERS, 2 * NF, LANES), ("row", "col"), split_axis=0, concat_axis=0, tiled=True
    ).reshape(W, LANES)
    pre = call(
        conv_body,
        shape((rows, channels, width), BF16),
        (x, above, below, sides, wl, wg, mix_weight, section),
        flops=3 * 10**9,
        scratch_shapes=[pltpu.VMEM((2, LANE, channels), BF16), pltpu.VMEM((2, channels, LANE), F32)],
    )
    returned, pre = after(returned, pre)

    piece = shape((width, LANES), BF16)
    out_affine = jnp.stack([out_scale, out_shift], 1)
    far, last = call(functools.partial(inverse_body, (2, 3)), (piece, piece), (me, inv_w, returned), smem=(0,))
    far, last = swap(far, 2), swap(last, 3)
    other, near = call(functools.partial(inverse_body, (1, 0)), (piece, piece), (me, inv_w, returned), smem=(0,))
    other = swap(other, 1)
    whole = shape((rows, channels, width), BF16)
    half = call(
        functools.partial(final_body, (0, 1)), whole, (me, x, pre, near, other, mix4, out_affine), smem=(0,)
    )
    result = call(
        functools.partial(final_body, (2, 3)),
        whole,
        (me, x, pre, far, last, mix4, out_affine, half),
        smem=(0,),
        input_output_aliases={7: 0},
    )
    return jnp.transpose(result, (1, 0, 2))


def solution(mesh):
    return jax.shard_map(
        per_device,
        mesh=mesh,
        in_specs=(P("img", "row", "col"), P(), P(), P(), P(), P(), P(), P(), P(), P(), P(), P()),
        out_specs=P("img", "row", "col"),
        check_vma=False,
    )
```

```python
import functools
import math

import jax
import jax.numpy as jnp
import numpy as np
from jax import lax
from jax.experimental import pallas as pl
from jax.experimental.pallas import tpu as pltpu
from jax.sharding import PartitionSpec as P

F32 = jnp.float32
BF16 = jnp.bfloat16
MIB = 1024 * 1024

H, W = 256, 1024
ROWS, COLS = 16, 4
PEERS = ROWS * COLS
NF = W // 2 // PEERS
CF = 96
HS = H // PEERS
LANES = HS * CF
LANE = 128
WIDE = HS * LANE
MID = H // HS
PARTS = 8
SPLIT = 9


def bf(table):
    return np.asarray(table, np.float32).astype(jnp.bfloat16)


@functools.lru_cache(None)
def width_tables():
    k = np.arange(W // 2)
    w = np.arange(W)
    angle = 2 * math.pi / W * ((w[:, None] * k[None, :]) % W)
    alternate = np.where(w % 2 == 0, 1.0, -1.0)
    cos, sin = np.cos(angle), np.sin(angle)
    fwd = np.stack([cos, np.where(k[None, :] == 0, alternate[:, None], -sin)], 0)
    inv = np.stack([np.where(k[None, :] == 0, 1.0, 2.0) * cos, np.where(k[None, :] == 0, alternate[:, None], -2.0 * sin)], 0)
    order = lambda t: t.reshape(2, W, PEERS, NF).transpose(2, 0, 3, 1).reshape(W, W)
    norm = 1.0 / math.sqrt(W)
    fwd = (order(fwd) * norm).reshape(W, COLS, W // COLS).transpose(1, 0, 2)
    inv = (order(inv) * norm).reshape(W, COLS, W // COLS).transpose(1, 0, 2)
    return bf(fwd), bf(inv)


@functools.lru_cache(None)
def height_tables():
    m = np.arange(MID)
    angle = 2 * math.pi / MID * ((m[:, None] * m[None, :]) % MID)
    cos, sin, zero = np.cos(angle), np.sin(angle), np.zeros((MID, MID))
    norm = 1.0 / math.sqrt(H)
    fwd = np.block([[cos, sin], [-sin, cos]])
    inv = np.block([[cos, -sin], [sin, cos]])
    none = np.zeros_like(fwd)
    pair = lambda t: np.block([[t, none], [none, t]])
    fwd_edge = np.stack(
        [np.block([[fwd], [none]]), np.block([[cos, zero], [-sin, zero], [zero, cos], [zero, -sin]])], 0
    )
    inv_edge = np.stack(
        [np.block([[inv, none]]), np.block([[cos, -sin, zero, zero], [zero, zero, cos, -sin]])], 0
    )
    return tuple(bf(t * norm) for t in (pair(fwd), pair(inv), fwd_edge, inv_edge))


@functools.lru_cache(None)
def twiddles():
    m = np.arange(MID)[:, None]
    r = np.repeat(np.arange(HS), LANE)[None, :]
    angle = 2 * math.pi / H * (m * r)
    return np.stack([np.cos(angle), -np.sin(angle)], 0).astype(np.float32)


def dot(a, b):
    return jnp.dot(a, b, preferred_element_type=F32)


def dot_nt(a, b):
    return lax.dot_general(a, b, (((1,), (1,)), ((), ())), preferred_element_type=F32)


def staged(body, staged_at, total, outs, refs):
    ins, rest = list(refs[:total]), refs[total:]
    count = len(staged_at)
    targets, sem, rest = rest[outs : outs + count], rest[outs + count], rest[:outs] + rest[outs + count + 1 :]
    loads = [pltpu.make_async_copy(ins[i], t, sem.at[n]) for n, (i, t) in enumerate(zip(staged_at, targets))]
    for load in loads:
        load.start()
    for i, t in zip(staged_at, targets):
        ins[i] = t
    for load in loads:
        load.wait()
    body(*ins, *rest)


def call(body, out_shape, operands, smem=(), hbm=(), stage=(), hbm_out=(), limit=16, flops=10**6, scratch=(), **kw):
    place = lambda i: pltpu.SMEM if i in smem else pltpu.HBM if i in hbm or i in stage else pltpu.VMEM
    single = not isinstance(out_shape, tuple)
    outs = [out_shape] if single else list(out_shape)
    spaces = [pltpu.HBM if i in hbm_out else pltpu.VMEM for i in range(len(outs))]
    shapes = [space(s.shape, s.dtype) for space, s in zip(spaces, outs)]
    specs = [pl.BlockSpec(memory_space=space) for space in spaces]
    operands = [v if i in smem else pltpu.with_memory_space_constraint(v, place(i)) for i, v in enumerate(operands)]
    if stage:
        inner, total = body, len(operands)
        body = lambda *refs: staged(inner, stage, total, len(outs), refs)
        held = [pltpu.VMEM(operands[i].shape, operands[i].dtype) for i in stage]
        scratch = held + [pltpu.SemaphoreType.DMA((len(stage),))] + list(scratch)
    return pl.pallas_call(
        body,
        out_shape=shapes[0] if single else tuple(shapes),
        in_specs=[pl.BlockSpec(memory_space=place(i)) for i in range(len(operands))],
        out_specs=specs[0] if single else tuple(specs),
        scratch_shapes=scratch,
        compiler_params=pltpu.CompilerParams(vmem_limit_bytes=limit * MIB),
        cost_estimate=pl.CostEstimate(flops=flops, bytes_accessed=flops // 1000, transcendentals=0),
        **kw,
    )(*operands)


def column(row):
    count = row.shape[1]
    diagonal = lax.broadcasted_iota(jnp.int32, (count, count), 0) == lax.broadcasted_iota(jnp.int32, (count, count), 1)
    return jnp.sum(jnp.where(diagonal, jnp.broadcast_to(row, (count, count)), 0.0), 1, keepdims=True)


def section_rows(weight, scale, shift, x):
    return jnp.maximum(scale * dot(weight, x) + shift, 0.0).astype(BF16)


def first_body(
    me_ref, image_ref, w_ref, scale_ref, shift_ref, x_ref, far_ref, affine_ref, held, weight, scale_row, shift_row, sem
):
    channels = image_ref.shape[0]
    size = channels // PARTS
    small = [(w_ref, weight), (scale_ref, scale_row), (shift_ref, shift_row)]
    others = [pltpu.make_async_copy(a, b, sem.at[PARTS + i]) for i, (a, b) in enumerate(small)]
    loads = []
    for i in range(PARTS):
        span = pl.ds(i * size, size)
        loads.append(pltpu.make_async_copy(image_ref.at[span], held.at[span], sem.at[i]))
    for load in others + loads[::-1]:
        load.start()
    for load in others:
        load.wait()
    scale, shift = column(scale_row[...]), column(shift_row[...])
    affine_ref[:, 0:1] = scale
    affine_ref[:, 1:2] = shift
    for i in range(PARTS - 1, -1, -1):
        span = slice(i * size, (i + 1) * size)
        loads[i].wait()
        x_ref[:, span, :] = jnp.swapaxes(held[span], 0, 1)
    first = HS * lax.bitwise_xor(me_ref[0], 2)
    skip = channels - w_ref.shape[1]
    for r in range(HS):
        far_ref[r * CF : (r + 1) * CF] = section_rows(weight[...], scale, shift, x_ref[first + r, skip:, :])


def rest_body(me_ref, x_ref, w_ref, affine_ref, near_ref, next_ref, last_ref):
    rows, channels, width = x_ref.shape
    skip = channels - w_ref.shape[1]
    scale, shift = affine_ref[:, 0:1], affine_ref[:, 1:2]
    for s, o_ref in ((3, last_ref), (1, next_ref), (0, near_ref)):
        first = HS * lax.bitwise_xor(me_ref[0], s)
        for r in range(HS):
            o_ref[r * CF : (r + 1) * CF] = section_rows(w_ref[...], scale, shift, x_ref[first + r, skip:, :])
    place = lax.broadcasted_iota(jnp.int32, (2 * rows, width), 0)
    lane = lax.broadcasted_iota(jnp.int32, (2 * rows, width), 1)
    ends = jnp.zeros((2 * rows, channels), F32)
    for h in range(rows):
        pick = ((place == h) & (lane == 0)) | ((place == rows + h) & (lane == width - 1))
        ends = ends + dot_nt(pick.astype(F32).astype(BF16), x_ref[h])
    ends = ends.astype(BF16)
    last_ref[LANES:] = ends
    next_ref[LANES:] = ends


def halo_body(me_ref, x_ref, next_ref, last_ref, down_ref, up_ref, side_ref):
    rows, channels, _ = x_ref.shape
    me = me_ref[0]
    odd = lax.rem(me, 2).astype(F32)
    near = next_ref[LANES:].astype(F32)
    far = last_ref[LANES:].astype(F32)
    even = 1.0 - odd
    left = (odd * near[rows:] + even * far[rows:]) * jnp.where(me > 0, 1.0, 0.0)
    right = (odd * far[:rows] + even * near[:rows]) * jnp.where(me < COLS - 1, 1.0, 0.0)
    sides = jnp.concatenate([left, right], 0).astype(BF16)
    side_ref[...] = sides
    down_ref[:channels] = x_ref[rows - 1]
    down_ref[channels:] = sides
    up_ref[:channels] = x_ref[0]
    up_ref[channels:] = sides


def width_near_body(me_ref, t_ref, near_ref, next_ref, o_ref):
    me = me_ref[0]
    o_ref[...] = dot_nt(t_ref[me], near_ref[...]) + dot_nt(t_ref[lax.bitwise_xor(me, 1)], next_ref[:LANES])


def width_far_body(me_ref, t_ref, part_ref, far_ref, last_ref, o_ref, held, sem):
    me = me_ref[0]
    size = o_ref.shape[0] // 4
    copies = []
    for i in range(4):
        span = pl.ds(i * size, size)
        total = part_ref[span] + dot_nt(t_ref[lax.bitwise_xor(me, 2), span], far_ref[...])
        held[span] = (total + dot_nt(t_ref[lax.bitwise_xor(me, 3), span], last_ref[:LANES])).astype(BF16)
        copies.append(pltpu.make_async_copy(held.at[span], o_ref.at[span], sem.at[i]))
        copies[-1].start()
    for copy in copies:
        copy.wait()


def widen(d):
    gap = jnp.zeros((d.shape[0], LANE - CF), d.dtype)
    return jnp.concatenate(sum([[d[:, CF * r : CF * r + CF], gap] for r in range(HS)], []), 1)


def narrow(d):
    return jnp.concatenate([d[:, LANE * r : LANE * r + CF] for r in range(HS)], 1)


def turns(real, imag):
    s02r, d02r, s13r, d13r = real[0] + real[2], real[0] - real[2], real[1] + real[3], real[1] - real[3]
    s02i, d02i, s13i, d13i = imag[0] + imag[2], imag[0] - imag[2], imag[1] + imag[3], imag[1] - imag[3]
    return (
        (s02r + s13r, s02i + s13i),
        (d02r + d13i, d02i - d13r),
        (s02r - s13r, s02i - s13i),
        (d02r - d13i, d02i + d13r),
    )


def spread(t):
    gap = jnp.zeros((t.shape[0], LANE - CF), t.dtype)
    return jnp.concatenate([t[:, :CF], gap, t[:, CF:], gap], 1)


def middle_body(
    z_ref, d_ref, *refs
):
    o_ref = refs[8]
    wide, back_ref = refs[17], refs[18]
    held, sem = refs[19], refs[20]
    z = z_ref[0]
    tables = refs[9:17]
    loads = []
    for i, (source, target) in enumerate(zip(refs[:8], tables)):
        source = source.at[z] if i in (2, 3) else source
        loads.append(pltpu.make_async_copy(source, target, sem.at[i]))
        loads[-1].start()
    fwd, inv, fwd_edge, inv_edge, tw, fw, scale_row, shift_row = tables
    wide[...] = widen(jnp.swapaxes(d_ref[...], 0, 1).reshape(W, LANES))
    for load in loads:
        load.wait()
    twr, twi = tw[0], tw[1]
    mixer = spread(fw[...].T)
    low = jnp.zeros((LANE - CF, 2 * LANE), BF16)
    mixer = jnp.concatenate([mixer[:CF], low, mixer[CF:], low], 0)
    scale, shift = spread(scale_row[...]), spread(shift_row[...])
    groups = [slice(LANE * r, LANE * r + LANE) for r in range(HS)]
    for own in ((0,), (1, 2), (3, 4), (5, 6), (7,)):
        data = jnp.concatenate(
            [wide[(p * NF + f) * MID : (p * NF + f + 1) * MID] for f in own for p in range(2)], 0
        )
        count = 2 if own == (0,) else len(own)
        half = 2 * MID * len(own)
        ahead = fwd_edge[...] if own == (0,) else fwd[:half, :half]
        u = dot(ahead, data)
        rows = []
        for f in range(count):
            ur = u[2 * f * MID : (2 * f + 1) * MID]
            ui = u[(2 * f + 1) * MID : (2 * f + 2) * MID]
            vr = ur * twr - ui * twi
            vi = ur * twi + ui * twr
            for real, imag in turns([vr[:, g] for g in groups], [vi[:, g] for g in groups]):
                rows.append(jnp.concatenate([real, imag], 1).astype(BF16))
        mixed = dot(jnp.concatenate(rows, 0), mixer)
        active = jnp.maximum(scale * mixed + shift, 0.0)
        rows = []
        for f in range(count):
            part = [active[(HS * f + j) * MID : (HS * f + j + 1) * MID] for j in (0, 3, 2, 1)]
            turned = turns([v[:, :LANE] for v in part], [v[:, LANE:] for v in part])
            br = jnp.concatenate([v[0] for v in turned], 1)
            bi = jnp.concatenate([v[1] for v in turned], 1)
            rows.append((br * twr + bi * twi).astype(BF16))
            rows.append((bi * twr - br * twi).astype(BF16))
        behind = inv_edge[...] if own == (0,) else inv[:half, :half]
        done = narrow(dot(behind, jnp.concatenate(rows, 0)).astype(BF16))
        for i, f in enumerate(own):
            for p in range(2):
                back_ref[p * NF + f] = done[(2 * i + p) * MID : (2 * i + p + 1) * MID]
    stores = []
    size = MID // 4
    for i in range(4):
        span = pl.ds(i * size, size)
        held[span] = jnp.swapaxes(back_ref[:, i * size : (i + 1) * size, :], 0, 1)
        stores.append(pltpu.make_async_copy(held.at[span], o_ref.at[span], sem.at[8 + i]))
        stores[-1].start()
    for store in stores:
        store.wait()


def inverse_body(pieces, me_ref, t_ref, d_ref, *refs):
    count = len(pieces)
    table, sem = refs[count:]
    loads = []
    for i, s in enumerate(pieces):
        loads.append(pltpu.make_async_copy(t_ref.at[lax.bitwise_xor(me_ref[0], s)], table.at[i], sem.at[i]))
        loads[-1].start()
    data = d_ref[...].T
    for i in range(count):
        loads[i].wait()
        refs[i][...] = dot(data, table[i]).astype(BF16)


def conv_setup(fl_ref, fg_ref, wl_ref, wg_ref):
    cl, channels = fl_ref.shape[1], fl_ref.shape[2]
    for dx in range(3):
        wl_ref[dx * channels : (dx + 1) * channels] = jnp.concatenate([fl_ref[3 * dy + dx] for dy in range(3)], 0).T
        wg_ref[dx * cl : (dx + 1) * cl] = jnp.concatenate([fg_ref[3 * dy + dx] for dy in range(3)], 1)


def conv_edges(side_ref, around, wl_ref, wg_ref, cols, edge):
    rows, channels = side_ref.shape[0] // 2, side_ref.shape[1]
    cl, cg = wl_ref.shape[1] // 3, wg_ref.shape[1] // 3
    cols[...] = jnp.zeros_like(cols)
    for side in range(2):
        own = pl.ds(side * rows, rows)
        cols[side, rows : 2 * rows] = side_ref[own]
        for i, other in enumerate(around):
            cols[side, 2 * i * rows : (2 * i + 1) * rows] = other[pl.ds(channels + side * rows, rows)]
        dx = 2 * side
        total = None
        for dy in range(3):
            taps = wl_ref[dx * channels : (dx + 1) * channels, dy * cl : (dy + 1) * cl]
            term = dot_nt(taps, cols[side, :, :cl])
            taps = wg_ref[dx * cl : (dx + 1) * cl, dy * cg : (dy + 1) * cg]
            extra = dot_nt(taps, cols[side, :, cl:])
            term = jnp.concatenate([term[:cl] + extra, term[cl:]], 0)
            term = pltpu.roll(term, LANE - (rows - 1 + dy), 1)
            total = term if total is None else total + term
        edge[side] = total


def edge_lanes(h, edge, before, behind):
    lane = lax.broadcasted_iota(jnp.int32, edge.shape[1:], 1)
    width = before.shape[1]
    first = pltpu.roll(edge[0], lax.rem(LANE - h, LANE), 1)
    final = pltpu.roll(edge[1], LANE - 1 - h, 1)
    before = jnp.concatenate([jnp.where(lane == 0, first, before[:, :LANE]), before[:, LANE:]], 1)
    last = jnp.where(lane == LANE - 1, final, behind[:, width - LANE :])
    return before, jnp.concatenate([behind[:, : width - LANE], last], 1)


def conv_row(h, three, wl_ref, wg_ref, wm_ref, ws_ref, affine_ref, edge, o_ref, out_ref, sem):
    channels, width = three[1].shape
    cl = wl_ref.shape[1] // 3
    local = jnp.concatenate([row[:cl] for row in three], 0)
    other = jnp.concatenate([row[cl:] for row in three], 0)
    parts = []
    for dx in range(3):
        yl = dot(wl_ref[dx * channels : (dx + 1) * channels], local)
        yg = dot(wg_ref[dx * cl : (dx + 1) * cl], other)
        parts.append(jnp.concatenate([yl[:cl] + yg, yl[cl:]], 0))
    before = pltpu.roll(parts[0], 1, 1)
    behind = pltpu.roll(parts[2], width - 1, 1)
    before, behind = edge_lanes(h, edge, before, behind)
    acc = parts[1] + before + behind
    mix = dot(wm_ref[...], section_rows(ws_ref[...], affine_ref[:, 0:1], affine_ref[:, 1:2], three[1][cl:]))
    o_ref[h, :cl] = acc[:cl].astype(BF16)
    o_ref[h, cl:] = (acc[cl:] + mix).astype(BF16)
    pltpu.make_async_copy(o_ref.at[h], out_ref.at[h], sem.at[0]).start()


def conv_inner_body(
    x_ref, fl_ref, fg_ref, wm_ref, ws_ref, affine_ref, out_ref, o_ref, edge, wl_ref, wg_ref, sem
):
    conv_setup(fl_ref, fg_ref, wl_ref, wg_ref)
    edge[...] = jnp.zeros_like(edge)

    def step(h, carry):
        three = [x_ref[h - 1], x_ref[h], x_ref[h + 1]]
        conv_row(h, three, wl_ref, wg_ref, wm_ref, ws_ref, affine_ref, edge, o_ref, out_ref, sem)
        return carry

    lax.fori_loop(1, SPLIT, step, 0)
    done = pl.ds(1, SPLIT - 1)
    pltpu.make_async_copy(o_ref.at[done], out_ref.at[done], sem.at[0]).wait()


def conv_outer_body(
    x_ref,
    side_ref,
    fl_ref,
    fg_ref,
    wm_ref,
    ws_ref,
    affine_ref,
    above_ref,
    below_ref,
    given_ref,
    out_ref,
    o_ref,
    cols,
    edge,
    wl_ref,
    wg_ref,
    sem,
):
    rows, channels, width = x_ref.shape
    inner = pl.ds(1, SPLIT - 1)
    load = pltpu.make_async_copy(given_ref.at[inner], o_ref.at[inner], sem.at[1])
    load.start()
    conv_setup(fl_ref, fg_ref, wl_ref, wg_ref)
    conv_edges(side_ref, (above_ref, below_ref), wl_ref, wg_ref, cols, edge)
    rest = (wl_ref, wg_ref, wm_ref, ws_ref, affine_ref, edge, o_ref, out_ref, sem)

    def step(h, carry):
        conv_row(h, [x_ref[h - 1], x_ref[h], x_ref[h + 1]], *rest)
        return carry

    lax.fori_loop(SPLIT, rows - 1, step, 0)
    conv_row(0, [above_ref[:channels], x_ref[0], x_ref[1]], *rest)
    conv_row(rows - 1, [x_ref[rows - 2], x_ref[rows - 1], below_ref[:channels]], *rest)
    load.wait()

    def fix(h, carry):
        none = jnp.zeros((channels, width), F32)
        before, behind = edge_lanes(h, edge, none, none)
        o_ref[h] = (o_ref[h].astype(F32) + before + behind).astype(BF16)
        return carry

    lax.fori_loop(1, SPLIT, fix, 0)
    store = pltpu.make_async_copy(o_ref.at[inner], out_ref.at[inner], sem.at[1])
    store.start()
    for done in (pl.ds(SPLIT, rows - SPLIT), pl.ds(0, 1)):
        pltpu.make_async_copy(o_ref.at[done], out_ref.at[done], sem.at[0]).wait()
    store.wait()


def final_rows(pieces, me_ref, x_ref, pre_ref, w_ref, affine_ref, o_ref, finish=None):
    channels = x_ref.shape[1]
    count = w_ref.shape[0]
    size = channels - count
    mixed = {}
    for s, piece in pieces:
        for r in range(HS):
            mixed[s, r] = dot(w_ref[...], piece[r * CF : (r + 1) * CF])
    for k in range(channels // size):
        span = slice(k * size, (k + 1) * size)
        scale, shift = affine_ref[span, 0:1], affine_ref[span, 1:2]
        for s, _ in pieces:
            first = HS * lax.bitwise_xor(me_ref[0], s)
            for r in range(HS):
                pre = pre_ref[first + r, span].astype(F32)
                if k:
                    pre = pre + mixed[s, r][(k - 1) * size : k * size]
                act = jnp.maximum(scale * pre + shift, 0.0)
                o_ref[first + r, span] = (x_ref[first + r, span].astype(F32) + act).astype(BF16)
        if finish is not None:
            finish(k, span)


def final_near_body(me_ref, x_ref, pre_ref, w_ref, affine_ref, t_ref, d_ref, next_ref, o_ref, table, sem):
    load = pltpu.make_async_copy(t_ref.at[me_ref[0]], table, sem.at[0])
    load.start()
    data = d_ref[...].T
    load.wait()
    near = dot(data, table[...]).astype(BF16)
    final_rows(((0, near), (1, next_ref)), me_ref, x_ref, pre_ref, w_ref, affine_ref, o_ref)


def final_far_body(me_ref, x_ref, pre_ref, w_ref, affine_ref, far_ref, given_ref, o_ref):
    final_rows(((2, far_ref),), me_ref, x_ref, pre_ref, w_ref, affine_ref, o_ref)


def final_last_body(me_ref, x_ref, pre_ref, w_ref, affine_ref, last_ref, given_ref, o_ref, out_ref, held, sem):
    copies = []

    def finish(k, span):
        held[span] = jnp.swapaxes(o_ref[:, span, :], 0, 1)
        copies.append(pltpu.make_async_copy(held.at[span], out_ref.at[span], sem.at[k]))
        copies[-1].start()

    final_rows(((3, last_ref),), me_ref, x_ref, pre_ref, w_ref, affine_ref, o_ref, finish)
    for copy in copies:
        copy.wait()


def shift_along(block, axis, step):
    count = lax.axis_size(axis)
    pairs = [(i, i + step) for i in range(count) if 0 <= i + step < count]
    return lax.ppermute(block, axis, pairs)


def swap(block, s):
    return lax.ppermute(block, "col", [(i, i ^ s) for i in range(COLS)])


def after(value, *others):
    return lax.optimization_barrier((value,) + others)


def per_device(
    image,
    from_local,
    from_global,
    section_weight,
    section_scale,
    section_shift,
    fourier_weight,
    fourier_scale,
    fourier_shift,
    mix_weight,
    out_scale,
    out_shift,
):
    channels, rows, width = image.shape
    cl = from_local.shape[2]
    cg = channels - cl
    me = lax.axis_index("col").astype(jnp.int32).reshape(1)
    z = jnp.logical_and(lax.axis_index("row") == 0, lax.axis_index("col") == 0).astype(jnp.int32).reshape(1)
    shape = jax.ShapeDtypeStruct
    dma = pltpu.SemaphoreType.DMA

    whole = shape((rows, channels, width), BF16)
    block, block_ends = shape((LANES, width), BF16), shape((LANES + 2 * rows, width), BF16)
    x, far, section_affine = call(
        first_body,
        (whole, block, shape((CF, 2), F32)),
        (me, image, section_weight, section_scale[None], section_shift[None]),
        smem=(0,),
        hbm=(1, 2, 3, 4),
        scratch=[
            pltpu.VMEM((channels, rows, width), BF16),
            pltpu.VMEM((CF, cg), BF16),
            pltpu.VMEM((1, CF), F32),
            pltpu.VMEM((1, CF), F32),
            dma((PARTS + 3,)),
        ],
    )
    far = swap(far, 2)
    near, other, last = call(
        rest_body, (block, block_ends, block_ends), (me, x, section_weight, section_affine), smem=(0,)
    )
    last, other = swap(last, 3), swap(other, 1)

    weights = (jnp.transpose(from_local, (0, 2, 1)), from_global, mix_weight, section_weight, section_affine)
    scratch = [
        pltpu.VMEM((rows, channels, width), BF16),
        pltpu.VMEM((2, LANE, channels), BF16),
        pltpu.VMEM((2, channels, LANE), F32),
        pltpu.VMEM((3 * channels, 3 * cl), BF16),
        pltpu.VMEM((3 * cl, 3 * cg), BF16),
        dma((2,)),
    ]
    pre = call(
        conv_inner_body,
        whole,
        (x,) + weights,
        hbm_out=(0,),
        stage=tuple(range(1, 6)),
        flops=10**9,
        scratch=scratch[:1] + scratch[2:],
    )
    fwd_w, inv_w = (jnp.asarray(t) for t in width_tables())
    part = call(width_near_body, shape((W, LANES), F32), (me, fwd_w, near, other), smem=(0,))
    part, pre = after(part, pre)
    spectra = call(
        width_far_body,
        shape((W, LANES), BF16),
        (me, fwd_w, part, far, last),
        smem=(0,),
        hbm_out=(0,),
        scratch=[pltpu.VMEM((W, LANES), BF16), dma((4,))],
    )
    spectra, other, last = after(spectra, other, last)
    spectra = lax.all_to_all(
        spectra.reshape(PEERS, 2 * NF, LANES), ("row", "col"), split_axis=0, concat_axis=0, tiled=True
    )
    ends = shape((channels + 2 * rows, width), BF16)
    down, up, sides = call(
        halo_body, (ends, ends, shape((2 * rows, channels), BF16)), (me, x, other, last), smem=(0,)
    )
    above, below = shift_along(down, "row", 1), shift_along(up, "row", -1)

    tables = [jnp.asarray(t) for t in height_tables() + (twiddles(),)]
    tables += [fourier_weight, fourier_scale[None], fourier_shift[None]]
    sizes = [t.shape[1:] if i in (2, 3) else t.shape for i, t in enumerate(tables)]
    returned = call(
        middle_body,
        shape((PEERS, 2 * NF, LANES), BF16),
        (z, spectra, *tables),
        smem=(0,),
        hbm=range(2, 10),
        hbm_out=(0,),
        limit=24,
        scratch=[pltpu.VMEM(s, t.dtype) for s, t in zip(sizes, tables)]
        + [
            pltpu.VMEM((W, WIDE), BF16),
            pltpu.VMEM((2 * NF, MID, LANES), BF16),
            pltpu.VMEM((PEERS, 2 * NF, LANES), BF16),
            dma((12,)),
        ],
    )
    returned, above, below = after(returned, above, below)
    returned = lax.all_to_all(returned, ("row", "col"), split_axis=0, concat_axis=0, tiled=True).reshape(W, LANES)
    pre = call(
        conv_outer_body,
        whole,
        (x, sides) + weights + (above, below, pre),
        hbm=(9,),
        hbm_out=(0,),
        stage=tuple(range(1, 9)),
        flops=10**9,
        input_output_aliases={9: 0},
        scratch=scratch,
    )
    returned, pre = after(returned, pre)

    piece = shape((LANES, width), BF16)
    affine = jnp.stack([out_scale, out_shift], 1)
    far, last, other = call(
        functools.partial(inverse_body, (2, 3, 1)),
        (piece,) * 3,
        (me, inv_w, returned),
        smem=(0,),
        hbm=(1,),
        scratch=[pltpu.VMEM((3, W, width), BF16), dma((3,))],
    )
    far, last, other = swap(far, 2), swap(last, 3), swap(other, 1)
    common = (me, x, pre, mix_weight, affine)
    half = call(
        final_near_body,
        whole,
        common + (inv_w, returned, other),
        smem=(0,),
        hbm=(5,),
        stage=(2, 3, 4),
        scratch=[pltpu.VMEM((W, width), BF16), dma((1,))],
    )
    half = call(
        final_far_body, whole, common + (far, half), smem=(0,), stage=(2, 3, 4), input_output_aliases={6: 0}
    )
    _, result = call(
        final_last_body,
        (whole, shape(image.shape, BF16)),
        common + (last, half),
        smem=(0,),
        hbm_out=(1,),
        input_output_aliases={6: 0},
        scratch=[pltpu.VMEM(image.shape, BF16), dma((8,))],
    )
    return result


def solution(mesh):
    return jax.shard_map(
        per_device,
        mesh=mesh,
        in_specs=(P("img", "row", "col"), P(), P(), P(), P(), P(), P(), P(), P(), P(), P(), P()),
        out_specs=P("img", "row", "col"),
        check_vma=False,
    )
```

```python
import functools
import math

import jax
import jax.numpy as jnp
import numpy as np
from jax import lax
from jax.experimental import pallas as pl
from jax.experimental.pallas import tpu as pltpu
from jax.sharding import PartitionSpec as P

F32 = jnp.float32
BF16 = jnp.bfloat16
MIB = 1024 * 1024

H, W = 256, 1024
ROWS, COLS = 16, 4
PEERS = ROWS * COLS
NF = W // 2 // PEERS
CF = 96
HS = H // PEERS
LANES = HS * CF
LANE = 128
WIDE = HS * LANE
MID = H // HS
PARTS = 8
SPLIT = 9


def bf(table):
    return np.asarray(table, np.float32).astype(jnp.bfloat16)


@functools.lru_cache(None)
def width_tables():
    k = np.arange(W // 2)
    w = np.arange(W)
    angle = 2 * math.pi / W * ((w[:, None] * k[None, :]) % W)
    alternate = np.where(w % 2 == 0, 1.0, -1.0)
    cos, sin = np.cos(angle), np.sin(angle)
    fwd = np.stack([cos, np.where(k[None, :] == 0, alternate[:, None], -sin)], 0)
    inv = np.stack([np.where(k[None, :] == 0, 1.0, 2.0) * cos, np.where(k[None, :] == 0, alternate[:, None], -2.0 * sin)], 0)
    order = lambda t: t.reshape(2, W, PEERS, NF).transpose(2, 0, 3, 1).reshape(W, W)
    norm = 1.0 / math.sqrt(W)
    fwd = (order(fwd) * norm).reshape(W, COLS, W // COLS).transpose(1, 0, 2)
    inv = (order(inv) * norm).reshape(W, COLS, W // COLS).transpose(1, 0, 2)
    return bf(fwd), bf(inv)


@functools.lru_cache(None)
def height_tables():
    m = np.arange(MID)
    angle = 2 * math.pi / MID * ((m[:, None] * m[None, :]) % MID)
    cos, sin, zero = np.cos(angle), np.sin(angle), np.zeros((MID, MID))
    norm = 1.0 / math.sqrt(H)
    fwd = np.block([[cos, sin], [-sin, cos]])
    inv = np.block([[cos, -sin], [sin, cos]])
    none = np.zeros_like(fwd)
    pair = lambda t: np.block([[t, none], [none, t]])
    fwd_edge = np.stack(
        [np.block([[fwd], [none]]), np.block([[cos, zero], [-sin, zero], [zero, cos], [zero, -sin]])], 0
    )
    inv_edge = np.stack(
        [np.block([[inv, none]]), np.block([[cos, -sin, zero, zero], [zero, zero, cos, -sin]])], 0
    )
    inv_edge = inv_edge.reshape(2, 2 * MID, 2, 2 * MID).transpose(0, 2, 1, 3).reshape(2, 4 * MID, 2 * MID)
    tw = twiddles().reshape(2, MID, 2, 2 * LANE).transpose(0, 2, 1, 3).reshape(4 * MID, 2 * LANE)
    high = bf(tw)
    low = bf(tw - high.astype(np.float32))
    pairs = np.stack([bf(pair(fwd) * norm), bf(pair(inv) * norm), high, low], 0)
    return pairs, bf(fwd_edge * norm), bf(inv_edge * norm)


@functools.lru_cache(None)
def twiddles():
    m = np.arange(MID)[:, None]
    r = np.repeat(np.arange(HS), LANE)[None, :]
    angle = 2 * math.pi / H * (m * r)
    return np.stack([np.cos(angle), -np.sin(angle)], 0).astype(np.float32)


def dot(a, b):
    return jnp.dot(a, b, preferred_element_type=F32)


def dot_nt(a, b):
    return lax.dot_general(a, b, (((1,), (1,)), ((), ())), preferred_element_type=F32)


def staged(body, staged_at, total, outs, refs):
    ins, rest = list(refs[:total]), refs[total:]
    count = len(staged_at)
    targets, sem, rest = rest[outs : outs + count], rest[outs + count], rest[:outs] + rest[outs + count + 1 :]
    loads = [pltpu.make_async_copy(ins[i], t, sem.at[n]) for n, (i, t) in enumerate(zip(staged_at, targets))]
    for load in loads:
        load.start()
    for i, t in zip(staged_at, targets):
        ins[i] = t
    for load in loads:
        load.wait()
    body(*ins, *rest)


def call(body, out_shape, operands, smem=(), hbm=(), stage=(), hbm_out=(), limit=16, flops=10**6, scratch=(), **kw):
    place = lambda i: pltpu.SMEM if i in smem else pltpu.HBM if i in hbm or i in stage else pltpu.VMEM
    single = not isinstance(out_shape, tuple)
    outs = [out_shape] if single else list(out_shape)
    spaces = [pltpu.HBM if i in hbm_out else pltpu.VMEM for i in range(len(outs))]
    shapes = [space(s.shape, s.dtype) for space, s in zip(spaces, outs)]
    specs = [pl.BlockSpec(memory_space=space) for space in spaces]
    operands = [v if i in smem else pltpu.with_memory_space_constraint(v, place(i)) for i, v in enumerate(operands)]
    if stage:
        inner, total = body, len(operands)
        body = lambda *refs: staged(inner, stage, total, len(outs), refs)
        held = [pltpu.VMEM(operands[i].shape, operands[i].dtype) for i in stage]
        scratch = held + [pltpu.SemaphoreType.DMA((len(stage),))] + list(scratch)
    return pl.pallas_call(
        body,
        out_shape=shapes[0] if single else tuple(shapes),
        in_specs=[pl.BlockSpec(memory_space=place(i)) for i in range(len(operands))],
        out_specs=specs[0] if single else tuple(specs),
        scratch_shapes=scratch,
        compiler_params=pltpu.CompilerParams(vmem_limit_bytes=limit * MIB),
        cost_estimate=pl.CostEstimate(flops=flops, bytes_accessed=flops // 1000, transcendentals=0),
        **kw,
    )(*operands)


def column(row):
    count = row.shape[1]
    diagonal = lax.broadcasted_iota(jnp.int32, (count, count), 0) == lax.broadcasted_iota(jnp.int32, (count, count), 1)
    return jnp.sum(jnp.where(diagonal, jnp.broadcast_to(row, (count, count)), 0.0), 1, keepdims=True)


def section_rows(weight, scale, shift, x):
    return jnp.maximum(scale * dot(weight, x) + shift, 0.0).astype(BF16)


def first_body(
    me_ref, image_ref, w_ref, scale_ref, shift_ref, x_ref, far_ref, affine_ref, held, weight, scale_row, shift_row, sem
):
    channels = image_ref.shape[0]
    size = channels // PARTS
    small = [(w_ref, weight), (scale_ref, scale_row), (shift_ref, shift_row)]
    others = [pltpu.make_async_copy(a, b, sem.at[PARTS + i]) for i, (a, b) in enumerate(small)]
    loads = []
    for i in range(PARTS):
        span = pl.ds(i * size, size)
        loads.append(pltpu.make_async_copy(image_ref.at[span], held.at[span], sem.at[i]))
    for load in others + loads[::-1]:
        load.start()
    for load in others:
        load.wait()
    scale, shift = column(scale_row[...]), column(shift_row[...])
    affine_ref[:, 0:1] = scale
    affine_ref[:, 1:2] = shift
    for i in range(PARTS - 1, -1, -1):
        span = slice(i * size, (i + 1) * size)
        loads[i].wait()
        x_ref[:, span, :] = jnp.swapaxes(held[span], 0, 1)
    first = HS * lax.bitwise_xor(me_ref[0], 2)
    skip = channels - w_ref.shape[1]
    for r in range(HS):
        far_ref[r * CF : (r + 1) * CF] = section_rows(weight[...], scale, shift, x_ref[first + r, skip:, :])


def rest_body(me_ref, x_ref, w_ref, affine_ref, near_ref, next_ref, last_ref):
    rows, channels, width = x_ref.shape
    skip = channels - w_ref.shape[1]
    scale, shift = affine_ref[:, 0:1], affine_ref[:, 1:2]
    for s, o_ref in ((3, last_ref), (1, next_ref), (0, near_ref)):
        first = HS * lax.bitwise_xor(me_ref[0], s)
        for r in range(HS):
            o_ref[r * CF : (r + 1) * CF] = section_rows(w_ref[...], scale, shift, x_ref[first + r, skip:, :])
    place = lax.broadcasted_iota(jnp.int32, (2 * rows, width), 0)
    lane = lax.broadcasted_iota(jnp.int32, (2 * rows, width), 1)
    ends = jnp.zeros((2 * rows, channels), F32)
    for h in range(rows):
        pick = ((place == h) & (lane == 0)) | ((place == rows + h) & (lane == width - 1))
        ends = ends + dot_nt(pick.astype(F32).astype(BF16), x_ref[h])
    ends = ends.astype(BF16)
    last_ref[LANES:] = ends
    next_ref[LANES:] = ends


def halo_body(
    me_ref,
    z_ref,
    x_ref,
    next_ref,
    last_ref,
    fw_ref,
    pair_ref,
    fwd_edge_ref,
    inv_edge_ref,
    down_ref,
    up_ref,
    side_ref,
    kept_ref,
    sem,
):
    rows, channels = side_ref.shape[0] // 2, side_ref.shape[1]
    me, z = me_ref[0], z_ref[0]
    loads = [
        pltpu.make_async_copy(pair_ref, kept_ref.at[pl.ds(0, 4)], sem.at[0]),
        pltpu.make_async_copy(fwd_edge_ref.at[z], kept_ref.at[4, :, pl.ds(0, 2 * MID)], sem.at[1]),
        pltpu.make_async_copy(inv_edge_ref.at[z], kept_ref.at[4, :, pl.ds(2 * MID, 2 * MID)], sem.at[2]),
        pltpu.make_async_copy(x_ref.at[rows - 1], down_ref.at[pl.ds(0, channels)], sem.at[3]),
        pltpu.make_async_copy(x_ref.at[0], up_ref.at[pl.ds(0, channels)], sem.at[4]),
    ]
    for load in loads:
        load.start()
    odd = lax.rem(me, 2).astype(F32)
    near = next_ref[LANES:].astype(F32)
    far = last_ref[LANES:].astype(F32)
    even = 1.0 - odd
    left = (odd * near[rows:] + even * far[rows:]) * jnp.where(me > 0, 1.0, 0.0)
    right = (odd * far[:rows] + even * near[:rows]) * jnp.where(me < COLS - 1, 1.0, 0.0)
    sides = jnp.concatenate([left, right], 0).astype(BF16)
    side_ref[...] = sides
    down_ref[channels:] = sides
    up_ref[channels:] = sides
    mixer = spread(fw_ref[...].T)
    low = jnp.zeros((LANE - CF, 2 * LANE), BF16)
    kept_ref[5] = jnp.concatenate([mixer[:CF], low, mixer[CF:], low], 0)
    for load in loads:
        load.wait()


def width_near_body(me_ref, t_ref, near_ref, next_ref, o_ref):
    me = me_ref[0]
    o_ref[...] = dot_nt(t_ref[me], near_ref[...]) + dot_nt(t_ref[lax.bitwise_xor(me, 1)], next_ref[:LANES])


def width_far_body(me_ref, t_ref, part_ref, far_ref, last_ref, o_ref, held, sem):
    me = me_ref[0]
    size = o_ref.shape[0] // 4
    copies = []
    for i in range(4):
        span = pl.ds(i * size, size)
        total = part_ref[span] + dot_nt(t_ref[lax.bitwise_xor(me, 2), span], far_ref[...])
        held[span] = (total + dot_nt(t_ref[lax.bitwise_xor(me, 3), span], last_ref[:LANES])).astype(BF16)
        copies.append(pltpu.make_async_copy(held.at[span], o_ref.at[span], sem.at[i]))
        copies[-1].start()
    for copy in copies:
        copy.wait()


def widen(d):
    gap = jnp.zeros((d.shape[0], LANE - CF), d.dtype)
    return jnp.concatenate(sum([[d[:, CF * r : CF * r + CF], gap] for r in range(HS)], []), 1)


def narrow(d):
    return jnp.concatenate([d[:, LANE * r : LANE * r + CF] for r in range(HS)], 1)


def turns(real, imag):
    s02r, d02r, s13r, d13r = real[0] + real[2], real[0] - real[2], real[1] + real[3], real[1] - real[3]
    s02i, d02i, s13i, d13i = imag[0] + imag[2], imag[0] - imag[2], imag[1] + imag[3], imag[1] - imag[3]
    return (
        (s02r + s13r, s02i + s13i),
        (d02r + d13i, d02i - d13r),
        (s02r - s13r, s02i - s13i),
        (d02r - d13i, d02i + d13r),
    )


def spread(t):
    gap = jnp.zeros((t.shape[0], LANE - CF), t.dtype)
    return jnp.concatenate([t[:, :CF], gap, t[:, CF:], gap], 1)


def middle_body(d_ref, x_ref, scale_ref, shift_ref, o_ref, scale_row, shift_row, tw_ref, edge_ref, wide, back_ref, held, sem):
    loads = [
        pltpu.make_async_copy(scale_ref, scale_row, sem.at[0]),
        pltpu.make_async_copy(shift_ref, shift_row, sem.at[1]),
    ]
    for load in loads:
        load.start()
    first = 0
    wide[...] = widen(jnp.swapaxes(d_ref[...], 0, 1).reshape(W, LANES))
    fwd, inv, edges = x_ref.at[first], x_ref.at[first + 1], x_ref.at[first + 4]
    tw = x_ref[first + 2].astype(F32) + x_ref[first + 3].astype(F32)
    for i in range(4):
        half = slice((i % 2) * 2 * LANE, (i % 2 + 1) * 2 * LANE)
        tw_ref[i // 2, :, half] = tw[i * MID : (i + 1) * MID]
    twr, twi = tw_ref[0], tw_ref[1]
    fwd_edge = edges.at[:, : 2 * MID][...]
    edge_ref[:, : 2 * MID] = edges[: 2 * MID, 2 * MID :]
    edge_ref[:, 2 * MID :] = edges[2 * MID :, 2 * MID :]
    inv_edge = edge_ref[...]
    mixer = x_ref[first + 5]
    for load in loads:
        load.wait()
    scale, shift = spread(scale_row[...]), spread(shift_row[...])
    groups = [slice(LANE * r, LANE * r + LANE) for r in range(HS)]
    for own in ((0,), (1, 2), (3, 4), (5, 6), (7,)):
        data = jnp.concatenate(
            [wide[(p * NF + f) * MID : (p * NF + f + 1) * MID] for f in own for p in range(2)], 0
        )
        count = 2 if own == (0,) else len(own)
        half = 2 * MID * len(own)
        ahead = fwd_edge if own == (0,) else fwd[:half, :half]
        u = dot(ahead, data)
        rows = []
        for f in range(count):
            ur = u[2 * f * MID : (2 * f + 1) * MID]
            ui = u[(2 * f + 1) * MID : (2 * f + 2) * MID]
            vr, vi = [ur[:, groups[0]]], [ui[:, groups[0]]]
            for g in groups[1:]:
                vr.append(ur[:, g] * twr[:, g] - ui[:, g] * twi[:, g])
                vi.append(ur[:, g] * twi[:, g] + ui[:, g] * twr[:, g])
            for real, imag in turns(vr, vi):
                rows.append(jnp.concatenate([real, imag], 1).astype(BF16))
        mixed = dot(jnp.concatenate(rows, 0), mixer)
        active = jnp.maximum(scale * mixed + shift, 0.0)
        rows = []
        for f in range(count):
            part = [active[(HS * f + j) * MID : (HS * f + j + 1) * MID] for j in (0, 3, 2, 1)]
            turned = turns([v[:, :LANE] for v in part], [v[:, LANE:] for v in part])
            br, bi = [turned[0][0].astype(BF16)], [turned[0][1].astype(BF16)]
            for g, (real, imag) in zip(groups[1:], turned[1:]):
                br.append((real * twr[:, g] + imag * twi[:, g]).astype(BF16))
                bi.append((imag * twr[:, g] - real * twi[:, g]).astype(BF16))
            rows.append(jnp.concatenate(br, 1))
            rows.append(jnp.concatenate(bi, 1))
        behind = inv_edge if own == (0,) else inv[:half, :half]
        done = narrow(dot(behind, jnp.concatenate(rows, 0)).astype(BF16))
        for i, f in enumerate(own):
            for p in range(2):
                back_ref[p * NF + f] = done[(2 * i + p) * MID : (2 * i + p + 1) * MID]
    stores = []
    size = MID // 4
    for i in range(4):
        span = pl.ds(i * size, size)
        held[span] = jnp.swapaxes(back_ref[:, i * size : (i + 1) * size, :], 0, 1)
        stores.append(pltpu.make_async_copy(held.at[span], o_ref.at[span], sem.at[8 + i]))
        stores[-1].start()
    for store in stores:
        store.wait()


def inverse_body(t_ref, d_ref, *outs):
    data = d_ref[...].T
    for i, o_ref in enumerate(outs):
        o_ref[...] = dot(data, t_ref[i]).astype(BF16)


def conv_setup(fl_ref, fg_ref, wl_ref, wg_ref):
    cl, channels = fl_ref.shape[1], fl_ref.shape[2]
    for dx in range(3):
        wl_ref[dx * channels : (dx + 1) * channels] = jnp.concatenate([fl_ref[3 * dy + dx] for dy in range(3)], 0).T
        wg_ref[dx * cl : (dx + 1) * cl] = jnp.concatenate([fg_ref[3 * dy + dx] for dy in range(3)], 1)


def conv_edges(side_ref, around, wl_ref, wg_ref, cols, edge):
    rows, channels = side_ref.shape[0] // 2, side_ref.shape[1]
    cl, cg = wl_ref.shape[1] // 3, wg_ref.shape[1] // 3
    cols[...] = jnp.zeros_like(cols)
    for side in range(2):
        own = pl.ds(side * rows, rows)
        cols[side, rows : 2 * rows] = side_ref[own]
        for i, other in enumerate(around):
            cols[side, 2 * i * rows : (2 * i + 1) * rows] = other[pl.ds(channels + side * rows, rows)]
        dx = 2 * side
        total = None
        for dy in range(3):
            taps = wl_ref[dx * channels : (dx + 1) * channels, dy * cl : (dy + 1) * cl]
            term = dot_nt(taps, cols[side, :, :cl])
            taps = wg_ref[dx * cl : (dx + 1) * cl, dy * cg : (dy + 1) * cg]
            extra = dot_nt(taps, cols[side, :, cl:])
            term = jnp.concatenate([term[:cl] + extra, term[cl:]], 0)
            term = pltpu.roll(term, LANE - (rows - 1 + dy), 1)
            total = term if total is None else total + term
        edge[side] = total


def edge_lanes(h, edge, before, behind):
    lane = lax.broadcasted_iota(jnp.int32, edge.shape[1:], 1)
    width = before.shape[1]
    first = pltpu.roll(edge[0], lax.rem(LANE - h, LANE), 1)
    final = pltpu.roll(edge[1], LANE - 1 - h, 1)
    before = jnp.concatenate([jnp.where(lane == 0, first, before[:, :LANE]), before[:, LANE:]], 1)
    last = jnp.where(lane == LANE - 1, final, behind[:, width - LANE :])
    return before, jnp.concatenate([behind[:, : width - LANE], last], 1)


def conv_row(h, three, wl_ref, wg_ref, wm_ref, ws_ref, affine_ref, edge, o_ref, out_ref, sem):
    channels, width = three[1].shape
    cl = wl_ref.shape[1] // 3
    local = jnp.concatenate([row[:cl] for row in three], 0)
    other = jnp.concatenate([row[cl:] for row in three], 0)
    parts = []
    for dx in range(3):
        yl = dot(wl_ref[dx * channels : (dx + 1) * channels], local)
        yg = dot(wg_ref[dx * cl : (dx + 1) * cl], other)
        parts.append(jnp.concatenate([yl[:cl] + yg, yl[cl:]], 0))
    before = pltpu.roll(parts[0], 1, 1)
    behind = pltpu.roll(parts[2], width - 1, 1)
    before, behind = edge_lanes(h, edge, before, behind)
    acc = parts[1] + before + behind
    mix = dot(wm_ref[...], section_rows(ws_ref[...], affine_ref[:, 0:1], affine_ref[:, 1:2], three[1][cl:]))
    o_ref[h, :cl] = acc[:cl].astype(BF16)
    o_ref[h, cl:] = (acc[cl:] + mix).astype(BF16)
    pltpu.make_async_copy(o_ref.at[h], out_ref.at[h], sem.at[0]).start()


def conv_inner_body(
    x_ref, fl_ref, fg_ref, wm_ref, ws_ref, affine_ref, out_ref, kept_ref, o_ref, edge, wl_ref, wg_ref, sem
):
    keep = pltpu.make_async_copy(x_ref, kept_ref, sem.at[1])
    keep.start()
    conv_setup(fl_ref, fg_ref, wl_ref, wg_ref)
    edge[...] = jnp.zeros_like(edge)

    def step(h, carry):
        three = [x_ref[h - 1], x_ref[h], x_ref[h + 1]]
        conv_row(h, three, wl_ref, wg_ref, wm_ref, ws_ref, affine_ref, edge, o_ref, out_ref, sem)
        return carry

    lax.fori_loop(1, SPLIT, step, 0)
    done = pl.ds(1, SPLIT - 1)
    pltpu.make_async_copy(o_ref.at[done], out_ref.at[done], sem.at[0]).wait()
    keep.wait()


def conv_outer_body(
    x_ref,
    side_ref,
    fl_ref,
    fg_ref,
    wm_ref,
    ws_ref,
    affine_ref,
    above_ref,
    below_ref,
    given_ref,
    table_ref,
    me_ref,
    out_ref,
    kept_ref,
    o_ref,
    cols,
    edge,
    wl_ref,
    wg_ref,
    sem,
):
    rows, channels, width = x_ref.shape
    inner = pl.ds(1, SPLIT - 1)
    load = pltpu.make_async_copy(given_ref.at[inner], o_ref.at[inner], sem.at[1])
    load.start()
    keeps = []
    for i, s in enumerate((2, 3, 1)):
        source = table_ref.at[lax.bitwise_xor(me_ref[0], s)]
        keeps.append(pltpu.make_async_copy(source, kept_ref.at[i], sem.at[2 + i]))
        keeps[-1].start()
    conv_setup(fl_ref, fg_ref, wl_ref, wg_ref)
    conv_edges(side_ref, (above_ref, below_ref), wl_ref, wg_ref, cols, edge)
    rest = (wl_ref, wg_ref, wm_ref, ws_ref, affine_ref, edge, o_ref, out_ref, sem)

    def step(h, carry):
        conv_row(h, [x_ref[h - 1], x_ref[h], x_ref[h + 1]], *rest)
        return carry

    lax.fori_loop(SPLIT, rows - 1, step, 0)
    conv_row(0, [above_ref[:channels], x_ref[0], x_ref[1]], *rest)
    conv_row(rows - 1, [x_ref[rows - 2], x_ref[rows - 1], below_ref[:channels]], *rest)
    load.wait()

    def fix(h, carry):
        none = jnp.zeros((channels, width), F32)
        before, behind = edge_lanes(h, edge, none, none)
        o_ref[h] = (o_ref[h].astype(F32) + before + behind).astype(BF16)
        return carry

    lax.fori_loop(1, SPLIT, fix, 0)
    store = pltpu.make_async_copy(o_ref.at[inner], out_ref.at[inner], sem.at[1])
    store.start()
    for done in (pl.ds(SPLIT, rows - SPLIT), pl.ds(0, 1)):
        pltpu.make_async_copy(o_ref.at[done], out_ref.at[done], sem.at[0]).wait()
    store.wait()
    for keep in keeps:
        keep.wait()


def final_rows(pieces, me_ref, x_ref, pre_ref, w_ref, affine_ref, o_ref, finish=None):
    channels = x_ref.shape[1]
    count = w_ref.shape[0]
    size = channels - count
    mixed = {}
    for s, piece in pieces:
        for r in range(HS):
            mixed[s, r] = dot(w_ref[...], piece[r * CF : (r + 1) * CF])
    for k in range(channels // size):
        span = slice(k * size, (k + 1) * size)
        scale, shift = affine_ref[span, 0:1], affine_ref[span, 1:2]
        for s, _ in pieces:
            first = HS * lax.bitwise_xor(me_ref[0], s)
            for r in range(HS):
                pre = pre_ref[first + r, span].astype(F32)
                if k:
                    pre = pre + mixed[s, r][(k - 1) * size : k * size]
                act = jnp.maximum(scale * pre + shift, 0.0)
                o_ref[first + r, span] = (x_ref[first + r, span].astype(F32) + act).astype(BF16)
        if finish is not None:
            finish(k, span)


def fetch_rows(x_ref, pre_ref, first, count, x, pre, sem):
    span = pl.ds(first, count)
    loads = [
        pltpu.make_async_copy(x_ref.at[span], x.at[span], sem.at[0]),
        pltpu.make_async_copy(pre_ref.at[span], pre.at[span], sem.at[1]),
    ]
    for load in loads:
        load.start()
    return loads


def final_near_body(
    me_ref, x_ref, pre_ref, w_ref, scale_ref, shift_ref, t_ref, d_ref, next_ref, o_ref, affine_ref, x, pre, table, sem
):
    me = me_ref[0]
    load = pltpu.make_async_copy(t_ref.at[me], table, sem.at[2])
    load.start()
    loads = fetch_rows(x_ref, pre_ref, 2 * HS * (me // 2), 2 * HS, x, pre, sem)
    affine_ref[:, 0:1] = column(scale_ref[...])
    affine_ref[:, 1:2] = column(shift_ref[...])
    data = d_ref[...].T
    load.wait()
    near = dot(data, table[...]).astype(BF16)
    for load in loads:
        load.wait()
    final_rows(((0, near), (1, next_ref)), me_ref, x, pre, w_ref, affine_ref, o_ref)


def final_far_body(me_ref, x_ref, pre_ref, w_ref, affine_ref, far_ref, given_ref, o_ref, x, pre, sem):
    loads = fetch_rows(x_ref, pre_ref, HS * lax.bitwise_xor(me_ref[0], 2), HS, x, pre, sem)
    for load in loads:
        load.wait()
    final_rows(((2, far_ref),), me_ref, x, pre, w_ref, affine_ref, o_ref)


def final_last_body(me_ref, x_ref, pre_ref, w_ref, affine_ref, last_ref, given_ref, o_ref, out_ref, held, sem):
    copies = []

    def finish(k, span):
        held[span] = jnp.swapaxes(o_ref[:, span, :], 0, 1)
        copies.append(pltpu.make_async_copy(held.at[span], out_ref.at[span], sem.at[k]))
        copies[-1].start()

    final_rows(((3, last_ref),), me_ref, x_ref, pre_ref, w_ref, affine_ref, o_ref, finish)
    for copy in copies:
        copy.wait()


def shift_along(block, axis, step):
    count = lax.axis_size(axis)
    pairs = [(i, i + step) for i in range(count) if 0 <= i + step < count]
    return lax.ppermute(block, axis, pairs)


def swap(block, s):
    return lax.ppermute(block, "col", [(i, i ^ s) for i in range(COLS)])


def after(value, *others):
    return lax.optimization_barrier((value,) + others)


def per_device(
    image,
    from_local,
    from_global,
    section_weight,
    section_scale,
    section_shift,
    fourier_weight,
    fourier_scale,
    fourier_shift,
    mix_weight,
    out_scale,
    out_shift,
):
    channels, rows, width = image.shape
    cl = from_local.shape[2]
    cg = channels - cl
    me = lax.axis_index("col").astype(jnp.int32).reshape(1)
    z = jnp.logical_and(lax.axis_index("row") == 0, lax.axis_index("col") == 0).astype(jnp.int32).reshape(1)
    shape = jax.ShapeDtypeStruct
    dma = pltpu.SemaphoreType.DMA

    whole = shape((rows, channels, width), BF16)
    block, block_ends = shape((LANES, width), BF16), shape((LANES + 2 * rows, width), BF16)
    x, far, section_affine = call(
        first_body,
        (whole, block, shape((CF, 2), F32)),
        (me, image, section_weight, section_scale[None], section_shift[None]),
        smem=(0,),
        hbm=(1, 2, 3, 4),
        scratch=[
            pltpu.VMEM((channels, rows, width), BF16),
            pltpu.VMEM((CF, cg), BF16),
            pltpu.VMEM((1, CF), F32),
            pltpu.VMEM((1, CF), F32),
            dma((PARTS + 3,)),
        ],
    )
    far = swap(far, 2)
    near, other, last = call(
        rest_body, (block, block_ends, block_ends), (me, x, section_weight, section_affine), smem=(0,)
    )
    last, other = swap(last, 3), swap(other, 1)

    weights = (jnp.transpose(from_local, (0, 2, 1)), from_global, mix_weight, section_weight, section_affine)
    scratch = [
        pltpu.VMEM((rows, channels, width), BF16),
        pltpu.VMEM((2, LANE, channels), BF16),
        pltpu.VMEM((2, channels, LANE), F32),
        pltpu.VMEM((3 * channels, 3 * cl), BF16),
        pltpu.VMEM((3 * cl, 3 * cg), BF16),
        dma((5,)),
    ]
    pre, x = call(
        conv_inner_body,
        (whole, whole),
        (x,) + weights,
        hbm_out=(0, 1),
        stage=tuple(range(1, 6)),
        flops=10**9,
        scratch=scratch[:1] + scratch[2:],
    )
    fwd_w, inv_w = (jnp.asarray(t) for t in width_tables())
    part = call(width_near_body, shape((W, LANES), F32), (me, fwd_w, near, other), smem=(0,))
    part, pre = after(part, pre)
    spectra = call(
        width_far_body,
        shape((W, LANES), BF16),
        (me, fwd_w, part, far, last),
        smem=(0,),
        hbm_out=(0,),
        scratch=[pltpu.VMEM((W, LANES), BF16), dma((4,))],
    )
    spectra, other, last = after(spectra, other, last)
    spectra = lax.all_to_all(
        spectra.reshape(PEERS, 2 * NF, LANES), ("row", "col"), split_axis=0, concat_axis=0, tiled=True
    )
    ends = shape((channels + 2 * rows, width), BF16)
    pairs, fwd_edge, inv_edge = (jnp.asarray(t) for t in height_tables())
    down, up, sides, kept = call(
        halo_body,
        (ends, ends, shape((2 * rows, channels), BF16), shape((6, channels, width), BF16)),
        (me, z, x, other, last, fourier_weight, pairs, fwd_edge, inv_edge),
        smem=(0, 1),
        hbm=(2, 6, 7, 8),
        stage=(5,),
        scratch=[dma((5,))],
    )
    above, below = shift_along(down, "row", 1), shift_along(up, "row", -1)

    returned = call(
        middle_body,
        shape((PEERS, 2 * NF, LANES), BF16),
        (spectra, kept, fourier_scale[None], fourier_shift[None]),
        hbm=(2, 3),
        hbm_out=(0,),
        limit=24,
        scratch=[
            pltpu.VMEM((1, 2 * CF), F32),
            pltpu.VMEM((1, 2 * CF), F32),
            pltpu.VMEM((2, MID, WIDE), F32),
            pltpu.VMEM((2 * MID, 4 * MID), BF16),
            pltpu.VMEM((W, WIDE), BF16),
            pltpu.VMEM((2 * NF, MID, LANES), BF16),
            pltpu.VMEM((PEERS, 2 * NF, LANES), BF16),
            dma((12,)),
        ],
    )
    returned, above, below = after(returned, above, below)
    returned = lax.all_to_all(returned, ("row", "col"), split_axis=0, concat_axis=0, tiled=True).reshape(W, LANES)
    pre, table = call(
        conv_outer_body,
        (whole, shape((3, W, width), BF16)),
        (x, sides) + weights + (above, below, pre, inv_w, me),
        smem=(11,),
        hbm=(9, 10),
        hbm_out=(0,),
        stage=tuple(range(7)),
        flops=10**9,
        input_output_aliases={9: 0},
        scratch=scratch,
    )

    piece = shape((LANES, width), BF16)
    far, last, other = call(inverse_body, (piece,) * 3, (table, returned))
    far, last, other = swap(far, 2), swap(last, 3), swap(other, 1)
    rows_held = [pltpu.VMEM(whole.shape, BF16), pltpu.VMEM(whole.shape, BF16)]
    half, affine = call(
        final_near_body,
        (whole, shape((channels, 2), F32)),
        (me, x, pre, mix_weight, out_scale[None], out_shift[None], inv_w, returned, other),
        smem=(0,),
        hbm=(1, 2, 6),
        stage=(3, 4, 5),
        scratch=rows_held + [pltpu.VMEM((W, width), BF16), dma((3,))],
    )
    common = (me, x, pre, mix_weight, affine)
    half = call(
        final_far_body,
        whole,
        common + (far, half),
        smem=(0,),
        hbm=(1, 2),
        input_output_aliases={6: 0},
        scratch=rows_held + [dma((2,))],
    )
    _, result = call(
        final_last_body,
        (whole, shape(image.shape, BF16)),
        common + (last, half),
        smem=(0,),
        hbm_out=(1,),
        input_output_aliases={6: 0},
        scratch=[pltpu.VMEM(image.shape, BF16), dma((8,))],
    )
    return result


def solution(mesh):
    return jax.shard_map(
        per_device,
        mesh=mesh,
        in_specs=(P("img", "row", "col"), P(), P(), P(), P(), P(), P(), P(), P(), P(), P(), P()),
        out_specs=P("img", "row", "col"),
        check_vma=False,
    )
```

```python
import functools
import math

import jax
import jax.numpy as jnp
import numpy as np
from jax import lax
from jax.experimental import pallas as pl
from jax.experimental.pallas import tpu as pltpu
from jax.sharding import PartitionSpec as P

F32 = jnp.float32
BF16 = jnp.bfloat16
MIB = 1024 * 1024

H, W = 256, 1024
ROWS, COLS = 16, 4
PEERS = ROWS * COLS
NF = W // 2 // PEERS
CF = 96
HS = H // PEERS
LANES = HS * CF
LANE = 128
WIDE = HS * LANE
MID = H // HS
PARTS = 8


def bf(table):
    return np.asarray(table, np.float32).astype(jnp.bfloat16)


@functools.lru_cache(None)
def width_tables():
    k = np.arange(W // 2)
    w = np.arange(W)
    angle = 2 * math.pi / W * ((w[:, None] * k[None, :]) % W)
    alternate = np.where(w % 2 == 0, 1.0, -1.0)
    cos, sin = np.cos(angle), np.sin(angle)
    fwd = np.stack([cos, np.where(k[None, :] == 0, alternate[:, None], -sin)], 0)
    inv = np.stack([np.where(k[None, :] == 0, 1.0, 2.0) * cos, np.where(k[None, :] == 0, alternate[:, None], -2.0 * sin)], 0)
    order = lambda t: t.reshape(2, W, PEERS, NF).transpose(2, 0, 3, 1).reshape(W, W)
    norm = 1.0 / math.sqrt(W)
    fwd = (order(fwd) * norm).reshape(W, COLS, W // COLS).transpose(1, 0, 2)
    inv = (order(inv) * norm).reshape(W, COLS, W // COLS).transpose(1, 0, 2)
    return bf(fwd), bf(inv)


@functools.lru_cache(None)
def height_tables():
    m = np.arange(MID)
    angle = 2 * math.pi / MID * ((m[:, None] * m[None, :]) % MID)
    cos, sin, zero = np.cos(angle), np.sin(angle), np.zeros((MID, MID))
    norm = 1.0 / math.sqrt(H)
    fwd = np.block([[cos, sin], [-sin, cos]])
    inv = np.block([[cos, -sin], [sin, cos]])
    none = np.zeros_like(fwd)
    pair = lambda t: np.block([[t, none], [none, t]])
    fwd_edge = np.stack(
        [np.block([[fwd], [none]]), np.block([[cos, zero], [-sin, zero], [zero, cos], [zero, -sin]])], 0
    )
    inv_edge = np.stack(
        [np.block([[inv, none]]), np.block([[cos, -sin, zero, zero], [zero, zero, cos, -sin]])], 0
    )
    inv_edge = inv_edge.reshape(2, 2 * MID, 2, 2 * MID).transpose(0, 2, 1, 3).reshape(2, 4 * MID, 2 * MID)
    tw = twiddles().reshape(2, MID, 2, 2 * LANE).transpose(0, 2, 1, 3).reshape(4 * MID, 2 * LANE)
    high = bf(tw)
    low = bf(tw - high.astype(np.float32))
    pairs = np.stack([bf(pair(fwd) * norm), bf(pair(inv) * norm), high, low], 0)
    return pairs, bf(fwd_edge * norm), bf(inv_edge * norm)


@functools.lru_cache(None)
def twiddles():
    m = np.arange(MID)[:, None]
    r = np.repeat(np.arange(HS), LANE)[None, :]
    angle = 2 * math.pi / H * (m * r)
    return np.stack([np.cos(angle), -np.sin(angle)], 0).astype(np.float32)


def dot(a, b):
    return jnp.dot(a, b, preferred_element_type=F32)


def dot_nt(a, b):
    return lax.dot_general(a, b, (((1,), (1,)), ((), ())), preferred_element_type=F32)


def staged(body, staged_at, total, outs, refs):
    ins, rest = list(refs[:total]), refs[total:]
    count = len(staged_at)
    targets, sem, rest = rest[outs : outs + count], rest[outs + count], rest[:outs] + rest[outs + count + 1 :]
    loads = [pltpu.make_async_copy(ins[i], t, sem.at[n]) for n, (i, t) in enumerate(zip(staged_at, targets))]
    for load in loads:
        load.start()
    for i, t in zip(staged_at, targets):
        ins[i] = t
    for load in loads:
        load.wait()
    body(*ins, *rest)


def call(body, out_shape, operands, smem=(), hbm=(), stage=(), hbm_out=(), limit=16, flops=10**6, scratch=(), **kw):
    place = lambda i: pltpu.SMEM if i in smem else pltpu.HBM if i in hbm or i in stage else pltpu.VMEM
    single = not isinstance(out_shape, tuple)
    outs = [out_shape] if single else list(out_shape)
    spaces = [pltpu.HBM if i in hbm_out else pltpu.VMEM for i in range(len(outs))]
    shapes = [space(s.shape, s.dtype) for space, s in zip(spaces, outs)]
    specs = [pl.BlockSpec(memory_space=space) for space in spaces]
    operands = [v if i in smem else pltpu.with_memory_space_constraint(v, place(i)) for i, v in enumerate(operands)]
    if stage:
        inner, total = body, len(operands)
        body = lambda *refs: staged(inner, stage, total, len(outs), refs)
        held = [pltpu.VMEM(operands[i].shape, operands[i].dtype) for i in stage]
        scratch = held + [pltpu.SemaphoreType.DMA((len(stage),))] + list(scratch)
    return pl.pallas_call(
        body,
        out_shape=shapes[0] if single else tuple(shapes),
        in_specs=[pl.BlockSpec(memory_space=place(i)) for i in range(len(operands))],
        out_specs=specs[0] if single else tuple(specs),
        scratch_shapes=scratch,
        compiler_params=pltpu.CompilerParams(vmem_limit_bytes=limit * MIB),
        cost_estimate=pl.CostEstimate(flops=flops, bytes_accessed=flops // 1000, transcendentals=0),
        **kw,
    )(*operands)


def column(row):
    count = row.shape[1]
    diagonal = lax.broadcasted_iota(jnp.int32, (count, count), 0) == lax.broadcasted_iota(jnp.int32, (count, count), 1)
    return jnp.sum(jnp.where(diagonal, jnp.broadcast_to(row, (count, count)), 0.0), 1, keepdims=True)


def section_rows(weight, scale, shift, x):
    return jnp.maximum(scale * dot(weight, x) + shift, 0.0).astype(BF16)


def first_body(
    me_ref, image_ref, w_ref, scale_ref, shift_ref, x_ref, far_ref, affine_ref, held, weight, scale_row, shift_row, sem
):
    channels = image_ref.shape[0]
    size = channels // PARTS
    small = [(w_ref, weight), (scale_ref, scale_row), (shift_ref, shift_row)]
    others = [pltpu.make_async_copy(a, b, sem.at[PARTS + i]) for i, (a, b) in enumerate(small)]
    loads = []
    for i in range(PARTS):
        span = pl.ds(i * size, size)
        loads.append(pltpu.make_async_copy(image_ref.at[span], held.at[span], sem.at[i]))
    for load in others + loads[::-1]:
        load.start()
    for load in others:
        load.wait()
    scale, shift = column(scale_row[...]), column(shift_row[...])
    affine_ref[:, 0:1] = scale
    affine_ref[:, 1:2] = shift
    for i in range(PARTS - 1, -1, -1):
        span = slice(i * size, (i + 1) * size)
        loads[i].wait()
        x_ref[:, span, :] = jnp.swapaxes(held[span], 0, 1)
    first = HS * lax.bitwise_xor(me_ref[0], 2)
    skip = channels - w_ref.shape[1]
    for r in range(HS):
        far_ref[r * CF : (r + 1) * CF] = section_rows(weight[...], scale, shift, x_ref[first + r, skip:, :])


def rest_body(me_ref, x_ref, w_ref, affine_ref, near_ref, next_ref, last_ref):
    rows, channels, width = x_ref.shape
    skip = channels - w_ref.shape[1]
    scale, shift = affine_ref[:, 0:1], affine_ref[:, 1:2]
    for s, o_ref in ((3, last_ref), (1, next_ref), (0, near_ref)):
        first = HS * lax.bitwise_xor(me_ref[0], s)
        for r in range(HS):
            o_ref[r * CF : (r + 1) * CF] = section_rows(w_ref[...], scale, shift, x_ref[first + r, skip:, :])
    place = lax.broadcasted_iota(jnp.int32, (2 * rows, width), 0)
    lane = lax.broadcasted_iota(jnp.int32, (2 * rows, width), 1)
    ends = jnp.zeros((2 * rows, channels), F32)
    for h in range(rows):
        pick = ((place == h) & (lane == 0)) | ((place == rows + h) & (lane == width - 1))
        ends = ends + dot_nt(pick.astype(F32).astype(BF16), x_ref[h])
    ends = ends.astype(BF16)
    last_ref[LANES:] = ends
    next_ref[LANES:] = ends


def halo_body(
    me_ref,
    z_ref,
    x_ref,
    next_ref,
    last_ref,
    fw_ref,
    pair_ref,
    fwd_edge_ref,
    inv_edge_ref,
    down_ref,
    up_ref,
    side_ref,
    kept_ref,
    sem,
):
    rows, channels = side_ref.shape[0] // 2, side_ref.shape[1]
    me, z = me_ref[0], z_ref[0]
    loads = [
        pltpu.make_async_copy(pair_ref, kept_ref.at[pl.ds(0, 4)], sem.at[0]),
        pltpu.make_async_copy(fwd_edge_ref.at[z], kept_ref.at[4, :, pl.ds(0, 2 * MID)], sem.at[1]),
        pltpu.make_async_copy(inv_edge_ref.at[z], kept_ref.at[4, :, pl.ds(2 * MID, 2 * MID)], sem.at[2]),
        pltpu.make_async_copy(x_ref.at[rows - 1], down_ref.at[pl.ds(0, channels)], sem.at[3]),
        pltpu.make_async_copy(x_ref.at[0], up_ref.at[pl.ds(0, channels)], sem.at[4]),
    ]
    for load in loads:
        load.start()
    odd = lax.rem(me, 2).astype(F32)
    near = next_ref[LANES:].astype(F32)
    far = last_ref[LANES:].astype(F32)
    even = 1.0 - odd
    left = (odd * near[rows:] + even * far[rows:]) * jnp.where(me > 0, 1.0, 0.0)
    right = (odd * far[:rows] + even * near[:rows]) * jnp.where(me < COLS - 1, 1.0, 0.0)
    sides = jnp.concatenate([left, right], 0).astype(BF16)
    side_ref[...] = sides
    down_ref[channels:] = sides
    up_ref[channels:] = sides
    mixer = spread(fw_ref[...].T)
    low = jnp.zeros((LANE - CF, 2 * LANE), BF16)
    kept_ref[5] = jnp.concatenate([mixer[:CF], low, mixer[CF:], low], 0)
    for load in loads:
        load.wait()


def width_near_body(me_ref, t_ref, near_ref, next_ref, x_ref, o_ref, copy_ref, sem):
    me = me_ref[0]
    copy = pltpu.make_async_copy(x_ref, copy_ref, sem.at[0])
    copy.start()
    o_ref[...] = dot_nt(t_ref[me], near_ref[...]) + dot_nt(t_ref[lax.bitwise_xor(me, 1)], next_ref[:LANES])
    copy.wait()


def width_far_body(me_ref, t_ref, part_ref, far_ref, last_ref, o_ref, held, sem):
    me = me_ref[0]
    size = o_ref.shape[0] // 4
    copies = []
    for i in range(4):
        span = pl.ds(i * size, size)
        total = part_ref[span] + dot_nt(t_ref[lax.bitwise_xor(me, 2), span], far_ref[...])
        held[span] = (total + dot_nt(t_ref[lax.bitwise_xor(me, 3), span], last_ref[:LANES])).astype(BF16)
        copies.append(pltpu.make_async_copy(held.at[span], o_ref.at[span], sem.at[i]))
        copies[-1].start()
    for copy in copies:
        copy.wait()


def widen(d):
    gap = jnp.zeros((d.shape[0], LANE - CF), d.dtype)
    return jnp.concatenate(sum([[d[:, CF * r : CF * r + CF], gap] for r in range(HS)], []), 1)


def narrow(d):
    return jnp.concatenate([d[:, LANE * r : LANE * r + CF] for r in range(HS)], 1)


def turns(real, imag):
    s02r, d02r, s13r, d13r = real[0] + real[2], real[0] - real[2], real[1] + real[3], real[1] - real[3]
    s02i, d02i, s13i, d13i = imag[0] + imag[2], imag[0] - imag[2], imag[1] + imag[3], imag[1] - imag[3]
    return (
        (s02r + s13r, s02i + s13i),
        (d02r + d13i, d02i - d13r),
        (s02r - s13r, s02i - s13i),
        (d02r - d13i, d02i + d13r),
    )


def spread(t):
    gap = jnp.zeros((t.shape[0], LANE - CF), t.dtype)
    return jnp.concatenate([t[:, :CF], gap, t[:, CF:], gap], 1)


def middle_body(d_ref, x_ref, scale_ref, shift_ref, o_ref, scale_row, shift_row, tw_ref, edge_ref, wide, back_ref, held, sem):
    loads = [
        pltpu.make_async_copy(scale_ref, scale_row, sem.at[0]),
        pltpu.make_async_copy(shift_ref, shift_row, sem.at[1]),
    ]
    for load in loads:
        load.start()
    first = 0
    wide[...] = widen(jnp.swapaxes(d_ref[...], 0, 1).reshape(W, LANES))
    fwd, inv, edges = x_ref.at[first], x_ref.at[first + 1], x_ref.at[first + 4]
    tw = x_ref[first + 2].astype(F32) + x_ref[first + 3].astype(F32)
    for i in range(4):
        half = slice((i % 2) * 2 * LANE, (i % 2 + 1) * 2 * LANE)
        tw_ref[i // 2, :, half] = tw[i * MID : (i + 1) * MID]
    twr, twi = tw_ref[0], tw_ref[1]
    fwd_edge = edges.at[:, : 2 * MID][...]
    edge_ref[:, : 2 * MID] = edges[: 2 * MID, 2 * MID :]
    edge_ref[:, 2 * MID :] = edges[2 * MID :, 2 * MID :]
    inv_edge = edge_ref[...]
    mixer = x_ref[first + 5]
    for load in loads:
        load.wait()
    scale, shift = spread(scale_row[...]), spread(shift_row[...])
    groups = [slice(LANE * r, LANE * r + LANE) for r in range(HS)]
    for own in ((0,), (1, 2), (3, 4), (5, 6), (7,)):
        data = jnp.concatenate(
            [wide[(p * NF + f) * MID : (p * NF + f + 1) * MID] for f in own for p in range(2)], 0
        )
        count = 2 if own == (0,) else len(own)
        half = 2 * MID * len(own)
        ahead = fwd_edge if own == (0,) else fwd[:half, :half]
        u = dot(ahead, data)
        rows = []
        for f in range(count):
            ur = u[2 * f * MID : (2 * f + 1) * MID]
            ui = u[(2 * f + 1) * MID : (2 * f + 2) * MID]
            vr, vi = [ur[:, groups[0]]], [ui[:, groups[0]]]
            for g in groups[1:]:
                vr.append(ur[:, g] * twr[:, g] - ui[:, g] * twi[:, g])
                vi.append(ur[:, g] * twi[:, g] + ui[:, g] * twr[:, g])
            for real, imag in turns(vr, vi):
                rows.append(jnp.concatenate([real, imag], 1).astype(BF16))
        mixed = dot(jnp.concatenate(rows, 0), mixer)
        active = jnp.maximum(scale * mixed + shift, 0.0)
        rows = []
        for f in range(count):
            part = [active[(HS * f + j) * MID : (HS * f + j + 1) * MID] for j in (0, 3, 2, 1)]
            turned = turns([v[:, :LANE] for v in part], [v[:, LANE:] for v in part])
            br, bi = [turned[0][0].astype(BF16)], [turned[0][1].astype(BF16)]
            for g, (real, imag) in zip(groups[1:], turned[1:]):
                br.append((real * twr[:, g] + imag * twi[:, g]).astype(BF16))
                bi.append((imag * twr[:, g] - real * twi[:, g]).astype(BF16))
            rows.append(jnp.concatenate(br, 1))
            rows.append(jnp.concatenate(bi, 1))
        behind = inv_edge if own == (0,) else inv[:half, :half]
        done = narrow(dot(behind, jnp.concatenate(rows, 0)).astype(BF16))
        for i, f in enumerate(own):
            for p in range(2):
                back_ref[p * NF + f] = done[(2 * i + p) * MID : (2 * i + p + 1) * MID]
    stores = []
    size = MID // 4
    for i in range(4):
        span = pl.ds(i * size, size)
        held[span] = jnp.swapaxes(back_ref[:, i * size : (i + 1) * size, :], 0, 1)
        stores.append(pltpu.make_async_copy(held.at[span], o_ref.at[span], sem.at[8 + i]))
        stores[-1].start()
    for store in stores:
        store.wait()


def inverse_body(t_ref, d_ref, *outs):
    data = d_ref[...].T
    for i, o_ref in enumerate(outs):
        o_ref[...] = dot(data, t_ref[i]).astype(BF16)


def conv_setup(fl_ref, fg_ref, wl_ref, wg_ref):
    cl, channels = fl_ref.shape[1], fl_ref.shape[2]
    for dx in range(3):
        wl_ref[dx * channels : (dx + 1) * channels] = jnp.concatenate([fl_ref[3 * dy + dx] for dy in range(3)], 0).T
        wg_ref[dx * cl : (dx + 1) * cl] = jnp.concatenate([fg_ref[3 * dy + dx] for dy in range(3)], 1)


def conv_edges(side_ref, around, wl_ref, wg_ref, cols, edge):
    rows, channels = side_ref.shape[0] // 2, side_ref.shape[1]
    cl, cg = wl_ref.shape[1] // 3, wg_ref.shape[1] // 3
    cols[...] = jnp.zeros_like(cols)
    for side in range(2):
        own = pl.ds(side * rows, rows)
        cols[side, rows : 2 * rows] = side_ref[own]
        for i, other in enumerate(around):
            cols[side, 2 * i * rows : (2 * i + 1) * rows] = other[pl.ds(channels + side * rows, rows)]
        dx = 2 * side
        total = None
        for dy in range(3):
            taps = wl_ref[dx * channels : (dx + 1) * channels, dy * cl : (dy + 1) * cl]
            term = dot_nt(taps, cols[side, :, :cl])
            taps = wg_ref[dx * cl : (dx + 1) * cl, dy * cg : (dy + 1) * cg]
            extra = dot_nt(taps, cols[side, :, cl:])
            term = jnp.concatenate([term[:cl] + extra, term[cl:]], 0)
            term = pltpu.roll(term, LANE - (rows - 1 + dy), 1)
            total = term if total is None else total + term
        edge[side] = total


def edge_lanes(h, edge, before, behind):
    lane = lax.broadcasted_iota(jnp.int32, edge.shape[1:], 1)
    width = before.shape[1]
    first = pltpu.roll(edge[0], lax.rem(LANE - h, LANE), 1)
    final = pltpu.roll(edge[1], LANE - 1 - h, 1)
    before = jnp.concatenate([jnp.where(lane == 0, first, before[:, :LANE]), before[:, LANE:]], 1)
    last = jnp.where(lane == LANE - 1, final, behind[:, width - LANE :])
    return before, jnp.concatenate([behind[:, : width - LANE], last], 1)


def conv_row(h, three, wl_ref, wg_ref, wm_ref, ws_ref, affine_ref, edge, o_ref, out_ref, sem):
    channels, width = three[1].shape
    cl = wl_ref.shape[1] // 3
    local = jnp.concatenate([row[:cl] for row in three], 0)
    other = jnp.concatenate([row[cl:] for row in three], 0)
    yl = dot(wl_ref[...], local)
    yg = dot(wg_ref[...], other)
    parts = []
    for dx in range(3):
        own = yl[dx * channels : (dx + 1) * channels]
        parts.append(jnp.concatenate([own[:cl] + yg[dx * cl : (dx + 1) * cl], own[cl:]], 0))
    before = pltpu.roll(parts[0], 1, 1)
    behind = pltpu.roll(parts[2], width - 1, 1)
    before, behind = edge_lanes(h, edge, before, behind)
    acc = parts[1] + before + behind
    mix = dot(wm_ref[...], section_rows(ws_ref[...], affine_ref[:, 0:1], affine_ref[:, 1:2], three[1][cl:]))
    o_ref[h, :cl] = acc[:cl].astype(BF16)
    o_ref[h, cl:] = (acc[cl:] + mix).astype(BF16)
    pltpu.make_async_copy(o_ref.at[h], out_ref.at[h], sem.at[0]).start()


def conv_body(
    x_ref,
    side_ref,
    fl_ref,
    fg_ref,
    wm_ref,
    ws_ref,
    affine_ref,
    above_ref,
    below_ref,
    table_ref,
    me_ref,
    out_ref,
    kept_ref,
    o_ref,
    cols,
    edge,
    wl_ref,
    wg_ref,
    sem,
):
    rows, channels, width = x_ref.shape
    others = []
    for i, s in enumerate((2, 3, 1)):
        source = table_ref.at[lax.bitwise_xor(me_ref[0], s)]
        others.append(pltpu.make_async_copy(source, kept_ref.at[i], sem.at[2 + i]))
    for other in others:
        other.start()
    conv_setup(fl_ref, fg_ref, wl_ref, wg_ref)
    conv_edges(side_ref, (above_ref, below_ref), wl_ref, wg_ref, cols, edge)
    rest = (wl_ref, wg_ref, wm_ref, ws_ref, affine_ref, edge, o_ref, out_ref, sem)
    conv_row(0, [above_ref[:channels], x_ref[0], x_ref[1]], *rest)

    def step(h, carry):
        conv_row(h, [x_ref[h - 1], x_ref[h], x_ref[h + 1]], *rest)
        return carry

    lax.fori_loop(1, rows - 1, step, 0, unroll=7)
    conv_row(rows - 1, [x_ref[rows - 2], x_ref[rows - 1], below_ref[:channels]], *rest)
    pltpu.make_async_copy(o_ref, out_ref, sem.at[0]).wait()
    for other in others:
        other.wait()


def final_rows(pieces, me_ref, x_ref, pre_ref, w_ref, affine_ref, o_ref, finish=None):
    channels = x_ref.shape[1]
    count = w_ref.shape[0]
    size = channels - count
    mixed = {}
    for s, piece in pieces:
        for r in range(HS):
            mixed[s, r] = dot(w_ref[...], piece[r * CF : (r + 1) * CF])
    for k in range(channels // size):
        span = slice(k * size, (k + 1) * size)
        scale, shift = affine_ref[span, 0:1], affine_ref[span, 1:2]
        for s, _ in pieces:
            first = HS * lax.bitwise_xor(me_ref[0], s)
            for r in range(HS):
                pre = pre_ref[first + r, span].astype(F32)
                if k:
                    pre = pre + mixed[s, r][(k - 1) * size : k * size]
                act = jnp.maximum(scale * pre + shift, 0.0)
                o_ref[first + r, span] = (x_ref[first + r, span].astype(F32) + act).astype(BF16)
        if finish is not None:
            finish(k, span)


def fetch_rows(x_ref, pre_ref, first, count, x, pre, sem):
    span = pl.ds(first, count)
    loads = [
        pltpu.make_async_copy(x_ref.at[span], x.at[span], sem.at[0]),
        pltpu.make_async_copy(pre_ref.at[span], pre.at[span], sem.at[1]),
    ]
    for load in loads:
        load.start()
    return loads


def final_near_body(
    me_ref, x_ref, pre_ref, w_ref, scale_ref, shift_ref, t_ref, d_ref, next_ref, o_ref, affine_ref, x, pre, table, sem
):
    me = me_ref[0]
    load = pltpu.make_async_copy(t_ref.at[me], table, sem.at[2])
    load.start()
    loads = fetch_rows(x_ref, pre_ref, 2 * HS * (me // 2), 2 * HS, x, pre, sem)
    affine_ref[:, 0:1] = column(scale_ref[...])
    affine_ref[:, 1:2] = column(shift_ref[...])
    data = d_ref[...].T
    load.wait()
    near = dot(data, table[...]).astype(BF16)
    for load in loads:
        load.wait()
    final_rows(((0, near), (1, next_ref)), me_ref, x, pre, w_ref, affine_ref, o_ref)


def final_far_body(me_ref, x_ref, pre_ref, w_ref, affine_ref, far_ref, given_ref, o_ref, x, pre, sem):
    loads = fetch_rows(x_ref, pre_ref, HS * lax.bitwise_xor(me_ref[0], 2), HS, x, pre, sem)
    for load in loads:
        load.wait()
    final_rows(((2, far_ref),), me_ref, x, pre, w_ref, affine_ref, o_ref)


def final_last_body(me_ref, x_ref, pre_ref, w_ref, affine_ref, last_ref, given_ref, o_ref, out_ref, held, sem):
    copies = []

    def finish(k, span):
        held[span] = jnp.swapaxes(o_ref[:, span, :], 0, 1)
        copies.append(pltpu.make_async_copy(held.at[span], out_ref.at[span], sem.at[k]))
        copies[-1].start()

    final_rows(((3, last_ref),), me_ref, x_ref, pre_ref, w_ref, affine_ref, o_ref, finish)
    for copy in copies:
        copy.wait()


def shift_along(block, axis, step):
    count = lax.axis_size(axis)
    pairs = [(i, i + step) for i in range(count) if 0 <= i + step < count]
    return lax.ppermute(block, axis, pairs)


def swap(block, s):
    return lax.ppermute(block, "col", [(i, i ^ s) for i in range(COLS)])


def after(value, *others):
    return lax.optimization_barrier((value,) + others)


def per_device(
    image,
    from_local,
    from_global,
    section_weight,
    section_scale,
    section_shift,
    fourier_weight,
    fourier_scale,
    fourier_shift,
    mix_weight,
    out_scale,
    out_shift,
):
    channels, rows, width = image.shape
    cl = from_local.shape[2]
    cg = channels - cl
    me = lax.axis_index("col").astype(jnp.int32).reshape(1)
    z = jnp.logical_and(lax.axis_index("row") == 0, lax.axis_index("col") == 0).astype(jnp.int32).reshape(1)
    shape = jax.ShapeDtypeStruct
    dma = pltpu.SemaphoreType.DMA

    whole = shape((rows, channels, width), BF16)
    block, block_ends = shape((LANES, width), BF16), shape((LANES + 2 * rows, width), BF16)
    x, far, section_affine = call(
        first_body,
        (whole, block, shape((CF, 2), F32)),
        (me, image, section_weight, section_scale[None], section_shift[None]),
        smem=(0,),
        hbm=(1, 2, 3, 4),
        scratch=[
            pltpu.VMEM((channels, rows, width), BF16),
            pltpu.VMEM((CF, cg), BF16),
            pltpu.VMEM((1, CF), F32),
            pltpu.VMEM((1, CF), F32),
            dma((PARTS + 3,)),
        ],
    )
    far = swap(far, 2)
    near, other, last = call(
        rest_body, (block, block_ends, block_ends), (me, x, section_weight, section_affine), smem=(0,)
    )
    last, other = swap(last, 3), swap(other, 1)

    weights = (jnp.transpose(from_local, (0, 2, 1)), from_global, mix_weight, section_weight, section_affine)
    scratch = [
        pltpu.VMEM((rows, channels, width), BF16),
        pltpu.VMEM((2, LANE, channels), BF16),
        pltpu.VMEM((2, channels, LANE), F32),
        pltpu.VMEM((3 * channels, 3 * cl), BF16),
        pltpu.VMEM((3 * cl, 3 * cg), BF16),
        dma((5,)),
    ]
    fwd_w, inv_w = (jnp.asarray(t) for t in width_tables())
    near, far = after(near, far)
    part, x = call(
        width_near_body,
        (shape((W, LANES), F32), whole),
        (me, fwd_w, near, other, x),
        smem=(0,),
        flops=10**9,
        hbm_out=(1,),
        scratch=[dma((1,))],
    )
    spectra = call(
        width_far_body,
        shape((W, LANES), BF16),
        (me, fwd_w, part, far, last),
        smem=(0,),
        hbm_out=(0,),
        scratch=[pltpu.VMEM((W, LANES), BF16), dma((4,))],
    )
    spectra, other, last = after(spectra, other, last)
    spectra = lax.all_to_all(
        spectra.reshape(PEERS, 2 * NF, LANES), ("row", "col"), split_axis=0, concat_axis=0, tiled=True
    )
    ends = shape((channels + 2 * rows, width), BF16)
    pairs, fwd_edge, inv_edge = (jnp.asarray(t) for t in height_tables())
    down, up, sides, kept = call(
        halo_body,
        (ends, ends, shape((2 * rows, channels), BF16), shape((6, channels, width), BF16)),
        (me, z, x, other, last, fourier_weight, pairs, fwd_edge, inv_edge),
        smem=(0, 1),
        hbm=(2, 6, 7, 8),
        stage=(5,),
        scratch=[dma((5,))],
    )
    above, below = shift_along(down, "row", 1), shift_along(up, "row", -1)

    returned = call(
        middle_body,
        shape((PEERS, 2 * NF, LANES), BF16),
        (spectra, kept, fourier_scale[None], fourier_shift[None]),
        hbm=(2, 3),
        hbm_out=(0,),
        limit=24,
        scratch=[
            pltpu.VMEM((1, 2 * CF), F32),
            pltpu.VMEM((1, 2 * CF), F32),
            pltpu.VMEM((2, MID, WIDE), F32),
            pltpu.VMEM((2 * MID, 4 * MID), BF16),
            pltpu.VMEM((W, WIDE), BF16),
            pltpu.VMEM((2 * NF, MID, LANES), BF16),
            pltpu.VMEM((PEERS, 2 * NF, LANES), BF16),
            dma((12,)),
        ],
    )
    returned, above, below = after(returned, above, below)
    returned = lax.all_to_all(returned, ("row", "col"), split_axis=0, concat_axis=0, tiled=True).reshape(W, LANES)
    pre, table = call(
        conv_body,
        (whole, shape((3, W, width), BF16)),
        (x, sides) + weights + (above, below, inv_w, me),
        smem=(10,),
        hbm=(9,),
        hbm_out=(0,),
        stage=tuple(range(7)),
        flops=10**9,
        scratch=scratch,
    )

    piece = shape((LANES, width), BF16)
    far, last, other = call(inverse_body, (piece,) * 3, (table, returned))
    far, last, other = swap(far, 2), swap(last, 3), swap(other, 1)
    rows_held = [pltpu.VMEM(whole.shape, BF16), pltpu.VMEM(whole.shape, BF16)]
    half, affine = call(
        final_near_body,
        (whole, shape((channels, 2), F32)),
        (me, x, pre, mix_weight, out_scale[None], out_shift[None], inv_w, returned, other),
        smem=(0,),
        hbm=(1, 2, 6),
        stage=(3, 4, 5),
        scratch=rows_held + [pltpu.VMEM((W, width), BF16), dma((3,))],
    )
    common = (me, x, pre, mix_weight, affine)
    half = call(
        final_far_body,
        whole,
        common + (far, half),
        smem=(0,),
        hbm=(1, 2),
        input_output_aliases={6: 0},
        scratch=rows_held + [dma((2,))],
    )
    _, result = call(
        final_last_body,
        (whole, shape(image.shape, BF16)),
        common + (last, half),
        smem=(0,),
        hbm_out=(1,),
        input_output_aliases={6: 0},
        scratch=[pltpu.VMEM(image.shape, BF16), dma((8,))],
    )
    return result


def solution(mesh):
    return jax.shard_map(
        per_device,
        mesh=mesh,
        in_specs=(P("img", "row", "col"), P(), P(), P(), P(), P(), P(), P(), P(), P(), P(), P()),
        out_specs=P("img", "row", "col"),
        check_vma=False,
    )
```

```python
import functools
import math

import jax
import jax.numpy as jnp
import numpy as np
from jax import lax
from jax.experimental import pallas as pl
from jax.experimental.pallas import tpu as pltpu
from jax.sharding import PartitionSpec as P

F32 = jnp.float32
BF16 = jnp.bfloat16
MIB = 1024 * 1024

H, W = 256, 1024
ROWS, COLS = 16, 4
PEERS = ROWS * COLS
NF = W // 2 // PEERS
CF = 96
HS = H // PEERS
LANES = HS * CF
LANE = 128
WIDE = HS * LANE
MID = H // HS
PARTS = 8


def bf(table):
    return np.asarray(table, np.float32).astype(jnp.bfloat16)


@functools.lru_cache(None)
def width_tables():
    k = np.arange(W // 2)
    w = np.arange(W)
    angle = 2 * math.pi / W * ((w[:, None] * k[None, :]) % W)
    alternate = np.where(w % 2 == 0, 1.0, -1.0)
    cos, sin = np.cos(angle), np.sin(angle)
    fwd = np.stack([cos, np.where(k[None, :] == 0, alternate[:, None], -sin)], 0)
    inv = np.stack([np.where(k[None, :] == 0, 1.0, 2.0) * cos, np.where(k[None, :] == 0, alternate[:, None], -2.0 * sin)], 0)
    order = lambda t: t.reshape(2, W, PEERS, NF).transpose(2, 0, 3, 1).reshape(W, W)
    norm = 1.0 / math.sqrt(W)
    fwd = (order(fwd) * norm).reshape(W, COLS, W // COLS).transpose(1, 0, 2)
    inv = (order(inv) * norm).reshape(W, COLS, W // COLS).transpose(1, 0, 2)
    return bf(fwd), bf(inv)


@functools.lru_cache(None)
def height_tables():
    m = np.arange(MID)
    angle = 2 * math.pi / MID * ((m[:, None] * m[None, :]) % MID)
    cos, sin, zero = np.cos(angle), np.sin(angle), np.zeros((MID, MID))
    norm = 1.0 / math.sqrt(H)
    fwd = np.block([[cos, sin], [-sin, cos]])
    inv = np.block([[cos, -sin], [sin, cos]])
    none = np.zeros_like(fwd)
    pair = lambda t: np.block([[t, none], [none, t]])
    fwd_edge = np.stack(
        [np.block([[fwd], [none]]), np.block([[cos, zero], [-sin, zero], [zero, cos], [zero, -sin]])], 0
    )
    inv_edge = np.stack(
        [np.block([[inv, none]]), np.block([[cos, -sin, zero, zero], [zero, zero, cos, -sin]])], 0
    )
    inv_edge = inv_edge.reshape(2, 2 * MID, 2, 2 * MID).transpose(0, 2, 1, 3).reshape(2, 4 * MID, 2 * MID)
    tw = twiddles().reshape(2, MID, 2, 2 * LANE).transpose(0, 2, 1, 3).reshape(4 * MID, 2 * LANE)
    high = bf(tw)
    low = bf(tw - high.astype(np.float32))
    pairs = np.stack([bf(pair(fwd) * norm), bf(pair(inv) * norm), high, low], 0)
    return pairs, bf(fwd_edge * norm), bf(inv_edge * norm)


@functools.lru_cache(None)
def twiddles():
    m = np.arange(MID)[:, None]
    r = np.repeat(np.arange(HS), LANE)[None, :]
    angle = 2 * math.pi / H * (m * r)
    return np.stack([np.cos(angle), -np.sin(angle)], 0).astype(np.float32)


def dot(a, b):
    return jnp.dot(a, b, preferred_element_type=F32)


def dot_nt(a, b):
    return lax.dot_general(a, b, (((1,), (1,)), ((), ())), preferred_element_type=F32)


def staged(body, staged_at, total, outs, refs):
    ins, rest = list(refs[:total]), refs[total:]
    count = len(staged_at)
    targets, sem, rest = rest[outs : outs + count], rest[outs + count], rest[:outs] + rest[outs + count + 1 :]
    loads = [pltpu.make_async_copy(ins[i], t, sem.at[n]) for n, (i, t) in enumerate(zip(staged_at, targets))]
    for load in loads:
        load.start()
    for i, t in zip(staged_at, targets):
        ins[i] = t
    for load in loads:
        load.wait()
    body(*ins, *rest)


def call(body, out_shape, operands, smem=(), hbm=(), stage=(), hbm_out=(), limit=16, flops=10**6, scratch=(), **kw):
    place = lambda i: pltpu.SMEM if i in smem else pltpu.HBM if i in hbm or i in stage else pltpu.VMEM
    single = not isinstance(out_shape, tuple)
    outs = [out_shape] if single else list(out_shape)
    spaces = [pltpu.HBM if i in hbm_out else pltpu.VMEM for i in range(len(outs))]
    shapes = [space(s.shape, s.dtype) for space, s in zip(spaces, outs)]
    specs = [pl.BlockSpec(memory_space=space) for space in spaces]
    operands = [v if i in smem else pltpu.with_memory_space_constraint(v, place(i)) for i, v in enumerate(operands)]
    if stage:
        inner, total = body, len(operands)
        body = lambda *refs: staged(inner, stage, total, len(outs), refs)
        held = [pltpu.VMEM(operands[i].shape, operands[i].dtype) for i in stage]
        scratch = held + [pltpu.SemaphoreType.DMA((len(stage),))] + list(scratch)
    return pl.pallas_call(
        body,
        out_shape=shapes[0] if single else tuple(shapes),
        in_specs=[pl.BlockSpec(memory_space=place(i)) for i in range(len(operands))],
        out_specs=specs[0] if single else tuple(specs),
        scratch_shapes=scratch,
        compiler_params=pltpu.CompilerParams(vmem_limit_bytes=limit * MIB),
        cost_estimate=pl.CostEstimate(flops=flops, bytes_accessed=flops // 1000, transcendentals=0),
        **kw,
    )(*operands)


def column(row):
    count = row.shape[1]
    diagonal = lax.broadcasted_iota(jnp.int32, (count, count), 0) == lax.broadcasted_iota(jnp.int32, (count, count), 1)
    return jnp.sum(jnp.where(diagonal, jnp.broadcast_to(row, (count, count)), 0.0), 1, keepdims=True)


def section_rows(weight, scale, shift, x):
    return jnp.maximum(scale * dot(weight, x) + shift, 0.0).astype(BF16)


def first_body(
    me_ref, image_ref, w_ref, scale_ref, shift_ref, x_ref, far_ref, affine_ref, held, weight, scale_row, shift_row, sem
):
    channels = image_ref.shape[0]
    size = channels // PARTS
    small = [(w_ref, weight), (scale_ref, scale_row), (shift_ref, shift_row)]
    others = [pltpu.make_async_copy(a, b, sem.at[PARTS + i]) for i, (a, b) in enumerate(small)]
    loads = []
    for i in range(PARTS):
        span = pl.ds(i * size, size)
        loads.append(pltpu.make_async_copy(image_ref.at[span], held.at[span], sem.at[i]))
    for load in others + loads[::-1]:
        load.start()
    for load in others:
        load.wait()
    scale, shift = column(scale_row[...]), column(shift_row[...])
    affine_ref[:, 0:1] = scale
    affine_ref[:, 1:2] = shift
    for i in range(PARTS - 1, -1, -1):
        span = slice(i * size, (i + 1) * size)
        loads[i].wait()
        x_ref[:, span, :] = jnp.swapaxes(held[span], 0, 1)
    first = HS * lax.bitwise_xor(me_ref[0], 2)
    skip = channels - w_ref.shape[1]
    for r in range(HS):
        far_ref[r * CF : (r + 1) * CF] = section_rows(weight[...], scale, shift, x_ref[first + r, skip:, :])


def rest_body(me_ref, x_ref, w_ref, affine_ref, near_ref, next_ref, last_ref):
    rows, channels, width = x_ref.shape
    skip = channels - w_ref.shape[1]
    scale, shift = affine_ref[:, 0:1], affine_ref[:, 1:2]
    for s, o_ref in ((3, last_ref), (1, next_ref), (0, near_ref)):
        first = HS * lax.bitwise_xor(me_ref[0], s)
        for r in range(HS):
            o_ref[r * CF : (r + 1) * CF] = section_rows(w_ref[...], scale, shift, x_ref[first + r, skip:, :])
    place = lax.broadcasted_iota(jnp.int32, (2 * rows, width), 0)
    lane = lax.broadcasted_iota(jnp.int32, (2 * rows, width), 1)
    ends = jnp.zeros((2 * rows, channels), F32)
    for h in range(rows):
        pick = ((place == h) & (lane == 0)) | ((place == rows + h) & (lane == width - 1))
        ends = ends + dot_nt(pick.astype(F32).astype(BF16), x_ref[h])
    ends = ends.astype(BF16)
    last_ref[LANES:] = ends
    next_ref[LANES:] = ends


def halo_body(
    me_ref,
    z_ref,
    x_ref,
    next_ref,
    last_ref,
    fw_ref,
    pair_ref,
    fwd_edge_ref,
    inv_edge_ref,
    down_ref,
    up_ref,
    side_ref,
    kept_ref,
    sem,
):
    rows, channels = side_ref.shape[0] // 2, side_ref.shape[1]
    me, z = me_ref[0], z_ref[0]
    loads = [
        pltpu.make_async_copy(pair_ref, kept_ref.at[pl.ds(0, 4)], sem.at[0]),
        pltpu.make_async_copy(fwd_edge_ref.at[z], kept_ref.at[4, :, pl.ds(0, 2 * MID)], sem.at[1]),
        pltpu.make_async_copy(inv_edge_ref.at[z], kept_ref.at[4, :, pl.ds(2 * MID, 2 * MID)], sem.at[2]),
        pltpu.make_async_copy(x_ref.at[rows - 1], down_ref.at[pl.ds(0, channels)], sem.at[3]),
        pltpu.make_async_copy(x_ref.at[0], up_ref.at[pl.ds(0, channels)], sem.at[4]),
    ]
    for load in loads:
        load.start()
    odd = lax.rem(me, 2).astype(F32)
    near = next_ref[LANES:].astype(F32)
    far = last_ref[LANES:].astype(F32)
    even = 1.0 - odd
    left = (odd * near[rows:] + even * far[rows:]) * jnp.where(me > 0, 1.0, 0.0)
    right = (odd * far[:rows] + even * near[:rows]) * jnp.where(me < COLS - 1, 1.0, 0.0)
    sides = jnp.concatenate([left, right], 0).astype(BF16)
    side_ref[...] = sides
    down_ref[channels:] = sides
    up_ref[channels:] = sides
    mixer = spread(fw_ref[...].T)
    low = jnp.zeros((LANE - CF, 2 * LANE), BF16)
    kept_ref[5] = jnp.concatenate([mixer[:CF], low, mixer[CF:], low], 0)
    for load in loads:
        load.wait()


def width_near_body(me_ref, t_ref, near_ref, far_ref, x_ref, o_ref, copy_ref, sem):
    me = me_ref[0]
    copy = pltpu.make_async_copy(x_ref, copy_ref, sem.at[0])
    copy.start()
    o_ref[...] = dot_nt(t_ref[me], near_ref[...]) + dot_nt(t_ref[lax.bitwise_xor(me, 2)], far_ref[...])
    copy.wait()


def width_last_body(me_ref, t_ref, part_ref, next_ref, last_ref, o_ref, held, sem):
    me = me_ref[0]
    size = o_ref.shape[0] // 4
    copies = []
    for i in range(4):
        span = pl.ds(i * size, size)
        total = part_ref[span] + dot_nt(t_ref[lax.bitwise_xor(me, 1), span], next_ref[:LANES])
        held[span] = (total + dot_nt(t_ref[lax.bitwise_xor(me, 3), span], last_ref[:LANES])).astype(BF16)
        copies.append(pltpu.make_async_copy(held.at[span], o_ref.at[span], sem.at[i]))
        copies[-1].start()
    for copy in copies:
        copy.wait()


def widen(d):
    gap = jnp.zeros((d.shape[0], LANE - CF), d.dtype)
    return jnp.concatenate(sum([[d[:, CF * r : CF * r + CF], gap] for r in range(HS)], []), 1)


def narrow(d):
    return jnp.concatenate([d[:, LANE * r : LANE * r + CF] for r in range(HS)], 1)


def turns(real, imag):
    s02r, d02r, s13r, d13r = real[0] + real[2], real[0] - real[2], real[1] + real[3], real[1] - real[3]
    s02i, d02i, s13i, d13i = imag[0] + imag[2], imag[0] - imag[2], imag[1] + imag[3], imag[1] - imag[3]
    return (
        (s02r + s13r, s02i + s13i),
        (d02r + d13i, d02i - d13r),
        (s02r - s13r, s02i - s13i),
        (d02r - d13i, d02i + d13r),
    )


def spread(t):
    gap = jnp.zeros((t.shape[0], LANE - CF), t.dtype)
    return jnp.concatenate([t[:, :CF], gap, t[:, CF:], gap], 1)


def middle_body(d_ref, x_ref, scale_ref, shift_ref, o_ref, scale_row, shift_row, tw_ref, edge_ref, wide, back_ref, held, sem):
    loads = [
        pltpu.make_async_copy(scale_ref, scale_row, sem.at[0]),
        pltpu.make_async_copy(shift_ref, shift_row, sem.at[1]),
    ]
    for load in loads:
        load.start()
    first = 0
    wide[...] = widen(jnp.swapaxes(d_ref[...], 0, 1).reshape(W, LANES))
    fwd, inv, edges = x_ref.at[first], x_ref.at[first + 1], x_ref.at[first + 4]
    tw = x_ref[first + 2].astype(F32) + x_ref[first + 3].astype(F32)
    for i in range(4):
        half = slice((i % 2) * 2 * LANE, (i % 2 + 1) * 2 * LANE)
        tw_ref[i // 2, :, half] = tw[i * MID : (i + 1) * MID]
    twr, twi = tw_ref[0], tw_ref[1]
    fwd_edge = edges.at[:, : 2 * MID][...]
    edge_ref[:, : 2 * MID] = edges[: 2 * MID, 2 * MID :]
    edge_ref[:, 2 * MID :] = edges[2 * MID :, 2 * MID :]
    inv_edge = edge_ref[...]
    mixer = x_ref[first + 5]
    for load in loads:
        load.wait()
    scale, shift = spread(scale_row[...]), spread(shift_row[...])
    groups = [slice(LANE * r, LANE * r + LANE) for r in range(HS)]
    for own in ((0,), (1, 2), (3, 4), (5, 6), (7,)):
        data = jnp.concatenate(
            [wide[(p * NF + f) * MID : (p * NF + f + 1) * MID] for f in own for p in range(2)], 0
        )
        count = 2 if own == (0,) else len(own)
        half = 2 * MID * len(own)
        ahead = fwd_edge if own == (0,) else fwd[:half, :half]
        u = dot(ahead, data)
        rows = []
        for f in range(count):
            ur = u[2 * f * MID : (2 * f + 1) * MID]
            ui = u[(2 * f + 1) * MID : (2 * f + 2) * MID]
            vr, vi = [ur[:, groups[0]]], [ui[:, groups[0]]]
            for g in groups[1:]:
                vr.append(ur[:, g] * twr[:, g] - ui[:, g] * twi[:, g])
                vi.append(ur[:, g] * twi[:, g] + ui[:, g] * twr[:, g])
            for real, imag in turns(vr, vi):
                rows.append(jnp.concatenate([real, imag], 1).astype(BF16))
        mixed = dot(jnp.concatenate(rows, 0), mixer)
        active = jnp.maximum(scale * mixed + shift, 0.0)
        rows = []
        for f in range(count):
            part = [active[(HS * f + j) * MID : (HS * f + j + 1) * MID] for j in (0, 3, 2, 1)]
            turned = turns([v[:, :LANE] for v in part], [v[:, LANE:] for v in part])
            br, bi = [turned[0][0].astype(BF16)], [turned[0][1].astype(BF16)]
            for g, (real, imag) in zip(groups[1:], turned[1:]):
                br.append((real * twr[:, g] + imag * twi[:, g]).astype(BF16))
                bi.append((imag * twr[:, g] - real * twi[:, g]).astype(BF16))
            rows.append(jnp.concatenate(br, 1))
            rows.append(jnp.concatenate(bi, 1))
        behind = inv_edge if own == (0,) else inv[:half, :half]
        done = narrow(dot(behind, jnp.concatenate(rows, 0)).astype(BF16))
        for i, f in enumerate(own):
            for p in range(2):
                back_ref[p * NF + f] = done[(2 * i + p) * MID : (2 * i + p + 1) * MID]
    stores = []
    size = MID // 4
    for i in range(4):
        span = pl.ds(i * size, size)
        held[span] = jnp.swapaxes(back_ref[:, i * size : (i + 1) * size, :], 0, 1)
        stores.append(pltpu.make_async_copy(held.at[span], o_ref.at[span], sem.at[8 + i]))
        stores[-1].start()
    for store in stores:
        store.wait()


def inverse_body(t_ref, d_ref, *outs):
    data = d_ref[...].T
    for i, o_ref in enumerate(outs):
        o_ref[...] = dot(data, t_ref[i]).astype(BF16)


def conv_setup(fl_ref, fg_ref, wl_ref, wg_ref):
    cl, channels = fl_ref.shape[1], fl_ref.shape[2]
    for dx in range(3):
        wl_ref[dx * channels : (dx + 1) * channels] = jnp.concatenate([fl_ref[3 * dy + dx] for dy in range(3)], 0).T
        wg_ref[dx * cl : (dx + 1) * cl] = jnp.concatenate([fg_ref[3 * dy + dx] for dy in range(3)], 1)


def conv_edges(side_ref, around, wl_ref, wg_ref, cols, edge):
    rows, channels = side_ref.shape[0] // 2, side_ref.shape[1]
    cl, cg = wl_ref.shape[1] // 3, wg_ref.shape[1] // 3
    cols[...] = jnp.zeros_like(cols)
    for side in range(2):
        own = pl.ds(side * rows, rows)
        cols[side, rows : 2 * rows] = side_ref[own]
        for i, other in enumerate(around):
            cols[side, 2 * i * rows : (2 * i + 1) * rows] = other[pl.ds(channels + side * rows, rows)]
        dx = 2 * side
        total = None
        for dy in range(3):
            taps = wl_ref[dx * channels : (dx + 1) * channels, dy * cl : (dy + 1) * cl]
            term = dot_nt(taps, cols[side, :, :cl])
            taps = wg_ref[dx * cl : (dx + 1) * cl, dy * cg : (dy + 1) * cg]
            extra = dot_nt(taps, cols[side, :, cl:])
            term = jnp.concatenate([term[:cl] + extra, term[cl:]], 0)
            term = pltpu.roll(term, LANE - (rows - 1 + dy), 1)
            total = term if total is None else total + term
        edge[side] = total


def edge_lanes(h, edge, before, behind):
    lane = lax.broadcasted_iota(jnp.int32, edge.shape[1:], 1)
    width = before.shape[1]
    first = pltpu.roll(edge[0], lax.rem(LANE - h, LANE), 1)
    final = pltpu.roll(edge[1], LANE - 1 - h, 1)
    before = jnp.concatenate([jnp.where(lane == 0, first, before[:, :LANE]), before[:, LANE:]], 1)
    last = jnp.where(lane == LANE - 1, final, behind[:, width - LANE :])
    return before, jnp.concatenate([behind[:, : width - LANE], last], 1)


def conv_row(h, three, wl_ref, wg_ref, wm_ref, ws_ref, affine_ref, edge, o_ref, out_ref, sem):
    channels, width = three[1].shape
    cl = wl_ref.shape[1] // 3
    local = jnp.concatenate([row[:cl] for row in three], 0)
    other = jnp.concatenate([row[cl:] for row in three], 0)
    yl = dot(wl_ref[...], local)
    yg = dot(wg_ref[...], other)
    parts = []
    for dx in range(3):
        own = yl[dx * channels : (dx + 1) * channels]
        parts.append(jnp.concatenate([own[:cl] + yg[dx * cl : (dx + 1) * cl], own[cl:]], 0))
    before = pltpu.roll(parts[0], 1, 1)
    behind = pltpu.roll(parts[2], width - 1, 1)
    before, behind = edge_lanes(h, edge, before, behind)
    acc = parts[1] + before + behind
    mix = dot(wm_ref[...], section_rows(ws_ref[...], affine_ref[:, 0:1], affine_ref[:, 1:2], three[1][cl:]))
    o_ref[h, :cl] = acc[:cl].astype(BF16)
    o_ref[h, cl:] = (acc[cl:] + mix).astype(BF16)
    pltpu.make_async_copy(o_ref.at[h], out_ref.at[h], sem.at[0]).start()


def conv_body(
    x_ref,
    side_ref,
    fl_ref,
    fg_ref,
    wm_ref,
    ws_ref,
    affine_ref,
    above_ref,
    below_ref,
    table_ref,
    me_ref,
    out_ref,
    kept_ref,
    o_ref,
    cols,
    edge,
    wl_ref,
    wg_ref,
    sem,
):
    rows, channels, width = x_ref.shape
    others = []
    for i, s in enumerate((2, 3, 1)):
        source = table_ref.at[lax.bitwise_xor(me_ref[0], s)]
        others.append(pltpu.make_async_copy(source, kept_ref.at[i], sem.at[2 + i]))
    for other in others:
        other.start()
    conv_setup(fl_ref, fg_ref, wl_ref, wg_ref)
    conv_edges(side_ref, (above_ref, below_ref), wl_ref, wg_ref, cols, edge)
    rest = (wl_ref, wg_ref, wm_ref, ws_ref, affine_ref, edge, o_ref, out_ref, sem)
    conv_row(0, [above_ref[:channels], x_ref[0], x_ref[1]], *rest)

    def step(h, carry):
        conv_row(h, [x_ref[h - 1], x_ref[h], x_ref[h + 1]], *rest)
        return carry

    lax.fori_loop(1, rows - 1, step, 0, unroll=7)
    conv_row(rows - 1, [x_ref[rows - 2], x_ref[rows - 1], below_ref[:channels]], *rest)
    pltpu.make_async_copy(o_ref, out_ref, sem.at[0]).wait()
    for other in others:
        other.wait()


def final_rows(pieces, me_ref, x_ref, pre_ref, w_ref, affine_ref, o_ref, finish=None):
    channels = x_ref.shape[1]
    count = w_ref.shape[0]
    size = channels - count
    mixed = {}
    for s, piece in pieces:
        for r in range(HS):
            mixed[s, r] = dot(w_ref[...], piece[r * CF : (r + 1) * CF])
    for k in range(channels // size):
        span = slice(k * size, (k + 1) * size)
        scale, shift = affine_ref[span, 0:1], affine_ref[span, 1:2]
        for s, _ in pieces:
            first = HS * lax.bitwise_xor(me_ref[0], s)
            for r in range(HS):
                pre = pre_ref[first + r, span].astype(F32)
                if k:
                    pre = pre + mixed[s, r][(k - 1) * size : k * size]
                act = jnp.maximum(scale * pre + shift, 0.0)
                o_ref[first + r, span] = (x_ref[first + r, span].astype(F32) + act).astype(BF16)
        if finish is not None:
            finish(k, span)


def fetch_rows(x_ref, pre_ref, first, count, x, pre, sem):
    span = pl.ds(first, count)
    loads = [
        pltpu.make_async_copy(x_ref.at[span], x.at[span], sem.at[0]),
        pltpu.make_async_copy(pre_ref.at[span], pre.at[span], sem.at[1]),
    ]
    for load in loads:
        load.start()
    return loads


def final_near_body(
    me_ref, x_ref, pre_ref, w_ref, scale_ref, shift_ref, t_ref, d_ref, next_ref, o_ref, affine_ref, x, pre, table, sem
):
    me = me_ref[0]
    load = pltpu.make_async_copy(t_ref.at[me], table, sem.at[2])
    load.start()
    loads = fetch_rows(x_ref, pre_ref, 2 * HS * (me // 2), 2 * HS, x, pre, sem)
    affine_ref[:, 0:1] = column(scale_ref[...])
    affine_ref[:, 1:2] = column(shift_ref[...])
    data = d_ref[...].T
    load.wait()
    near = dot(data, table[...]).astype(BF16)
    for load in loads:
        load.wait()
    final_rows(((0, near), (1, next_ref)), me_ref, x, pre, w_ref, affine_ref, o_ref)


def final_far_body(me_ref, x_ref, pre_ref, w_ref, affine_ref, far_ref, given_ref, o_ref, x, pre, sem):
    loads = fetch_rows(x_ref, pre_ref, HS * lax.bitwise_xor(me_ref[0], 2), HS, x, pre, sem)
    for load in loads:
        load.wait()
    final_rows(((2, far_ref),), me_ref, x, pre, w_ref, affine_ref, o_ref)


def final_last_body(me_ref, x_ref, pre_ref, w_ref, affine_ref, last_ref, given_ref, o_ref, out_ref, held, sem):
    copies = []

    def finish(k, span):
        held[span] = jnp.swapaxes(o_ref[:, span, :], 0, 1)
        copies.append(pltpu.make_async_copy(held.at[span], out_ref.at[span], sem.at[k]))
        copies[-1].start()

    final_rows(((3, last_ref),), me_ref, x_ref, pre_ref, w_ref, affine_ref, o_ref, finish)
    for copy in copies:
        copy.wait()


def shift_along(block, axis, step):
    count = lax.axis_size(axis)
    pairs = [(i, i + step) for i in range(count) if 0 <= i + step < count]
    return lax.ppermute(block, axis, pairs)


def swap(block, s):
    return lax.ppermute(block, "col", [(i, i ^ s) for i in range(COLS)])


def after(value, *others):
    return lax.optimization_barrier((value,) + others)


def per_device(
    image,
    from_local,
    from_global,
    section_weight,
    section_scale,
    section_shift,
    fourier_weight,
    fourier_scale,
    fourier_shift,
    mix_weight,
    out_scale,
    out_shift,
):
    channels, rows, width = image.shape
    cl = from_local.shape[2]
    cg = channels - cl
    me = lax.axis_index("col").astype(jnp.int32).reshape(1)
    z = jnp.logical_and(lax.axis_index("row") == 0, lax.axis_index("col") == 0).astype(jnp.int32).reshape(1)
    shape = jax.ShapeDtypeStruct
    dma = pltpu.SemaphoreType.DMA

    whole = shape((rows, channels, width), BF16)
    block, block_ends = shape((LANES, width), BF16), shape((LANES + 2 * rows, width), BF16)
    x, far, section_affine = call(
        first_body,
        (whole, block, shape((CF, 2), F32)),
        (me, image, section_weight, section_scale[None], section_shift[None]),
        smem=(0,),
        hbm=(1, 2, 3, 4),
        scratch=[
            pltpu.VMEM((channels, rows, width), BF16),
            pltpu.VMEM((CF, cg), BF16),
            pltpu.VMEM((1, CF), F32),
            pltpu.VMEM((1, CF), F32),
            dma((PARTS + 3,)),
        ],
    )
    far = swap(far, 2)
    near, other, last = call(
        rest_body, (block, block_ends, block_ends), (me, x, section_weight, section_affine), smem=(0,)
    )
    last, other = swap(last, 3), swap(other, 1)

    weights = (jnp.transpose(from_local, (0, 2, 1)), from_global, mix_weight, section_weight, section_affine)
    scratch = [
        pltpu.VMEM((rows, channels, width), BF16),
        pltpu.VMEM((2, LANE, channels), BF16),
        pltpu.VMEM((2, channels, LANE), F32),
        pltpu.VMEM((3 * channels, 3 * cl), BF16),
        pltpu.VMEM((3 * cl, 3 * cg), BF16),
        dma((5,)),
    ]
    fwd_w, inv_w = (jnp.asarray(t) for t in width_tables())
    part, x = call(
        width_near_body,
        (shape((W, LANES), F32), whole),
        (me, fwd_w, near, far, x),
        smem=(0,),
        flops=10**9,
        hbm_out=(1,),
        scratch=[dma((1,))],
    )
    spectra = call(
        width_last_body,
        shape((W, LANES), BF16),
        (me, fwd_w, part, other, last),
        smem=(0,),
        hbm_out=(0,),
        scratch=[pltpu.VMEM((W, LANES), BF16), dma((4,))],
    )
    spectra, other, last = after(spectra, other, last)
    spectra = lax.all_to_all(
        spectra.reshape(PEERS, 2 * NF, LANES), ("row", "col"), split_axis=0, concat_axis=0, tiled=True
    )
    ends = shape((channels + 2 * rows, width), BF16)
    pairs, fwd_edge, inv_edge = (jnp.asarray(t) for t in height_tables())
    down, up, sides, kept = call(
        halo_body,
        (ends, ends, shape((2 * rows, channels), BF16), shape((6, channels, width), BF16)),
        (me, z, x, other, last, fourier_weight, pairs, fwd_edge, inv_edge),
        smem=(0, 1),
        hbm=(2, 6, 7, 8),
        stage=(5,),
        scratch=[dma((5,))],
    )
    above, below = shift_along(down, "row", 1), shift_along(up, "row", -1)

    returned = call(
        middle_body,
        shape((PEERS, 2 * NF, LANES), BF16),
        (spectra, kept, fourier_scale[None], fourier_shift[None]),
        hbm=(2, 3),
        hbm_out=(0,),
        limit=24,
        scratch=[
            pltpu.VMEM((1, 2 * CF), F32),
            pltpu.VMEM((1, 2 * CF), F32),
            pltpu.VMEM((2, MID, WIDE), F32),
            pltpu.VMEM((2 * MID, 4 * MID), BF16),
            pltpu.VMEM((W, WIDE), BF16),
            pltpu.VMEM((2 * NF, MID, LANES), BF16),
            pltpu.VMEM((PEERS, 2 * NF, LANES), BF16),
            dma((12,)),
        ],
    )
    returned, above, below = after(returned, above, below)
    returned = lax.all_to_all(returned, ("row", "col"), split_axis=0, concat_axis=0, tiled=True).reshape(W, LANES)
    pre, table = call(
        conv_body,
        (whole, shape((3, W, width), BF16)),
        (x, sides) + weights + (above, below, inv_w, me),
        smem=(10,),
        hbm=(9,),
        hbm_out=(0,),
        stage=tuple(range(7)),
        flops=10**9,
        scratch=scratch,
    )

    piece = shape((LANES, width), BF16)
    far, last, other = call(inverse_body, (piece,) * 3, (table, returned))
    far, last, other = swap(far, 2), swap(last, 3), swap(other, 1)
    rows_held = [pltpu.VMEM(whole.shape, BF16), pltpu.VMEM(whole.shape, BF16)]
    half, affine = call(
        final_near_body,
        (whole, shape((channels, 2), F32)),
        (me, x, pre, mix_weight, out_scale[None], out_shift[None], inv_w, returned, other),
        smem=(0,),
        hbm=(1, 2, 6),
        stage=(3, 4, 5),
        scratch=rows_held + [pltpu.VMEM((W, width), BF16), dma((3,))],
    )
    common = (me, x, pre, mix_weight, affine)
    half = call(
        final_far_body,
        whole,
        common + (far, half),
        smem=(0,),
        hbm=(1, 2),
        input_output_aliases={6: 0},
        scratch=rows_held + [dma((2,))],
    )
    _, result = call(
        final_last_body,
        (whole, shape(image.shape, BF16)),
        common + (last, half),
        smem=(0,),
        hbm_out=(1,),
        input_output_aliases={6: 0},
        scratch=[pltpu.VMEM(image.shape, BF16), dma((8,))],
    )
    return result


def solution(mesh):
    return jax.shard_map(
        per_device,
        mesh=mesh,
        in_specs=(P("img", "row", "col"), P(), P(), P(), P(), P(), P(), P(), P(), P(), P(), P()),
        out_specs=P("img", "row", "col"),
        check_vma=False,
    )
```

```python
import functools
import math

import jax
import jax.numpy as jnp
import numpy as np
from jax import lax
from jax.experimental import pallas as pl
from jax.experimental.pallas import tpu as pltpu
from jax.sharding import PartitionSpec as P

F32 = jnp.float32
BF16 = jnp.bfloat16
MIB = 1024 * 1024

H, W = 256, 1024
ROWS, COLS = 16, 4
PEERS = ROWS * COLS
NF = W // 2 // PEERS
CF = 96
HS = H // PEERS
LANES = HS * CF
LANE = 128
WIDE = HS * LANE
MID = H // HS
PARTS = 4


def bf(table):
    return np.asarray(table, np.float32).astype(jnp.bfloat16)


@functools.lru_cache(None)
def width_tables():
    k = np.arange(W // 2)
    w = np.arange(W)
    angle = 2 * math.pi / W * ((w[:, None] * k[None, :]) % W)
    alternate = np.where(w % 2 == 0, 1.0, -1.0)
    cos, sin = np.cos(angle), np.sin(angle)
    fwd = np.stack([cos, np.where(k[None, :] == 0, alternate[:, None], -sin)], 0)
    inv = np.stack([np.where(k[None, :] == 0, 1.0, 2.0) * cos, np.where(k[None, :] == 0, alternate[:, None], -2.0 * sin)], 0)
    order = lambda t: t.reshape(2, W, PEERS, NF).transpose(2, 0, 3, 1).reshape(W, W)
    norm = 1.0 / math.sqrt(W)
    fwd = (order(fwd) * norm).reshape(W, COLS, W // COLS).transpose(1, 0, 2)
    inv = (order(inv) * norm).reshape(W, COLS, W // COLS).transpose(1, 0, 2)
    return bf(fwd), bf(inv)


@functools.lru_cache(None)
def height_tables():
    m = np.arange(MID)
    angle = 2 * math.pi / MID * ((m[:, None] * m[None, :]) % MID)
    cos, sin, zero = np.cos(angle), np.sin(angle), np.zeros((MID, MID))
    norm = 1.0 / math.sqrt(H)
    fwd = np.block([[cos, sin], [-sin, cos]])
    inv = np.block([[cos, -sin], [sin, cos]])
    none = np.zeros_like(fwd)
    pair = lambda t: np.block([[t, none], [none, t]])
    fwd_edge = np.stack(
        [np.block([[fwd], [none]]), np.block([[cos, zero], [-sin, zero], [zero, cos], [zero, -sin]])], 0
    )
    inv_edge = np.stack(
        [np.block([[inv, none]]), np.block([[cos, -sin, zero, zero], [zero, zero, cos, -sin]])], 0
    )
    inv_edge = inv_edge.reshape(2, 2 * MID, 2, 2 * MID).transpose(0, 2, 1, 3).reshape(2, 4 * MID, 2 * MID)
    tw = twiddles().reshape(2, MID, 2, 2 * LANE).transpose(0, 2, 1, 3).reshape(4 * MID, 2 * LANE)
    high = bf(tw)
    low = bf(tw - high.astype(np.float32))
    pairs = np.stack([bf(pair(fwd) * norm), bf(pair(inv) * norm), high, low], 0)
    return pairs, bf(fwd_edge * norm), bf(inv_edge * norm)


@functools.lru_cache(None)
def twiddles():
    m = np.arange(MID)[:, None]
    r = np.repeat(np.arange(HS), LANE)[None, :]
    angle = 2 * math.pi / H * (m * r)
    return np.stack([np.cos(angle), -np.sin(angle)], 0).astype(np.float32)


def dot(a, b):
    return jnp.dot(a, b, preferred_element_type=F32)


def dot_nt(a, b):
    return lax.dot_general(a, b, (((1,), (1,)), ((), ())), preferred_element_type=F32)


def staged(body, staged_at, total, outs, refs):
    ins, rest = list(refs[:total]), refs[total:]
    count = len(staged_at)
    targets, sem, rest = rest[outs : outs + count], rest[outs + count], rest[:outs] + rest[outs + count + 1 :]
    loads = [pltpu.make_async_copy(ins[i], t, sem.at[n]) for n, (i, t) in enumerate(zip(staged_at, targets))]
    for load in loads:
        load.start()
    for i, t in zip(staged_at, targets):
        ins[i] = t
    for load in loads:
        load.wait()
    body(*ins, *rest)


def call(body, out_shape, operands, smem=(), hbm=(), stage=(), hbm_out=(), limit=16, flops=10**6, scratch=(), **kw):
    place = lambda i: pltpu.SMEM if i in smem else pltpu.HBM if i in hbm or i in stage else pltpu.VMEM
    single = not isinstance(out_shape, tuple)
    outs = [out_shape] if single else list(out_shape)
    spaces = [pltpu.HBM if i in hbm_out else pltpu.VMEM for i in range(len(outs))]
    shapes = [space(s.shape, s.dtype) for space, s in zip(spaces, outs)]
    specs = [pl.BlockSpec(memory_space=space) for space in spaces]
    operands = [v if i in smem else pltpu.with_memory_space_constraint(v, place(i)) for i, v in enumerate(operands)]
    if stage:
        inner, total = body, len(operands)
        body = lambda *refs: staged(inner, stage, total, len(outs), refs)
        held = [pltpu.VMEM(operands[i].shape, operands[i].dtype) for i in stage]
        scratch = held + [pltpu.SemaphoreType.DMA((len(stage),))] + list(scratch)
    return pl.pallas_call(
        body,
        out_shape=shapes[0] if single else tuple(shapes),
        in_specs=[pl.BlockSpec(memory_space=place(i)) for i in range(len(operands))],
        out_specs=specs[0] if single else tuple(specs),
        scratch_shapes=scratch,
        compiler_params=pltpu.CompilerParams(vmem_limit_bytes=limit * MIB),
        cost_estimate=pl.CostEstimate(flops=flops, bytes_accessed=flops // 1000, transcendentals=0),
        **kw,
    )(*operands)


def column(row):
    count = row.shape[1]
    diagonal = lax.broadcasted_iota(jnp.int32, (count, count), 0) == lax.broadcasted_iota(jnp.int32, (count, count), 1)
    return jnp.sum(jnp.where(diagonal, jnp.broadcast_to(row, (count, count)), 0.0), 1, keepdims=True)


def section_rows(weight, scale, shift, x):
    return jnp.maximum(scale * dot(weight, x) + shift, 0.0).astype(BF16)


def first_body(
    me_ref, image_ref, w_ref, scale_ref, shift_ref, x_ref, far_ref, affine_ref, held, weight, scale_row, shift_row, sem
):
    channels = image_ref.shape[0]
    size = channels // PARTS
    small = [(w_ref, weight), (scale_ref, scale_row), (shift_ref, shift_row)]
    others = [pltpu.make_async_copy(a, b, sem.at[PARTS + i]) for i, (a, b) in enumerate(small)]
    loads = []
    for i in range(PARTS):
        span = pl.ds(i * size, size)
        loads.append(pltpu.make_async_copy(image_ref.at[span], held.at[span], sem.at[i]))
    for load in others + loads[::-1]:
        load.start()
    for load in others:
        load.wait()
    scale, shift = column(scale_row[...]), column(shift_row[...])
    affine_ref[:, 0:1] = scale
    affine_ref[:, 1:2] = shift
    for i in range(PARTS - 1, -1, -1):
        span = slice(i * size, (i + 1) * size)
        loads[i].wait()
        x_ref[:, span, :] = jnp.swapaxes(held[span], 0, 1)
    first = HS * lax.bitwise_xor(me_ref[0], 2)
    skip = channels - w_ref.shape[1]
    for r in range(HS):
        far_ref[r * CF : (r + 1) * CF] = section_rows(weight[...], scale, shift, x_ref[first + r, skip:, :])


def rest_body(me_ref, x_ref, w_ref, affine_ref, near_ref, next_ref, last_ref):
    rows, channels, width = x_ref.shape
    skip = channels - w_ref.shape[1]
    scale, shift = affine_ref[:, 0:1], affine_ref[:, 1:2]
    for s, o_ref in ((3, last_ref), (1, next_ref), (0, near_ref)):
        first = HS * lax.bitwise_xor(me_ref[0], s)
        for r in range(HS):
            o_ref[r * CF : (r + 1) * CF] = section_rows(w_ref[...], scale, shift, x_ref[first + r, skip:, :])
    place = lax.broadcasted_iota(jnp.int32, (2 * rows, width), 0)
    lane = lax.broadcasted_iota(jnp.int32, (2 * rows, width), 1)
    ends = jnp.zeros((2 * rows, channels), F32)
    for h in range(rows):
        pick = ((place == h) & (lane == 0)) | ((place == rows + h) & (lane == width - 1))
        ends = ends + dot_nt(pick.astype(F32).astype(BF16), x_ref[h])
    ends = ends.astype(BF16)
    last_ref[LANES:] = ends
    next_ref[LANES:] = ends


def halo_body(
    me_ref,
    z_ref,
    x_ref,
    next_ref,
    last_ref,
    fw_ref,
    pair_ref,
    fwd_edge_ref,
    inv_edge_ref,
    down_ref,
    up_ref,
    side_ref,
    kept_ref,
    sem,
):
    rows, channels = side_ref.shape[0] // 2, side_ref.shape[1]
    me, z = me_ref[0], z_ref[0]
    loads = [
        pltpu.make_async_copy(pair_ref, kept_ref.at[pl.ds(0, 4)], sem.at[0]),
        pltpu.make_async_copy(fwd_edge_ref.at[z], kept_ref.at[4, :, pl.ds(0, 2 * MID)], sem.at[1]),
        pltpu.make_async_copy(inv_edge_ref.at[z], kept_ref.at[4, :, pl.ds(2 * MID, 2 * MID)], sem.at[2]),
        pltpu.make_async_copy(x_ref.at[rows - 1], down_ref.at[pl.ds(0, channels)], sem.at[3]),
        pltpu.make_async_copy(x_ref.at[0], up_ref.at[pl.ds(0, channels)], sem.at[4]),
    ]
    for load in loads:
        load.start()
    odd = lax.rem(me, 2).astype(F32)
    near = next_ref[LANES:].astype(F32)
    far = last_ref[LANES:].astype(F32)
    even = 1.0 - odd
    left = (odd * near[rows:] + even * far[rows:]) * jnp.where(me > 0, 1.0, 0.0)
    right = (odd * far[:rows] + even * near[:rows]) * jnp.where(me < COLS - 1, 1.0, 0.0)
    sides = jnp.concatenate([left, right], 0).astype(BF16)
    side_ref[...] = sides
    down_ref[channels:] = sides
    up_ref[channels:] = sides
    mixer = spread(fw_ref[...].T)
    low = jnp.zeros((LANE - CF, 2 * LANE), BF16)
    kept_ref[5] = jnp.concatenate([mixer[:CF], low, mixer[CF:], low], 0)
    for load in loads:
        load.wait()


def width_near_body(me_ref, t_ref, near_ref, far_ref, x_ref, o_ref, copy_ref, sem):
    me = me_ref[0]
    copy = pltpu.make_async_copy(x_ref, copy_ref, sem.at[0])
    copy.start()
    o_ref[...] = dot_nt(t_ref[me], near_ref[...]) + dot_nt(t_ref[lax.bitwise_xor(me, 2)], far_ref[...])
    copy.wait()


def width_last_body(me_ref, t_ref, part_ref, next_ref, last_ref, o_ref, held, sem):
    me = me_ref[0]
    size = o_ref.shape[0] // 4
    copies = []
    for i in range(4):
        span = pl.ds(i * size, size)
        total = part_ref[span] + dot_nt(t_ref[lax.bitwise_xor(me, 1), span], next_ref[:LANES])
        held[span] = (total + dot_nt(t_ref[lax.bitwise_xor(me, 3), span], last_ref[:LANES])).astype(BF16)
        copies.append(pltpu.make_async_copy(held.at[span], o_ref.at[span], sem.at[i]))
        copies[-1].start()
    for copy in copies:
        copy.wait()


def widen(d):
    gap = jnp.zeros((d.shape[0], LANE - CF), d.dtype)
    return jnp.concatenate(sum([[d[:, CF * r : CF * r + CF], gap] for r in range(HS)], []), 1)


def narrow(d):
    return jnp.concatenate([d[:, LANE * r : LANE * r + CF] for r in range(HS)], 1)


def turns(real, imag):
    s02r, d02r, s13r, d13r = real[0] + real[2], real[0] - real[2], real[1] + real[3], real[1] - real[3]
    s02i, d02i, s13i, d13i = imag[0] + imag[2], imag[0] - imag[2], imag[1] + imag[3], imag[1] - imag[3]
    return (
        (s02r + s13r, s02i + s13i),
        (d02r + d13i, d02i - d13r),
        (s02r - s13r, s02i - s13i),
        (d02r - d13i, d02i + d13r),
    )


def spread(t):
    gap = jnp.zeros((t.shape[0], LANE - CF), t.dtype)
    return jnp.concatenate([t[:, :CF], gap, t[:, CF:], gap], 1)


def middle_body(d_ref, x_ref, scale_ref, shift_ref, o_ref, scale_row, shift_row, tw_ref, edge_ref, wide, back_ref, held, sem):
    loads = [
        pltpu.make_async_copy(scale_ref, scale_row, sem.at[0]),
        pltpu.make_async_copy(shift_ref, shift_row, sem.at[1]),
    ]
    for load in loads:
        load.start()
    first = 0
    wide[...] = widen(jnp.swapaxes(d_ref[...], 0, 1).reshape(W, LANES))
    fwd, inv, edges = x_ref.at[first], x_ref.at[first + 1], x_ref.at[first + 4]
    tw = x_ref[first + 2].astype(F32) + x_ref[first + 3].astype(F32)
    for i in range(4):
        half = slice((i % 2) * 2 * LANE, (i % 2 + 1) * 2 * LANE)
        tw_ref[i // 2, :, half] = tw[i * MID : (i + 1) * MID]
    twr, twi = tw_ref[0], tw_ref[1]
    fwd_edge = edges.at[:, : 2 * MID][...]
    edge_ref[:, : 2 * MID] = edges[: 2 * MID, 2 * MID :]
    edge_ref[:, 2 * MID :] = edges[2 * MID :, 2 * MID :]
    inv_edge = edge_ref[...]
    mixer = x_ref[first + 5]
    for load in loads:
        load.wait()
    scale, shift = spread(scale_row[...]), spread(shift_row[...])
    groups = [slice(LANE * r, LANE * r + LANE) for r in range(HS)]
    for own in ((0,), (1, 2), (3, 4), (5, 6), (7,)):
        data = jnp.concatenate(
            [wide[(p * NF + f) * MID : (p * NF + f + 1) * MID] for f in own for p in range(2)], 0
        )
        count = 2 if own == (0,) else len(own)
        half = 2 * MID * len(own)
        ahead = fwd_edge if own == (0,) else fwd[:half, :half]
        u = dot(ahead, data)
        rows = []
        for f in range(count):
            ur = u[2 * f * MID : (2 * f + 1) * MID]
            ui = u[(2 * f + 1) * MID : (2 * f + 2) * MID]
            vr, vi = [ur[:, groups[0]]], [ui[:, groups[0]]]
            for g in groups[1:]:
                vr.append(ur[:, g] * twr[:, g] - ui[:, g] * twi[:, g])
                vi.append(ur[:, g] * twi[:, g] + ui[:, g] * twr[:, g])
            for real, imag in turns(vr, vi):
                rows.append(jnp.concatenate([real, imag], 1).astype(BF16))
        mixed = dot(jnp.concatenate(rows, 0), mixer)
        active = jnp.maximum(scale * mixed + shift, 0.0)
        rows = []
        for f in range(count):
            part = [active[(HS * f + j) * MID : (HS * f + j + 1) * MID] for j in (0, 3, 2, 1)]
            turned = turns([v[:, :LANE] for v in part], [v[:, LANE:] for v in part])
            br, bi = [turned[0][0].astype(BF16)], [turned[0][1].astype(BF16)]
            for g, (real, imag) in zip(groups[1:], turned[1:]):
                br.append((real * twr[:, g] + imag * twi[:, g]).astype(BF16))
                bi.append((imag * twr[:, g] - real * twi[:, g]).astype(BF16))
            rows.append(jnp.concatenate(br, 1))
            rows.append(jnp.concatenate(bi, 1))
        behind = inv_edge if own == (0,) else inv[:half, :half]
        done = narrow(dot(behind, jnp.concatenate(rows, 0)).astype(BF16))
        for i, f in enumerate(own):
            for p in range(2):
                back_ref[p * NF + f] = done[(2 * i + p) * MID : (2 * i + p + 1) * MID]
    stores = []
    size = MID // 4
    for i in range(4):
        span = pl.ds(i * size, size)
        held[span] = jnp.swapaxes(back_ref[:, i * size : (i + 1) * size, :], 0, 1)
        stores.append(pltpu.make_async_copy(held.at[span], o_ref.at[span], sem.at[8 + i]))
        stores[-1].start()
    for store in stores:
        store.wait()


def inverse_body(t_ref, d_ref, *outs):
    data = d_ref[...].T
    for i, o_ref in enumerate(outs):
        o_ref[...] = dot(data, t_ref[i]).astype(BF16)


def conv_setup(fl_ref, fg_ref, wl_ref, wg_ref):
    cl, channels = fl_ref.shape[1], fl_ref.shape[2]
    for dx in range(3):
        wl_ref[dx * channels : (dx + 1) * channels] = jnp.concatenate([fl_ref[3 * dy + dx] for dy in range(3)], 0).T
        wg_ref[dx * cl : (dx + 1) * cl] = jnp.concatenate([fg_ref[3 * dy + dx] for dy in range(3)], 1)


def conv_edges(side_ref, around, wl_ref, wg_ref, cols, edge):
    rows, channels = side_ref.shape[0] // 2, side_ref.shape[1]
    cl, cg = wl_ref.shape[1] // 3, wg_ref.shape[1] // 3
    cols[...] = jnp.zeros_like(cols)
    for side in range(2):
        own = pl.ds(side * rows, rows)
        cols[side, rows : 2 * rows] = side_ref[own]
        for i, other in enumerate(around):
            cols[side, 2 * i * rows : (2 * i + 1) * rows] = other[pl.ds(channels + side * rows, rows)]
        dx = 2 * side
        total = None
        for dy in range(3):
            taps = wl_ref[dx * channels : (dx + 1) * channels, dy * cl : (dy + 1) * cl]
            term = dot_nt(taps, cols[side, :, :cl])
            taps = wg_ref[dx * cl : (dx + 1) * cl, dy * cg : (dy + 1) * cg]
            extra = dot_nt(taps, cols[side, :, cl:])
            term = jnp.concatenate([term[:cl] + extra, term[cl:]], 0)
            term = pltpu.roll(term, LANE - (rows - 1 + dy), 1)
            total = term if total is None else total + term
        edge[side] = total


def edge_lanes(h, edge, before, behind):
    lane = lax.broadcasted_iota(jnp.int32, edge.shape[1:], 1)
    width = before.shape[1]
    first = pltpu.roll(edge[0], lax.rem(LANE - h, LANE), 1)
    final = pltpu.roll(edge[1], LANE - 1 - h, 1)
    before = jnp.concatenate([jnp.where(lane == 0, first, before[:, :LANE]), before[:, LANE:]], 1)
    last = jnp.where(lane == LANE - 1, final, behind[:, width - LANE :])
    return before, jnp.concatenate([behind[:, : width - LANE], last], 1)


def conv_row(h, three, wl_ref, wg_ref, wm_ref, ws_ref, affine_ref, edge, o_ref, out_ref, sem):
    channels, width = three[1].shape
    cl = wl_ref.shape[1] // 3
    local = jnp.concatenate([row[:cl] for row in three], 0)
    other = jnp.concatenate([row[cl:] for row in three], 0)
    yl = dot(wl_ref[...], local)
    yg = dot(wg_ref[...], other)
    parts = []
    for dx in range(3):
        own = yl[dx * channels : (dx + 1) * channels]
        parts.append(jnp.concatenate([own[:cl] + yg[dx * cl : (dx + 1) * cl], own[cl:]], 0))
    before = pltpu.roll(parts[0], 1, 1)
    behind = pltpu.roll(parts[2], width - 1, 1)
    before, behind = edge_lanes(h, edge, before, behind)
    acc = parts[1] + before + behind
    mix = dot(wm_ref[...], section_rows(ws_ref[...], affine_ref[:, 0:1], affine_ref[:, 1:2], three[1][cl:]))
    o_ref[h, :cl] = acc[:cl].astype(BF16)
    o_ref[h, cl:] = (acc[cl:] + mix).astype(BF16)
    pltpu.make_async_copy(o_ref.at[h], out_ref.at[h], sem.at[0]).start()


def conv_body(
    x_ref,
    side_ref,
    fl_ref,
    fg_ref,
    wm_ref,
    ws_ref,
    affine_ref,
    above_ref,
    below_ref,
    table_ref,
    me_ref,
    out_ref,
    kept_ref,
    o_ref,
    cols,
    edge,
    wl_ref,
    wg_ref,
    sem,
):
    rows, channels, width = x_ref.shape
    others = []
    for i, s in enumerate((2, 3, 1)):
        source = table_ref.at[lax.bitwise_xor(me_ref[0], s)]
        others.append(pltpu.make_async_copy(source, kept_ref.at[i], sem.at[2 + i]))
    for other in others:
        other.start()
    conv_setup(fl_ref, fg_ref, wl_ref, wg_ref)
    conv_edges(side_ref, (above_ref, below_ref), wl_ref, wg_ref, cols, edge)
    rest = (wl_ref, wg_ref, wm_ref, ws_ref, affine_ref, edge, o_ref, out_ref, sem)
    conv_row(0, [above_ref[:channels], x_ref[0], x_ref[1]], *rest)

    def step(h, carry):
        conv_row(h, [x_ref[h - 1], x_ref[h], x_ref[h + 1]], *rest)
        return carry

    lax.fori_loop(1, rows - 1, step, 0, unroll=7)
    conv_row(rows - 1, [x_ref[rows - 2], x_ref[rows - 1], below_ref[:channels]], *rest)
    pltpu.make_async_copy(o_ref, out_ref, sem.at[0]).wait()
    for other in others:
        other.wait()


def final_rows(pieces, me_ref, x_ref, pre_ref, w_ref, affine_ref, o_ref, finish=None):
    channels = x_ref.shape[1]
    count = w_ref.shape[0]
    size = channels - count
    mixed = {}
    for s, piece in pieces:
        for r in range(HS):
            mixed[s, r] = dot(w_ref[...], piece[r * CF : (r + 1) * CF])
    for k in range(channels // size):
        span = slice(k * size, (k + 1) * size)
        scale, shift = affine_ref[span, 0:1], affine_ref[span, 1:2]
        for s, _ in pieces:
            first = HS * lax.bitwise_xor(me_ref[0], s)
            for r in range(HS):
                pre = pre_ref[first + r, span].astype(F32)
                if k:
                    pre = pre + mixed[s, r][(k - 1) * size : k * size]
                act = jnp.maximum(scale * pre + shift, 0.0)
                o_ref[first + r, span] = (x_ref[first + r, span].astype(F32) + act).astype(BF16)
        if finish is not None:
            finish(k, span)


def fetch_rows(x_ref, pre_ref, first, count, x, pre, sem):
    span = pl.ds(first, count)
    loads = [
        pltpu.make_async_copy(x_ref.at[span], x.at[span], sem.at[0]),
        pltpu.make_async_copy(pre_ref.at[span], pre.at[span], sem.at[1]),
    ]
    for load in loads:
        load.start()
    return loads


def final_near_body(
    me_ref, x_ref, pre_ref, w_ref, scale_ref, shift_ref, t_ref, d_ref, next_ref, o_ref, affine_ref, x, pre, table, sem
):
    me = me_ref[0]
    load = pltpu.make_async_copy(t_ref.at[me], table, sem.at[2])
    load.start()
    loads = fetch_rows(x_ref, pre_ref, 2 * HS * (me // 2), 2 * HS, x, pre, sem)
    affine_ref[:, 0:1] = column(scale_ref[...])
    affine_ref[:, 1:2] = column(shift_ref[...])
    data = d_ref[...].T
    load.wait()
    near = dot(data, table[...]).astype(BF16)
    for load in loads:
        load.wait()
    final_rows(((0, near), (1, next_ref)), me_ref, x, pre, w_ref, affine_ref, o_ref)


def final_far_body(me_ref, x_ref, pre_ref, w_ref, affine_ref, far_ref, given_ref, o_ref, x, pre, sem):
    loads = fetch_rows(x_ref, pre_ref, HS * lax.bitwise_xor(me_ref[0], 2), HS, x, pre, sem)
    for load in loads:
        load.wait()
    final_rows(((2, far_ref),), me_ref, x, pre, w_ref, affine_ref, o_ref)


def final_last_body(me_ref, x_ref, pre_ref, w_ref, affine_ref, last_ref, given_ref, o_ref, out_ref, held, sem):
    copies = []

    def finish(k, span):
        held[span] = jnp.swapaxes(o_ref[:, span, :], 0, 1)
        copies.append(pltpu.make_async_copy(held.at[span], out_ref.at[span], sem.at[k]))
        copies[-1].start()

    final_rows(((3, last_ref),), me_ref, x_ref, pre_ref, w_ref, affine_ref, o_ref, finish)
    for copy in copies:
        copy.wait()


def shift_along(block, axis, step):
    count = lax.axis_size(axis)
    pairs = [(i, i + step) for i in range(count) if 0 <= i + step < count]
    return lax.ppermute(block, axis, pairs)


def swap(block, s):
    return lax.ppermute(block, "col", [(i, i ^ s) for i in range(COLS)])


def after(value, *others):
    return lax.optimization_barrier((value,) + others)


def per_device(
    image,
    from_local,
    from_global,
    section_weight,
    section_scale,
    section_shift,
    fourier_weight,
    fourier_scale,
    fourier_shift,
    mix_weight,
    out_scale,
    out_shift,
):
    channels, rows, width = image.shape
    cl = from_local.shape[2]
    cg = channels - cl
    me = lax.axis_index("col").astype(jnp.int32).reshape(1)
    z = jnp.logical_and(lax.axis_index("row") == 0, lax.axis_index("col") == 0).astype(jnp.int32).reshape(1)
    shape = jax.ShapeDtypeStruct
    dma = pltpu.SemaphoreType.DMA

    whole = shape((rows, channels, width), BF16)
    block, block_ends = shape((LANES, width), BF16), shape((LANES + 2 * rows, width), BF16)
    x, far, section_affine = call(
        first_body,
        (whole, block, shape((CF, 2), F32)),
        (me, image, section_weight, section_scale[None], section_shift[None]),
        smem=(0,),
        hbm=(1, 2, 3, 4),
        scratch=[
            pltpu.VMEM((channels, rows, width), BF16),
            pltpu.VMEM((CF, cg), BF16),
            pltpu.VMEM((1, CF), F32),
            pltpu.VMEM((1, CF), F32),
            dma((PARTS + 3,)),
        ],
    )
    far = swap(far, 2)
    near, other, last = call(
        rest_body, (block, block_ends, block_ends), (me, x, section_weight, section_affine), smem=(0,)
    )
    last, other = swap(last, 3), swap(other, 1)

    weights = (jnp.transpose(from_local, (0, 2, 1)), from_global, mix_weight, section_weight, section_affine)
    scratch = [
        pltpu.VMEM((rows, channels, width), BF16),
        pltpu.VMEM((2, LANE, channels), BF16),
        pltpu.VMEM((2, channels, LANE), F32),
        pltpu.VMEM((3 * channels, 3 * cl), BF16),
        pltpu.VMEM((3 * cl, 3 * cg), BF16),
        dma((5,)),
    ]
    fwd_w, inv_w = (jnp.asarray(t) for t in width_tables())
    part, x = call(
        width_near_body,
        (shape((W, LANES), F32), whole),
        (me, fwd_w, near, far, x),
        smem=(0,),
        flops=10**9,
        hbm_out=(1,),
        scratch=[dma((1,))],
    )
    spectra = call(
        width_last_body,
        shape((W, LANES), BF16),
        (me, fwd_w, part, other, last),
        smem=(0,),
        hbm_out=(0,),
        scratch=[pltpu.VMEM((W, LANES), BF16), dma((4,))],
    )
    spectra, other, last = after(spectra, other, last)
    spectra = lax.all_to_all(
        spectra.reshape(PEERS, 2 * NF, LANES), ("row", "col"), split_axis=0, concat_axis=0, tiled=True
    )
    ends = shape((channels + 2 * rows, width), BF16)
    pairs, fwd_edge, inv_edge = (jnp.asarray(t) for t in height_tables())
    down, up, sides, kept = call(
        halo_body,
        (ends, ends, shape((2 * rows, channels), BF16), shape((6, channels, width), BF16)),
        (me, z, x, other, last, fourier_weight, pairs, fwd_edge, inv_edge),
        smem=(0, 1),
        hbm=(2, 6, 7, 8),
        stage=(5,),
        scratch=[dma((5,))],
    )
    above, below = shift_along(down, "row", 1), shift_along(up, "row", -1)

    returned = call(
        middle_body,
        shape((PEERS, 2 * NF, LANES), BF16),
        (spectra, kept, fourier_scale[None], fourier_shift[None]),
        hbm=(2, 3),
        hbm_out=(0,),
        limit=24,
        scratch=[
            pltpu.VMEM((1, 2 * CF), F32),
            pltpu.VMEM((1, 2 * CF), F32),
            pltpu.VMEM((2, MID, WIDE), F32),
            pltpu.VMEM((2 * MID, 4 * MID), BF16),
            pltpu.VMEM((W, WIDE), BF16),
            pltpu.VMEM((2 * NF, MID, LANES), BF16),
            pltpu.VMEM((PEERS, 2 * NF, LANES), BF16),
            dma((12,)),
        ],
    )
    returned, above, below = after(returned, above, below)
    returned = lax.all_to_all(returned, ("row", "col"), split_axis=0, concat_axis=0, tiled=True).reshape(W, LANES)
    pre, table = call(
        conv_body,
        (whole, shape((3, W, width), BF16)),
        (x, sides) + weights + (above, below, inv_w, me),
        smem=(10,),
        hbm=(9,),
        hbm_out=(0,),
        stage=tuple(range(7)),
        flops=10**9,
        scratch=scratch,
    )

    piece = shape((LANES, width), BF16)
    far, last, other = call(inverse_body, (piece,) * 3, (table, returned))
    far, last, other = swap(far, 2), swap(last, 3), swap(other, 1)
    rows_held = [pltpu.VMEM(whole.shape, BF16), pltpu.VMEM(whole.shape, BF16)]
    half, affine = call(
        final_near_body,
        (whole, shape((channels, 2), F32)),
        (me, x, pre, mix_weight, out_scale[None], out_shift[None], inv_w, returned, other),
        smem=(0,),
        hbm=(1, 2, 6),
        stage=(3, 4, 5),
        scratch=rows_held + [pltpu.VMEM((W, width), BF16), dma((3,))],
    )
    common = (me, x, pre, mix_weight, affine)
    half = call(
        final_far_body,
        whole,
        common + (far, half),
        smem=(0,),
        hbm=(1, 2),
        input_output_aliases={6: 0},
        scratch=rows_held + [dma((2,))],
    )
    _, result = call(
        final_last_body,
        (whole, shape(image.shape, BF16)),
        common + (last, half),
        smem=(0,),
        hbm_out=(1,),
        input_output_aliases={6: 0},
        scratch=[pltpu.VMEM(image.shape, BF16), dma((8,))],
    )
    return result


def solution(mesh):
    return jax.shard_map(
        per_device,
        mesh=mesh,
        in_specs=(P("img", "row", "col"), P(), P(), P(), P(), P(), P(), P(), P(), P(), P(), P()),
        out_specs=P("img", "row", "col"),
        check_vma=False,
    )
```
